32 devices in a mesh: dp: 8 (over y, x, core), tensor: 4 (over z).
Axes of the slice: x: 2, y: 2, z: 4, core: 2. Of those that a mesh axis runs over, the one named last changes fastest.
Arguments:
- tokens: bfloat16 [4096, 768], P(('dp', 'tensor')), may hold values from -6 to 6
- segment_ids: int32 [8, 512], P('dp'), may hold values from 0 to 3, never falling along the last dimension, each value on 1 to 256 neighbouring positions
- w_query: bfloat16 [768, 768], P(None, 'tensor'), may hold values from -0.21875 to 0.21875
- b_query: bfloat16 [768], P('tensor'), may hold values from -3 to 3
- w_key: bfloat16 [768, 768], P(None, 'tensor'), may hold values from -0.21875 to 0.21875
- b_key: bfloat16 [768], P('tensor'), may hold values from -3 to 3
- w_value: bfloat16 [768, 768], P(None, 'tensor'), may hold values from -0.21875 to 0.21875
- b_value: bfloat16 [768], P('tensor'), may hold values from -3 to 3
- w_out: bfloat16 [768, 768], P('tensor'), may hold values from -0.625 to 0.625
- b_out: bfloat16 [768], replicated, may hold values from -3 to 3
- gain_mixer: bfloat16 [768], replicated, may hold values from 0.5 to 1.5
- shift_mixer: bfloat16 [768], replicated, may hold values from -3 to 3
- w_up: bfloat16 [768, 3072], P(None, 'tensor'), may hold values from -0.21875 to 0.21875
- b_up: bfloat16 [3072], P('tensor'), may hold values from -3 to 3
- w_down: bfloat16 [3072, 768], P('tensor'), may hold values from -0.15625 to 0.15625
- b_down: bfloat16 [768], replicated, may hold values from -3 to 3
- gain_feed: bfloat16 [768], replicated, may hold values from 0.5 to 1.5
- shift_feed: bfloat16 [768], replicated, may hold values from -3 to 3
- cotangent: bfloat16 [4096, 768], P(('dp', 'tensor')), may hold values from -6 to 6
Outputs:
- layer_out: bfloat16 [4096, 768], P(('dp', 'tensor'))
- grad_tokens: float32 [4096, 768], P(('dp', 'tensor'))
- grad_w_query: float32 [768, 768], P('dp', 'tensor')
- grad_b_query: float32 [768], replicated
- grad_w_key: float32 [768, 768], P('dp', 'tensor')
- grad_b_key: float32 [768], replicated
- grad_w_value: float32 [768, 768], P('dp', 'tensor')
- grad_b_value: float32 [768], replicated
- grad_w_out: float32 [768, 768], P('tensor', 'dp')
- grad_b_out: float32 [768], replicated
- grad_gain_mixer: float32 [768], replicated
- grad_shift_mixer: float32 [768], replicated
- grad_w_up: float32 [768, 3072], P('dp', 'tensor')
- grad_b_up: float32 [3072], replicated
- grad_w_down: float32 [3072, 768], P('tensor', 'dp')
- grad_b_down: float32 [768], replicated
- grad_gain_feed: float32 [768], replicated
- grad_shift_feed: float32 [768], replicated
The draws below stay inside these ranges and needn't reach their ends.
Inputs may be any that keep to these rules, and one draw needn't show every extreme that they name: `segment_ids`: ids never fall along a row of 512 tokens; each document (a run of equal ids) has 1 to 256 tokens, and some document has exactly 256.
All inputs are finite; a program needn't handle non-finite values.
Results may differ from the reference program's by a relative error of at most 0.017.
Values may be sent and summed in bfloat16 or wider, within the bound.
A program may use at most 64 MiB of HBM per device.

```python
import math
import jax
import jax.numpy as jnp
import numpy as np
from jax import lax

D = 768
HEADS = 12
HD = 64
FF = 3072
LEN = 512
SEQS = 8
TOKENS = 4096


def with_spikes(values, stream_key, source, target, parts, factor):
    owner, partner = [(jnp.arange(values.shape[dim]) // (values.shape[dim] // parts)).reshape([-1 if axis == dim else 1 for axis in range(values.ndim)]) for dim in (source, target)]
    chosen = jax.random.permutation(stream_key, parts)[partner]
    strong = (owner == chosen) | (owner == (partner + parts // 2) % parts)
    return jnp.where(strong, factor * values, values)


def block_levels(rng, extent, shards, least, high):
    level, own = 1.0, jax.random.fold_in(rng, 6)
    for axis_at, blocks in shards:
        heights = jnp.exp(jax.random.uniform(jax.random.fold_in(own, axis_at), (blocks,), jnp.float32, least / len(shards), high / len(shards)))
        level = level * jnp.repeat(heights, extent[axis_at] // blocks).reshape([-1 if axis == axis_at else 1 for axis in range(len(extent))])
    return level


def length_profile(amount, total, bound, lean):
    loads = [(1 << 20) // math.isqrt(rank ** lean) + 1 for rank in range(2, amount + 1)]
    rest, counts = total - bound - (amount - 1), [1] * (amount - 1)
    while rest > 0:
        candidates = [i for i in range(amount - 1) if counts[i] < bound]
        pool, left = sum([loads[i] for i in candidates]), rest
        for i in candidates:
            extra = min(bound - counts[i], max(1, left * loads[i] // pool), rest)
            counts[i] = counts[i] + extra
            rest = rest - extra
    return np.array([bound] + counts)


def ragged(own_key, count, total, most, slope):
    if count == 2:
        one = jax.random.randint(own_key, (), max(1, total - most), min(most, total - 1) + 1)
        return jnp.stack([one, total - one])
    sizes = jnp.asarray(length_profile(count, total, most, slope), jnp.int32)
    couples = (count - 1) // 2
    source_of, receiver = sizes[1:1 + 2 * couples:2], sizes[2:2 + 2 * couples:2]
    margin = jnp.minimum(source_of - 1, most - receiver)
    shifted = jax.random.randint(jax.random.fold_in(own_key, 1), (couples,), 0, 1 << 20) % (margin + 1)
    sizes = sizes.at[1:1 + 2 * couples:2].set(source_of - shifted).at[2:2 + 2 * couples:2].set(receiver + shifted)
    return sizes[jax.random.permutation(jax.random.fold_in(own_key, 2), count)]


def scatter_about(rng, extent, width, bound, split=(), held_as=jnp.bfloat16):
    array = width * jax.random.normal(rng, extent, jnp.float32)
    if split:
        array = array * block_levels(rng, extent, split, -0.22, 0.18)
    return jnp.clip(array, -bound, bound).astype(held_as)


def noise_with(key, dims, width, reach, pieces, heavy, kind=jnp.bfloat16):
    values = width * jax.random.normal(key, dims, jnp.float32)
    if pieces:
        values = values * block_levels(key, dims, pieces, -0.22, 0.18)
    return jnp.clip(with_spikes(values, jax.random.fold_in(key, 3), *heavy), -reach, reach).astype(kind)


def setup_inputs(seed: int = 0) -> dict:
    keys = jax.random.split(jax.random.key(seed), 20)
    return {
        "tokens": noise_with(keys[0], (TOKENS, D), 1.0, 6.0, ((0, 32),), (0, 1, 32, 2.75)),
        "segment_ids": jax.vmap(lambda own: jnp.searchsorted(jnp.cumsum(ragged(own, 4, LEN, LEN // 2, 1)), jnp.arange(LEN), side="right"))(jax.random.split(keys[1], SEQS)).reshape((SEQS, LEN)).astype(jnp.int32),
        "w_query": scatter_about(keys[2], (D, D), D ** -0.5, 0.21875, ((1, 4),)),
        "b_query": scatter_about(keys[3], (D,), 0.5, 3.0, ((0, 4),)),
        "w_key": scatter_about(keys[4], (D, D), D ** -0.5, 0.21875, ((1, 4),)),
        "b_key": scatter_about(keys[5], (D,), 0.5, 3.0, ((0, 4),)),
        "w_value": scatter_about(keys[6], (D, D), D ** -0.5, 0.21875, ((1, 4),)),
        "b_value": scatter_about(keys[7], (D,), 0.5, 3.0, ((0, 4),)),
        "w_out": scatter_about(keys[8], (D, D), (D // 8) ** -0.5, 0.625, ((0, 4),)),
        "b_out": scatter_about(keys[9], (D,), 0.5, 3.0),
        "gain_mixer": jnp.clip(1.0 + 0.1 * jax.random.normal(keys[10], (D,), jnp.float32), 0.5, 1.5).astype(jnp.bfloat16),
        "shift_mixer": scatter_about(keys[11], (D,), 0.5, 3.0),
        "w_up": scatter_about(keys[12], (D, FF), D ** -0.5, 0.21875, ((1, 4),)),
        "b_up": scatter_about(keys[13], (FF,), 0.5, 3.0, ((0, 4),)),
        "w_down": scatter_about(keys[14], (FF, D), (FF // 2) ** -0.5, 0.15625, ((0, 4),)),
        "b_down": scatter_about(keys[15], (D,), 0.5, 3.0),
        "gain_feed": jnp.clip(1.0 + 0.1 * jax.random.normal(keys[16], (D,), jnp.float32), 0.5, 1.5).astype(jnp.bfloat16),
        "shift_feed": scatter_about(keys[17], (D,), 0.5, 3.0),
        "cotangent": noise_with(keys[18], (TOKENS, D), 1.0, 6.0, ((0, 32),), (0, 1, 32, 2.75)),
    }


@jax.custom_vjp
def low(v):
    return lax.optimization_barrier(v.astype(jnp.bfloat16)).astype(jnp.float32)

@jax.custom_vjp
def low_back(v):
    return v

def low_keep(v):
    return (low(v), None)

def low_pass(kept, grad):
    return (grad,)

def back_keep(v):
    return (v, None)

def back_low(kept, grad):
    return (low(grad),)
low.defvjp(low_keep, low_pass)
low_back.defvjp(back_keep, back_low)
ln_eps = 1e-12

def matmul(left_side, right_side):
    return jnp.dot(left_side, right_side, precision=lax.Precision.HIGHEST)

def layer_norm(values, gain_vec, shift_vec):
    average = lax.optimization_barrier(jnp.mean(values, axis=-1, keepdims=True))
    centered = values - average
    variance = lax.optimization_barrier(jnp.mean(centered * centered, axis=-1, keepdims=True))
    return centered * lax.rsqrt(variance + ln_eps) * gain_vec + shift_vec

def rotary_tables(segment_rows, head_size):
    seq_count, length = segment_rows.shape
    places = lax.broadcasted_iota(jnp.int32, (seq_count, length), 1)
    earlier = jnp.concatenate([jnp.full((seq_count, 1), -1, jnp.int32), segment_rows[:, :-1]], axis=1)
    starts_at = lax.cummax(jnp.where(segment_rows != earlier, places, 0), axis=1)
    position = (places - starts_at).astype(jnp.float32)
    half_size = head_size // 2
    frequency = jnp.exp(jnp.arange(half_size, dtype=jnp.float32) * (-math.log(10000.0) / half_size))
    angles = position[:, :, None] * frequency
    cosine = jnp.concatenate([jnp.cos(angles), jnp.cos(angles)], axis=-1)
    sine = jnp.concatenate([jnp.sin(angles), jnp.sin(angles)], axis=-1)
    return (cosine, sine)

def rotate(values, cosine, sine):
    half_size = values.shape[-1] // 2
    rotated = jnp.concatenate([-values[..., half_size:], values[..., :half_size]], axis=-1)
    return values * cosine[:, :, None, :] + rotated * sine[:, :, None, :]

def forward(flat, segment_rows, w_query, b_query, w_key, b_key, w_value, b_value, w_out, b_out, gain_mixer, shift_mixer, w_up, b_up, w_down, b_down, gain_feed, shift_feed):
    seq_count = segment_rows.shape[0]
    head_shape = (seq_count, LEN, HEADS, HD)
    flat_low = low(flat)
    query_pre = low_back(matmul(flat_low, w_query) + b_query)
    key_pre = low_back(matmul(flat_low, w_key) + b_key)
    value_low = low(low_back(matmul(flat_low, w_value) + b_value)).reshape(head_shape)
    cosine, sine = rotary_tables(segment_rows, HD)
    query_low = low(rotate(query_pre.reshape(head_shape), cosine, sine))
    key_low = low(rotate(key_pre.reshape(head_shape), cosine, sine))
    scores = jnp.einsum('sqhd,skhd->shqk', query_low, key_low, precision=lax.Precision.HIGHEST)
    scores = low_back(scores * HD ** (-0.5))
    same_doc = segment_rows[:, :, None] == segment_rows[:, None, :]
    scores = jnp.where(same_doc[:, None], scores, -1e+30)
    attention = low(jax.nn.softmax(scores, axis=-1))
    heads = jnp.einsum('shqk,skhd->sqhd', attention, value_low, precision=lax.Precision.HIGHEST)
    head_rows = low(low_back(heads.reshape(seq_count * LEN, HEADS * HD)))
    first_in = flat + low_back(matmul(head_rows, w_out)) + b_out
    normed = layer_norm(first_in, gain_mixer, shift_mixer)
    hidden = low_back(matmul(low(normed), w_up) + b_up)
    activated = low(jax.nn.gelu(hidden, approximate=False))
    second_in = normed + low_back(matmul(activated, w_down)) + b_down
    return layer_norm(second_in, gain_feed, shift_feed)

def reference(tokens, segment_ids, w_query, b_query, w_key, b_key, w_value, b_value, w_out, b_out, gain_mixer, shift_mixer, w_up, b_up, w_down, b_down, gain_feed, shift_feed, cotangent):
    params = tuple((array_in.astype(jnp.float32) for array_in in (w_query, b_query, w_key, b_key, w_value, b_value, w_out, b_out, gain_mixer, shift_mixer, w_up, b_up, w_down, b_down, gain_feed, shift_feed)))
    group_size = math.gcd(SEQS, max(1, 4096 // LEN))
    group_count = SEQS // group_size
    inputs_all = tokens.astype(jnp.float32).reshape(group_count, group_size * LEN, D)
    segments_all = segment_ids.reshape(group_count, group_size, LEN)
    upstream_all = cotangent.astype(jnp.float32).reshape(group_count, group_size * LEN, D)

    def one_group(totals, inputs):
        flat, segment_rows, upstream = inputs

        def local_forward(flat_in, *weights):
            return forward(flat_in, segment_rows, *weights)
        output, pullback = jax.vjp(local_forward, flat, *params)
        gradients = pullback(upstream)
        totals = tuple((total + grad_one for total, grad_one in zip(totals, gradients[1:])))
        return (totals, (output, gradients[0]))
    start_totals = tuple((jnp.zeros(array_in.shape, jnp.float32) for array_in in params))
    totals, (outputs, grad_rows) = lax.scan(one_group, start_totals, (inputs_all, segments_all, upstream_all))
    layer_out = outputs.reshape(TOKENS, D).astype(jnp.bfloat16)
    grad_tokens = grad_rows.reshape(TOKENS, D)
    return (layer_out, grad_tokens, totals[0], totals[1], totals[2], totals[3], totals[4], totals[5], totals[6], totals[7], totals[8], totals[9], totals[10], totals[11], totals[12], totals[13], totals[14], totals[15])
```

```python
from functools import partial
import math

import jax
import jax.numpy as jnp
from jax import lax
from jax.experimental import pallas as pl
from jax.experimental.pallas import tpu as pltpu
from jax.sharding import PartitionSpec as P

HD = 64
MESH = pl.DeviceIdType.MESH
F32 = jnp.float32
BF16 = jnp.bfloat16
LN_EPS = 1e-12
B_QKV, B_UP, B_OUT, G_MIX, S_MIX, B_DOWN, G_FEED, S_FEED = range(8)
DOWN, UP, OUT, QKV = range(4)


def nn(left, right):
    return lax.dot_general(left, right, (((1,), (0,)), ((), ())), preferred_element_type=F32)


def nt(left, right):
    return lax.dot_general(left, right, (((1,), (1,)), ((), ())), preferred_element_type=F32)


def norm_stats(values):
    centered = values - jnp.mean(values, axis=-1, keepdims=True)
    factor = lax.rsqrt(jnp.mean(centered * centered, axis=-1, keepdims=True) + LN_EPS)
    return centered * factor, factor


def norm_back(grads, normalized, factor, gain):
    scaled = grads * gain
    first = jnp.mean(scaled, axis=-1, keepdims=True)
    second = jnp.mean(scaled * normalized, axis=-1, keepdims=True)
    return factor * (scaled - first - normalized * second)


def copy_to(src, dst, send, recv, device):
    return pltpu.make_async_remote_copy(
        src_ref=src, dst_ref=dst, send_sem=send, recv_sem=recv, device_id=device,
        device_id_type=MESH,
    )


def layer_kernel(
    tight,
    tokens, cotangent, small, w_query, w_key, w_value, w_out, w_up, w_down,
    result_o, grad_o, sums_a, sums_b, vec_o,
    x_all, h_all, g2_all, g1_all, x_t, h_t, g2_t, g1_t,
    parts, landed, passed,
    small_v, cot_v, land, staged, wqkv, wo, wu, wd,
    seg_cols, cos_t, sin_t,
    qkv_s, k2_s, probs, probs_low, ds_s, o_s, act, dgelu, dz_s, do_s, dqkv_s,
    q_t, do_t, dk_t, dv_t, h_own, g_own, own_part,
    grads, grads_in, grads_sum, vec, vec_in, vec_col,
    ag_s, ag_r, rs_s, rs_r, sw_s, sw_r, wx_s, wx_r, dx_s, dx_r, dz_sem_s, dz_sem_r,
    vx_s, vx_r, vc_s, vc_r, out_s, out_r, loc,
):
    grad_pieces = grads
    dp, ten = lax.axis_index("dp"), lax.axis_index("tensor")
    low = lax.rem(ten, 2)
    if tight:
        col, core, half = dp // 2, lax.rem(dp, 2), ten // 2
        slot = low + 2 * core
        mate_slot = low + 2 * (1 - core)
        far_slot = 1 - low + 2 * core
        last_slot = 1 - low + 2 * (1 - core)
        mate = {"dp": col * 2 + 1 - core, "tensor": ten}
        far = {"dp": dp, "tensor": ten + 1 - 2 * low}
        other = lax.rem(ten + 2, 4)
        partner = {"dp": col * 2 + 1 - core, "tensor": other}
        across = {"dp": dp, "tensor": other}
        cols = [{"dp": lax.rem(col + j, 4) * 2 + core, "tensor": ten} for j in (1, 2, 3)]
        home = core == half
        away = core != half
    else:
        slot = ten
        mate_slot = ten + 1 - 2 * low
        far_slot = lax.rem(ten + 2, 4)
        last_slot = 3 - ten
        mate = {"dp": dp, "tensor": mate_slot}
        far = {"dp": dp, "tensor": far_slot}

    def all_column():
        for dz in (1, 2, 3):
            yield {"dp": dp, "tensor": lax.rem(ten + dz, 4)}
        for dz in (0, 1, 2, 3):
            yield {"dp": col * 2 + 1 - core, "tensor": lax.rem(ten + dz, 4)}

    rows = x_all.shape[1]
    length = 4 * rows

    def local(src, dst, sem):
        return pltpu.make_async_copy(src, dst, sem)

    raw = [local(w, land.at[i], loc.at[i]) for i, w in enumerate((w_query, w_key, w_value))]
    for copy in raw:
        copy.start()

    to_small = local(small, small_v, sw_r.at[0])
    to_tokens = local(tokens, x_all.at[slot], sw_r.at[1])
    to_cot = local(cotangent, cot_v, sw_r.at[2])
    wo_rows = w_out.shape[0]
    to_out = local(w_out, wo.at[pl.ds(0, wo_rows)], loc.at[3])
    to_up = local(w_up, wu, loc.at[4])
    to_down = local(w_down, wd, loc.at[5])

    def load_own():
        for copy in (to_small, to_tokens, to_out, to_up, to_down, to_cot):
            copy.start()

    if tight:
        pl.when(home)(load_own)
    else:
        load_own()

    barrier = pltpu.get_barrier_semaphore()
    met = list(all_column()) + cols if tight else [mate, far]
    for device in met:
        pl.semaphore_signal(barrier, inc=1, device_id=device, device_id_type=MESH)
    zeros_low = jnp.zeros((wo.shape[0] - wo_rows, wo.shape[1]), BF16)
    wo[wo_rows:, :] = zeros_low
    pl.semaphore_wait(barrier, len(met))

    def assemble(dst, take):
        parts3 = [land[i, take, :] for i in range(3)]
        for i in range(3):
            dst[:, i * 128:(i + 1) * 128] = parts3[i][:, :128]
        dst[:, 384:512] = jnp.concatenate([parts3[0][:, 128:], parts3[1][:, 128:]], axis=1)
        dst[:, 512:] = jnp.concatenate(
            [parts3[2][:, 128:], jnp.zeros_like(parts3[2][:, 128:])], axis=1
        )

    quarter = wqkv.shape[0] // 4
    wo_quarter = wo_rows // 4

    def swap_weight(i):
        size = wo_quarter if i == OUT else quarter
        take = pl.ds(col * size, size)
        dst = (wd, wu, wo, wqkv)[i].at[take]
        src = (w_down, w_up, w_out, None)[i]
        src = staged if src is None else src.at[take]
        return copy_to(src, dst, sw_s.at[3 + i], sw_r.at[3 + i], partner)

    def spread(i, j):
        size = wo_quarter if i == OUT else quarter
        ref = (wd, wu, wo, wqkv)[i].at[pl.ds(col * size, size)]
        return copy_to(ref, ref, wx_s.at[i, j], wx_r.at[i, j], cols[j])

    def spread_in(i, j):
        size = wo_quarter if i == OUT else quarter
        ref = (wd, wu, wo, wqkv)[i].at[pl.ds(lax.rem(col + 3 - j, 4) * size, size)]
        return copy_to(ref, ref, wx_s.at[i, j], wx_r.at[i, j], cols[j])

    def swap_arrays():
        return (
            copy_to(small, small_v, sw_s.at[0], sw_r.at[0], partner),
            copy_to(tokens, x_all.at[mate_slot], sw_s.at[1], sw_r.at[1], partner),
            copy_to(cotangent, cot_v, sw_s.at[2], sw_r.at[2], partner),
        )

    if tight:
        @pl.when(away)
        def _():
            first = swap_arrays()
            first[0].start()
            first[1].start()
            for copy in raw:
                copy.wait()
            assemble(staged, pl.ds(col * quarter, quarter))
            for i in (QKV, OUT, UP, DOWN):
                swap_weight(i).start()
            first[2].start()

        @pl.when(home)
        def _():
            for copy in raw:
                copy.wait()
            assemble(wqkv, slice(None))
    else:
        for copy in raw:
            copy.wait()
        assemble(wqkv, slice(None))

    def ag_own(i, buf):
        copy_to(buf.at[slot], buf.at[slot], ag_s.at[i, 0], ag_r.at[i, 0], mate).start()
        copy_to(buf.at[slot], buf.at[slot], ag_s.at[i, 1], ag_r.at[i, 1], far).start()

    def ag_mate(i, buf):
        ref = buf.at[mate_slot]
        copy_to(ref, ref, ag_s.at[i, 0], ag_r.at[i, 0], mate).wait_recv()

    def ag_far(i, buf):
        ref = buf.at[far_slot]
        copy_to(ref, ref, ag_s.at[i, 1], ag_r.at[i, 1], far).wait_recv()
        copy_to(ref, ref, ag_s.at[i, 2], ag_r.at[i, 2], mate).start()

    def ag_last(i, buf):
        ref = buf.at[last_slot]
        copy_to(ref, ref, ag_s.at[i, 2], ag_r.at[i, 2], mate).wait_recv()

    def ag_done(i, buf):
        copy_to(buf.at[slot], buf.at[slot], ag_s.at[i, 0], ag_r.at[i, 0], mate).wait_send()
        copy_to(buf.at[slot], buf.at[slot], ag_s.at[i, 1], ag_r.at[i, 1], far).wait_send()
        ref = buf.at[far_slot]
        copy_to(ref, ref, ag_s.at[i, 2], ag_r.at[i, 2], mate).wait_send()

    def rs_copy(i, j):
        src = (parts.at[i, 0], parts.at[i, 1], passed.at[i])[j]
        return copy_to(
            src, landed.at[i, j], rs_s.at[i, j], rs_r.at[i, j], far if j == 2 else mate
        )

    def reduce_scatter(i, piece):
        parts[i, 0] = piece(last_slot).astype(BF16)
        rs_copy(i, 0).start()
        parts[i, 1] = piece(mate_slot).astype(BF16)
        rs_copy(i, 1).start()
        own_part[...] = piece(far_slot)
        rs_copy(i, 0).wait_recv()
        passed[i] = (own_part[...] + landed[i, 0].astype(F32)).astype(BF16)
        rs_copy(i, 2).start()
        own_part[...] = piece(slot)

    def reduced(i):
        rs_copy(i, 1).wait_recv()
        rs_copy(i, 2).wait_recv()
        return own_part[...] + landed[i, 1].astype(F32) + landed[i, 2].astype(F32)

    to_small.wait()
    to_tokens.wait()
    ag_own(0, x_all)

    seg_row = small_v[8:9, :length]
    seg_cols[...] = jnp.transpose(jnp.broadcast_to(seg_row, (128, length)))
    segs = seg_cols[...]
    place = lax.broadcasted_iota(jnp.int32, (length, 128), 0).astype(F32)
    start = jnp.zeros((length, 128), F32)
    for s in range(4):
        before = jnp.sum(jnp.where(seg_row < s, 1.0, 0.0), axis=1, keepdims=True)
        start = jnp.where(segs == s, before, start)
    lane = lax.broadcasted_iota(jnp.int32, (1, 128), 1)
    frequency = jnp.exp(lax.rem(lane, 32).astype(F32) * (-math.log(10000.0) / 32))
    angle = (place - start) * frequency
    sign = jnp.where(lax.rem(lane, 64) < 32, -1.0, 1.0)
    cos_t[...] = jnp.cos(angle)
    sin_t[...] = jnp.sin(angle) * sign

    if tight:
        @pl.when(away)
        def _():
            for i in (QKV, OUT, UP, DOWN):
                swap_weight(i).wait_recv()
                for j in range(3):
                    spread(i, j).start()
                if i == QKV:
                    for j in range(3):
                        spread_in(i, j).wait_recv()

    def take(s):
        return pl.ds(pl.multiple_of(s * rows, rows), rows)

    low_lane = lane < 64

    def turn(values):
        return jnp.where(
            lax.rem(lane, 64) < 32, pltpu.roll(values, 96, 1), pltpu.roll(values, 32, 1)
        )

    def project_rows(s):
        here = take(s)
        x = x_all[s]
        x_t[:, here] = jnp.transpose(x)
        pre = nn(x, wqkv[...]) + small_v[B_QKV:B_QKV + 1, :640]
        cosine, sine = cos_t[here, :], sin_t[here, :]

        def rot(block):
            return block * cosine + turn(block) * sine

        scale = HD ** (-0.5)
        query, key, mixed = rot(pre[:, :128]), rot(pre[:, 128:256]), rot(pre[:, 384:512])
        qkv_s[here, 0:128] = (query.astype(BF16) * scale).astype(BF16)
        qkv_s[here, 128:256] = key.astype(BF16)
        qkv_s[here, 256:384] = pre[:, 256:384].astype(BF16)
        qkv_s[here, 384:512] = (jnp.where(low_lane, mixed, 0.0).astype(BF16) * scale).astype(BF16)
        qkv_s[here, 512:640] = pre[:, 512:640].astype(BF16)
        k2_s[here, :] = jnp.where(low_lane, pltpu.roll(mixed, 64, 1), 0.0).astype(BF16)

    project_rows(slot)
    ag_mate(0, x_all)
    project_rows(mate_slot)
    ag_far(0, x_all)
    project_rows(far_slot)
    ag_last(0, x_all)
    project_rows(last_slot)

    def masked(block, head):
        if head == 2:
            return block
        keep = low_lane if head == 0 else ~low_lane
        return jnp.where(keep, block, jnp.zeros_like(block))

    def attend(s, carry):
        here = take(s)
        same = seg_cols[here, 0:1] == seg_row
        outs = []
        for head in range(3):
            q_at, v_at = (0, 256) if head < 2 else (384, 512)
            query = masked(qkv_s[here, q_at:q_at + 128], head)
            keys = qkv_s[:, 128:256] if head < 2 else k2_s[...]
            scores = jnp.where(same, nt(query, keys), -1e30)
            scores = jnp.exp(scores - jnp.max(scores, axis=1, keepdims=True))
            weight = scores / jnp.sum(scores, axis=1, keepdims=True)
            probs[head, here, :] = weight
            weight_low = weight.astype(BF16)
            probs_low[head, here, :] = weight_low
            outs.append(nn(weight_low, qkv_s[:, v_at:v_at + 128]))
        o_s[here, 0:128] = jnp.where(low_lane, outs[0], outs[1]).astype(BF16)
        o_s[here, 128:256] = outs[2].astype(BF16)
        return carry

    lax.fori_loop(0, 4, attend, 0)

    if tight:
        @pl.when(home)
        def _():
            to_out.wait()

        @pl.when(away)
        def _():
            for j in range(3):
                spread_in(OUT, j).wait_recv()
    else:
        to_out.wait()

    reduce_scatter(0, lambda s: nn(o_s[take(s), :], wo[...]))
    first_in = reduced(0) + x_all[slot].astype(F32) + small_v[B_OUT:B_OUT + 1, :]
    normal1, factor1 = norm_stats(first_in)
    normed = normal1 * small_v[G_MIX:G_MIX + 1, :] + small_v[S_MIX:S_MIX + 1, :]
    h_own[0] = normed
    h_own[1] = normal1
    h_all[slot] = normed.astype(BF16)
    ag_own(1, h_all)

    if tight:
        @pl.when(home)
        def _():
            to_up.wait()
            to_down.wait()

        @pl.when(away)
        def _():
            for i in (UP, DOWN):
                for j in range(3):
                    spread_in(i, j).wait_recv()
    else:
        to_up.wait()
        to_down.wait()

    def feed(s):
        here = take(s)
        h = h_all[s]
        h_t[:, here] = jnp.transpose(h)
        z = nn(h, wu[...]) + small_v[B_UP:B_UP + 1, :]
        phi = 0.5 * (1.0 + lax.erf(z * (2.0 ** -0.5)))
        act[here, :] = (z * phi).astype(BF16)
        dgelu[here, :] = phi + z * (jnp.exp(-0.5 * z * z) * (1.0 / math.sqrt(2.0 * math.pi)))

    feed(slot)
    ag_mate(1, h_all)
    feed(mate_slot)
    ag_far(1, h_all)
    feed(far_slot)
    ag_last(1, h_all)
    feed(last_slot)
    reduce_scatter(1, lambda s: nn(act[take(s), :], wd[...]))
    second_in = reduced(1) + h_own[0] + small_v[B_DOWN:B_DOWN + 1, :]
    normal2, factor2 = norm_stats(second_in)
    out_rows = normal2 * small_v[G_FEED:G_FEED + 1, :] + small_v[S_FEED:S_FEED + 1, :]
    parts[4, 0] = out_rows.astype(BF16)

    def hand_out(i, src, dst):
        keep = local(src, dst, out_r.at[i])
        if not tight:
            keep.start()
            return
        pl.when(home)(keep.start)
        pl.when(away)(copy_to(src, dst, out_s.at[i], out_r.at[i], partner).start)

    hand_out(0, parts.at[4, 0], result_o)
    to_cot.wait()
    dy = cot_v[...].astype(F32)
    grad2 = norm_back(dy, normal2, factor2, small_v[G_FEED:G_FEED + 1, :])
    vec[3:4, :] = jnp.sum(grad2, axis=0, keepdims=True)
    vec[4:5, :] = jnp.sum(dy * normal2, axis=0, keepdims=True)
    vec[5:6, :] = jnp.sum(dy, axis=0, keepdims=True)
    g_own[0] = grad2
    g2_all[slot] = grad2.astype(BF16)
    ag_own(2, g2_all)

    def feed_back(s):
        here = take(s)
        g = g2_all[s]
        g2_t[:, here] = jnp.transpose(g)
        dz_s[here, :] = (nt(g, wd[...]) * dgelu[here, :]).astype(BF16)

    feed_back(slot)
    ag_mate(2, g2_all)
    feed_back(mate_slot)
    ag_far(2, g2_all)
    feed_back(far_slot)
    ag_last(2, g2_all)
    feed_back(last_slot)
    reduce_scatter(2, lambda s: nt(dz_s[take(s), :], wu[...]))

    def weight_grad(i, left, right):
        width = right.shape[1]
        size = left.shape[0] // 4

        def step(q, carry):
            at = pl.ds(pl.multiple_of(q * size, size), size)
            grad_pieces[i][q] = nn(left[at, :], right[...]).astype(BF16)
            return carry

        lax.fori_loop(0, 4, step, 0)
        if tight:
            for j in range(3):
                to = lax.rem(col + 1 + j, 4)
                copy_to(
                    grad_pieces[i].at[to], grads_in[i].at[j], dx_s.at[i, j], dx_r.at[i, j], cols[j]
                ).start()

    def grads_land(i):
        for j in range(3):
            to = lax.rem(col + 1 + j, 4)
            copy_to(
                grad_pieces[i].at[to], grads_in[i].at[j], dx_s.at[i, j], dx_r.at[i, j], cols[j]
            ).wait_recv()
        total = grad_pieces[i][col].astype(F32)
        for j in range(3):
            total = total + grads_in[i][j].astype(F32)
        grads_sum[i][...] = total.astype(BF16).reshape(grads_sum[i].shape)

        @pl.when(home)
        def _():
            keep_sum(i).start()
            mate_sum(i).start()

        @pl.when(away)
        def _():
            for copy in away_sums(i):
                copy.start()

    def keep_sum(i):
        return local(grads_sum[i].at[core], sums_a[i], dz_sem_r.at[i, 0])

    def mate_sum(i):
        return copy_to(
            grads_sum[i].at[1 - core], sums_a[i], dz_sem_s.at[i, 0], dz_sem_r.at[i, 0], mate
        )

    def away_sums(i):
        return (
            copy_to(
                grads_sum[i].at[core], sums_b[i], dz_sem_s.at[i, 0], dz_sem_r.at[i, 1], across
            ),
            copy_to(
                grads_sum[i].at[1 - core], sums_b[i], dz_sem_s.at[i, 1], dz_sem_r.at[i, 1], partner
            ),
        )

    weight_grad(DOWN, g2_t, act)
    weight_grad(UP, h_t, dz_s)
    vec[6:7, :] = jnp.sum(dz_s[...].astype(F32), axis=0, keepdims=True)

    dh = reduced(2) + g_own[0]
    normal1 = h_own[1]
    grad1 = norm_back(dh, normal1, factor1, small_v[G_MIX:G_MIX + 1, :])
    vec[0:1, :] = jnp.sum(grad1, axis=0, keepdims=True)
    vec[1:2, :] = jnp.sum(dh * normal1, axis=0, keepdims=True)
    vec[2:3, :] = jnp.sum(dh, axis=0, keepdims=True)
    g_own[1] = grad1
    g1_all[slot] = grad1.astype(BF16)
    ag_own(3, g1_all)

    def heads_back(s):
        here = take(s)
        g = g1_all[s]
        g1_t[:, here] = jnp.transpose(g)
        do_s[here, :] = nt(g, wo[...]).astype(BF16)

    heads_back(slot)
    ag_mate(3, g1_all)
    heads_back(mate_slot)
    ag_far(3, g1_all)
    heads_back(far_slot)
    ag_last(3, g1_all)
    heads_back(last_slot)
    weight_grad(OUT, g1_t, o_s)

    q_t[0:128, :] = jnp.transpose(qkv_s[:, 0:128])
    q_t[128:256, :] = jnp.transpose(qkv_s[:, 384:512])
    do_t[0:128, :] = jnp.transpose(do_s[:, 0:128])
    do_t[128:256, :] = jnp.transpose(do_s[:, 128:256])

    def back(values, here):
        return values * cos_t[here, :] - turn(values) * sin_t[here, :]

    def attend_back(s, carry):
        here = take(s)
        outs = []
        for head in range(3):
            v_at, o_at = (256, 0) if head < 2 else (512, 128)
            grad_o = masked(do_s[here, o_at:o_at + 128], head)
            grad_p = nt(grad_o, qkv_s[:, v_at:v_at + 128])
            weight = probs[head, here, :]
            dot = jnp.sum(grad_p * weight, axis=1, keepdims=True)
            ds = (weight * (grad_p - dot)).astype(BF16)
            ds_s[head, here, :] = ds
            keys = qkv_s[:, 128:256] if head < 2 else k2_s[...]
            outs.append(nn(ds, keys) * HD ** (-0.5))
        dqkv_s[here, 0:128] = back(jnp.where(low_lane, outs[0], outs[1]), here).astype(BF16)
        dqkv_s[here, 384:512] = back(outs[2], here).astype(BF16)
        return carry

    lax.fori_loop(0, 4, attend_back, 0)
    for head in range(3):
        at = slice(head * 64, head * 64 + 64)
        dk_t[at, :] = nn(q_t[at, :], ds_s[head])
        dv_t[at, :] = nn(do_t[at, :], probs_low[head])
    dk_t[192:, :] = jnp.zeros((64, length), F32)
    dv_t[192:, :] = jnp.zeros((64, length), F32)

    everything = slice(None)
    dqkv_s[:, 128:256] = back(jnp.transpose(dk_t[0:128, :]), everything).astype(BF16)
    key2 = back(jnp.transpose(dk_t[128:256, :]), everything)
    query2 = dqkv_s[:, 384:512].astype(F32)
    dqkv_s[:, 384:512] = jnp.where(low_lane, query2, pltpu.roll(key2, 64, 1)).astype(BF16)
    dqkv_s[:, 256:384] = jnp.transpose(dv_t[0:128, :]).astype(BF16)
    dqkv_s[:, 512:640] = jnp.transpose(dv_t[128:256, :]).astype(BF16)

    reduce_scatter(3, lambda s: nt(dqkv_s[take(s), :], wqkv[...]))
    weight_grad(QKV, x_t, dqkv_s)
    vec[7:8, 0:640] = jnp.sum(dqkv_s[...].astype(F32), axis=0, keepdims=True)
    vec[7:8, 640:] = jnp.zeros((1, vec.shape[1] - 640), F32)

    if tight:
        for j in range(3):
            copy_to(vec, vec_in.at[j], vx_s.at[j], vx_r.at[j], cols[j]).start()
        grads_land(DOWN)
        grads_land(UP)

    parts[4, 1] = (reduced(3) + g_own[1]).astype(BF16)
    hand_out(1, parts.at[4, 1], grad_o)

    if tight:
        for j in range(3):
            copy_to(vec, vec_in.at[j], vx_s.at[j], vx_r.at[j], cols[j]).wait_recv()
        mine = half * 4 + slot
        vec_col[mine] = vec[...] + vec_in[0] + vec_in[1] + vec_in[2]
        column = list(all_column())
        for j, device in enumerate(column):
            copy_to(vec_col.at[mine], vec_col.at[mine], vc_s.at[j], vc_r.at[j], device).start()
        grads_land(OUT)
        grads_land(QKV)

        sources = [(core, lax.rem(ten + 4 - dz, 4)) for dz in (1, 2, 3)]
        sources += [(1 - core, lax.rem(ten + 4 - dz, 4)) for dz in (0, 1, 2, 3)]
        for j, (core_j, ten_j) in enumerate(sources):
            at = (ten_j // 2) * 4 + lax.rem(ten_j, 2) + 2 * core_j
            ref = vec_col.at[at]
            copy_to(ref, ref, vc_s.at[j], vc_r.at[j], column[j]).wait_recv()
        keep = local(vec_col, vec_o, loc.at[6])
    else:
        keep = local(vec, vec_o, loc.at[6])
    keep.start()

    if not tight:
        outs = [local(grad_pieces[i], sums_a[i], dx_s.at[i, 0]) for i in range(4)]
        for copy in outs:
            copy.start()
        for copy in outs:
            copy.wait()
    local(parts.at[4, 0], result_o, out_r.at[0]).wait()
    local(parts.at[4, 1], grad_o, out_r.at[1]).wait()
    for i, buf in enumerate((x_all, h_all, g2_all, g1_all)):
        ag_done(i, buf)
        for j in range(3):
            rs_copy(i, j).wait_send()
    keep.wait()
    if tight:
        for i in range(4):
            keep_sum(i).wait()
            away_sums(i)[0].wait_recv()
            for j in range(3):
                to = lax.rem(col + 1 + j, 4)
                copy_to(
                    grad_pieces[i].at[to], grads_in[i].at[j], dx_s.at[i, j], dx_r.at[i, j], cols[j]
                ).wait_send()
        for j in range(3):
            copy_to(vec, vec_in.at[j], vx_s.at[j], vx_r.at[j], cols[j]).wait_send()
        for j, device in enumerate(column):
            copy_to(
                vec_col.at[mine], vec_col.at[mine], vc_s.at[j], vc_r.at[j], device
            ).wait_send()

        @pl.when(home)
        def _():
            for i in range(4):
                mate_sum(i).wait_send()

        @pl.when(away)
        def _():
            for i in range(4):
                for copy in away_sums(i):
                    copy.wait_send()
                for j in range(3):
                    spread(i, j).wait_send()
                swap_weight(i).wait_send()
            for copy in swap_arrays():
                copy.wait_send()
            copy_to(parts.at[4, 0], result_o, out_s.at[0], out_r.at[0], partner).wait_send()
            copy_to(parts.at[4, 1], grad_o, out_s.at[1], out_r.at[1], partner).wait_send()


def layer_call(tight, tokens, cotangent, small, w_query, w_key, w_value, w_out, w_up, w_down):
    rows, width = tokens.shape
    hidden = w_up.shape[1]
    length = 4 * rows
    heads_wide, qkv_wide = 256, 640
    widths = (hidden, hidden, heads_wide, qkv_wide)
    any_space = pl.BlockSpec(memory_space=pl.ANY)
    vmem = pl.BlockSpec(memory_space=pltpu.VMEM)
    slice_rows = width // 8
    if tight:
        sums = [jax.ShapeDtypeStruct((slice_rows, w), BF16) for w in widths]
        vec_shape = jax.ShapeDtypeStruct((8, 8, width), F32)
    else:
        sums = [jax.ShapeDtypeStruct((4, width // 4, w), BF16) for w in widths]
        vec_shape = jax.ShapeDtypeStruct((8, width), F32)
    sums_b = [jax.ShapeDtypeStruct((slice_rows, w), BF16) for w in widths]
    out_shape = (
        jax.ShapeDtypeStruct((rows, width), BF16),
        jax.ShapeDtypeStruct((rows, width), BF16),
        sums,
        sums_b,
        vec_shape,
    )
    V = pltpu.VMEM
    D = pltpu.SemaphoreType.DMA
    scratch = [
        *[V((4, rows, width), BF16)] * 4,
        *[V((width, length), BF16)] * 4,
        V((5, 2, rows, width), BF16), V((4, 3, rows, width), BF16), V((4, rows, width), BF16),
        V((16, width), F32), V((rows, width), BF16), V((3, width, 192), BF16),
        V((width // 4, qkv_wide), BF16), V((width, qkv_wide), BF16), V((heads_wide, width), BF16),
        V((width, hidden), BF16), V((hidden, width), BF16),
        V((length, 128), F32), V((length, 128), F32), V((length, 128), F32),
        V((length, qkv_wide), BF16), V((length, 128), BF16), V((3, length, length), F32),
        V((3, length, length), BF16), V((3, length, length), BF16), V((length, heads_wide), BF16),
        V((length, hidden), BF16), V((length, hidden), F32), V((length, hidden), BF16),
        V((length, heads_wide), BF16), V((length, qkv_wide), BF16),
        V((heads_wide, length), BF16), V((heads_wide, length), BF16),
        V((heads_wide, length), F32), V((heads_wide, length), F32),
        V((2, rows, width), F32), V((2, rows, width), F32), V((rows, width), F32),
        [V((4, width // 4, w), BF16) for w in widths],
        [V((3, width // 4, w), BF16) for w in widths],
        [V((2, width // 8, w), BF16) for w in widths],
        V((8, width), F32), V((3, 8, width), F32), V((8, 8, width), F32),
        D((4, 3)), D((4, 3)), D((4, 3)), D((4, 3)), D((7,)), D((7,)), D((4, 3)), D((4, 3)),
        D((4, 3)), D((4, 3)), D((4, 2)), D((4, 2)), D((3,)), D((3,)), D((7,)), D((7,)),
        D((2,)), D((2,)), D((7,)),
    ]
    return pl.pallas_call(
        partial(layer_kernel, tight),
        out_shape=out_shape,
        in_specs=[any_space] * 9,
        out_specs=jax.tree.map(lambda _: any_space, out_shape),
        scratch_shapes=scratch,
        compiler_params=pltpu.CompilerParams(
            collective_id=0, has_side_effects=True, vmem_limit_bytes=60 << 20
        ),
    )(tokens, cotangent, small, w_query, w_key, w_value, w_out, w_up, w_down)


def split_qkv(block):
    query = jnp.concatenate([block[..., :128], block[..., 384:448]], axis=-1)
    key = jnp.concatenate([block[..., 128:256], block[..., 448:512]], axis=-1)
    value = jnp.concatenate([block[..., 256:384], block[..., 512:576]], axis=-1)
    return query, key, value


def on_device(
    tight,
    tokens,
    segment_ids,
    w_query,
    b_query,
    w_key,
    b_key,
    w_value,
    b_value,
    w_out,
    b_out,
    gain_mixer,
    shift_mixer,
    w_up,
    b_up,
    w_down,
    b_down,
    gain_feed,
    shift_feed,
    cotangent,
):
    width = tokens.shape[1]
    vectors = [
        jnp.concatenate(
            [
                b_query[:128], b_key[:128], b_value[:128],
                b_query[128:], b_key[128:], b_value[128:],
                jnp.zeros((width - 576,), b_query.dtype),
            ]
        ),
        b_up, b_out, gain_mixer, shift_mixer, b_down, gain_feed, shift_feed,
    ]
    segment_row = jnp.pad(segment_ids[0].astype(F32), (0, width - segment_ids.shape[1]))
    small = jnp.concatenate(
        [
            jnp.stack(vectors).astype(F32),
            jnp.broadcast_to(segment_row[None], (8, width)),
        ]
    )
    result, grad_rows, sums_a, sums_b, vec = layer_call(
        tight, tokens, cotangent, small, w_query, w_key, w_value, w_out, w_up, w_down
    )
    grad_tokens = grad_rows.astype(F32)
    if tight:
        down, up, out, qkv = (
            a.astype(F32) + b.astype(F32) for a, b in zip(sums_a, sums_b)
        )
        totals = jnp.sum(vec, axis=0)
        by_slot = vec[:4] + vec[4:]
        bias_up = by_slot[:, 6].reshape(-1)
        biases = [b.reshape(-1) for b in split_qkv(by_slot[:, 7, :640])]
        sum_query, sum_key, sum_value = split_qkv(qkv)
        sum_out, sum_down, sum_up = out[:, :192].T, down.T, up
    else:
        flat = [a.reshape(width, a.shape[-1]).astype(F32) for a in sums_a]
        scatter = partial(lax.psum_scatter, axis_name="dp", scatter_dimension=0, tiled=True)
        sum_query, sum_key, sum_value = (scatter(b) for b in split_qkv(flat[QKV]))
        sum_out, sum_down = scatter(flat[OUT][:, :192]).T, scatter(flat[DOWN]).T
        sum_up = scatter(flat[UP])
        totals = lax.psum(vec, ("dp", "tensor"))
        by_slot = lax.all_gather(lax.psum(vec[6:], "dp"), "tensor")
        bias_up = by_slot[:, 0].reshape(-1)
        biases = [b.reshape(-1) for b in split_qkv(by_slot[:, 1, :640])]
    return (
        result,
        grad_tokens,
        sum_query,
        biases[0],
        sum_key,
        biases[1],
        sum_value,
        biases[2],
        sum_out,
        totals[0],
        totals[1],
        totals[2],
        sum_up,
        bias_up,
        sum_down,
        totals[3],
        totals[4],
        totals[5],
    )


def solution(mesh):
    in_specs = (
        P(("dp", "tensor"), None),
        P("dp", None),
        P(None, "tensor"),
        P("tensor"),
        P(None, "tensor"),
        P("tensor"),
        P(None, "tensor"),
        P("tensor"),
        P("tensor", None),
        P(),
        P(),
        P(),
        P(None, "tensor"),
        P("tensor"),
        P("tensor", None),
        P(),
        P(),
        P(),
        P(("dp", "tensor"), None),
    )
    out_specs = (
        P(("dp", "tensor"), None),
        P(("dp", "tensor"), None),
        P("dp", "tensor"),
        P(),
        P("dp", "tensor"),
        P(),
        P("dp", "tensor"),
        P(),
        P("tensor", "dp"),
        P(),
        P(),
        P(),
        P("dp", "tensor"),
        P(),
        P("tensor", "dp"),
        P(),
        P(),
        P(),
    )
    tight = mesh.shape["dp"] == 8
    return jax.shard_map(
        partial(on_device, tight), mesh=mesh, in_specs=in_specs, out_specs=out_specs,
        check_vma=False,
    )
```

```python
from functools import partial
import math

import jax
import jax.numpy as jnp
from jax import lax
from jax.experimental import pallas as pl
from jax.experimental.pallas import tpu as pltpu
from jax.sharding import PartitionSpec as P

HD = 64
MESH = pl.DeviceIdType.MESH
F32 = jnp.float32
BF16 = jnp.bfloat16
LN_EPS = 1e-12
B_QKV, B_UP, B_OUT, G_MIX, S_MIX, B_DOWN, G_FEED, S_FEED = range(8)
DOWN, UP, OUT, QKV = range(4)


def nn(left, right):
    return lax.dot_general(left, right, (((1,), (0,)), ((), ())), preferred_element_type=F32)


def nt(left, right):
    return lax.dot_general(left, right, (((1,), (1,)), ((), ())), preferred_element_type=F32)


def norm_stats(values):
    centered = values - jnp.mean(values, axis=-1, keepdims=True)
    factor = lax.rsqrt(jnp.mean(centered * centered, axis=-1, keepdims=True) + LN_EPS)
    return centered * factor, factor


def norm_back(grads, normalized, factor, gain):
    scaled = grads * gain
    first = jnp.mean(scaled, axis=-1, keepdims=True)
    second = jnp.mean(scaled * normalized, axis=-1, keepdims=True)
    return factor * (scaled - first - normalized * second)


def copy_to(src, dst, send, recv, device):
    return pltpu.make_async_remote_copy(
        src_ref=src, dst_ref=dst, send_sem=send, recv_sem=recv, device_id=device,
        device_id_type=MESH,
    )


def layer_kernel(
    tight,
    tokens, cotangent, wq_t, wk_t, wv_t, w_out, w_up, w_down,
    segment_ids, b_query, b_key, b_value, b_up, b_out, gain_mixer, shift_mixer, b_down,
    gain_feed, shift_feed,
    result_o, grad_o, sums_a, sums_b, vec_o, bias_o,
    x_all, h_all, g2_all, g1_all, x_t, h_t, g2_t, g1_t,
    part_last, part_mate, land_last, land_mate, land_far, passed, out_rows,
    small_own, small_v, cot_v, staged, wqkv, wo, wu, wd,
    seg_nat, seg_cols, cos_t, sin_t,
    qkv_s, k2_s, probs, probs_low, ds_s, o_s, act, dgelu, dz_s, do_s, dqkv_s,
    q_t, do_t, dk_t, dv_t, h_own, g_own, own_part,
    grads, first_in, second_in, grads_mid, grads_in, grads_sum,
    vec, vec_in, vec_col, bias, bias_in, bias_col,
    ag_s, ag_r, rs_s, rs_r, sw_s, sw_r, wx_s, wx_r, dx_s, dx_r, dq_s, dq_r, dz_sem_s, dz_sem_r,
    vx_s, vx_r, vc_s, vc_r, bx_s, bx_r, bc_s, bc_r, out_s, out_r, loc,
):
    dp, ten = lax.axis_index("dp"), lax.axis_index("tensor")
    low = lax.rem(ten, 2)
    if tight:
        col, core, half = dp // 2, lax.rem(dp, 2), ten // 2
        col_x, col_y = lax.rem(col, 2), col // 2
        slot = low + 2 * core
        mate_slot = low + 2 * (1 - core)
        far_slot = 1 - low + 2 * core
        last_slot = 1 - low + 2 * (1 - core)
        mate = {"dp": col * 2 + 1 - core, "tensor": ten}
        far = {"dp": dp, "tensor": ten + 1 - 2 * low}
        other = lax.rem(ten + 2, 4)
        partner = {"dp": col * 2 + 1 - core, "tensor": other}
        across = {"dp": dp, "tensor": other}
        cols = [{"dp": lax.rem(col + j, 4) * 2 + core, "tensor": ten} for j in (1, 2, 3)]
        next_x = {"dp": (col_y * 2 + 1 - col_x) * 2 + core, "tensor": ten}
        next_y = {"dp": ((1 - col_y) * 2 + col_x) * 2 + core, "tensor": ten}
        home = core == half
        away = core != half
        column = [{"dp": dp, "tensor": lax.rem(ten + dz, 4)} for dz in (1, 2, 3)]
        column += [
            {"dp": col * 2 + 1 - core, "tensor": lax.rem(ten + dz, 4)} for dz in (0, 1, 2, 3)
        ]
        met = column + cols
    else:
        slot = ten
        mate_slot = ten + 1 - 2 * low
        far_slot = lax.rem(ten + 2, 4)
        last_slot = 3 - ten
        mate = {"dp": dp, "tensor": mate_slot}
        far = {"dp": dp, "tensor": far_slot}
        met = [mate, far]

    rows, width = tokens.shape
    length = 4 * rows
    chunk = rows // 2
    units = ((0, 2 * rows), (2 * rows, rows), (3 * rows, rows))

    def local(src, dst, sem):
        return pltpu.make_async_copy(src, dst, sem)

    raw = []
    qkv_ref = staged if tight else wqkv
    for i, w in enumerate((wq_t, wk_t, wv_t)):
        raw.append((w.at[pl.ds(0, 128)], i * 128, 128))
        raw.append((w.at[pl.ds(128, 64)], 384 + i * 64, 64))

    def raw_copy(i, ref):
        src, at, size = raw[i]
        return local(src, ref.at[pl.ds(at, size)], loc.at[i])

    to_tokens = [
        local(tokens.at[pl.ds(c * chunk, chunk)], x_all.at[pl.ds(c * chunk, chunk)], sw_r.at[4 + c])
        for c in range(2)
    ]
    to_small = local(small_own, small_v, sw_r.at[0])
    to_cot = local(cotangent, cot_v, sw_r.at[11])
    wo_rows = w_out.shape[0]
    to_out = local(w_out, wo.at[pl.ds(0, wo_rows)], loc.at[6])
    to_up = local(w_up, wu, loc.at[7])
    to_down = local(w_down, wd, loc.at[8])

    def load_own():
        for copy in to_tokens:
            copy.start()
        for i in range(6):
            raw_copy(i, wqkv).start()
        for copy in (to_out, to_up, to_down, to_cot):
            copy.start()

    def stage_own():
        for i in range(6):
            raw_copy(i, staged).start()

    if tight:
        pl.when(home)(load_own)
        pl.when(away)(stage_own)
    else:
        load_own()

    barrier = pltpu.get_barrier_semaphore()
    for device in met:
        pl.semaphore_signal(barrier, inc=1, device_id=device, device_id_type=MESH)
    wo[wo_rows:, :] = jnp.zeros((wo.shape[0] - wo_rows, width), BF16)
    wqkv[576:, :] = jnp.zeros((wqkv.shape[0] - 576, width), BF16)

    def vector(ref):
        return ref[...].astype(F32).reshape(1, ref.shape[0])

    bq, bk, bv = vector(b_query), vector(b_key), vector(b_value)
    for i, b in enumerate((bq, bk, bv)):
        small_own[0:1, i * 128:(i + 1) * 128] = b[:, :128]
    small_own[0:1, 384:512] = jnp.concatenate([bq[:, 128:], bk[:, 128:]], axis=1)
    small_own[0:1, 512:640] = jnp.concatenate([bv[:, 128:], jnp.zeros((1, 64), F32)], axis=1)
    small_own[0:1, 640:] = jnp.zeros((1, width - 640), F32)
    for at, ref in (
        (B_UP, b_up), (B_OUT, b_out), (G_MIX, gain_mixer), (S_MIX, shift_mixer),
        (B_DOWN, b_down), (G_FEED, gain_feed), (S_FEED, shift_feed),
    ):
        small_own[at:at + 1, :] = vector(ref)
    small_own[8:16, :] = jnp.zeros((8, width), F32)
    small_own[8:9, :length] = segment_ids[...].astype(F32)
    pl.semaphore_wait(barrier, len(met))

    weight_items = {
        1: (wqkv, staged, 576, 0, 3), 2: (wqkv, staged, 576, 1, 3), 3: (wqkv, staged, 576, 2, 3),
        6: (wo, w_out, wo_rows, 0, 1),
        7: (wu, w_up, width, 0, 2), 8: (wu, w_up, width, 1, 2),
        9: (wd, w_down, width, 0, 2), 10: (wd, w_down, width, 1, 2),
    }
    item_rank = {item: i for i, item in enumerate(weight_items)}

    def item_rows(item, q):
        _, _, total, part, count = weight_items[item]
        size = total // 4 // count
        return pl.ds(q * (total // 4) + part * size, size)

    def swap(item):
        if item in weight_items:
            dst, src = weight_items[item][:2]
            at = item_rows(item, col)
            src, dst = src.at[at], dst.at[at]
        elif item == 0:
            src, dst = small_own, small_v
        elif item == 11:
            src, dst = cotangent, cot_v
        else:
            at = pl.ds((item - 4) * chunk, chunk)
            src, dst = tokens.at[at], x_all.at[at]
        return copy_to(src, dst, sw_s.at[item], sw_r.at[item], partner)

    def spread(item, j):
        ref = weight_items[item][0].at[item_rows(item, col)]
        rank = item_rank[item]
        return copy_to(ref, ref, wx_s.at[rank, j], wx_r.at[rank, j], cols[j])

    def spread_in(item, j):
        ref = weight_items[item][0].at[item_rows(item, lax.rem(col + 3 - j, 4))]
        rank = item_rank[item]
        return copy_to(ref, ref, wx_s.at[rank, j], wx_r.at[rank, j], cols[j])

    def relay(*items):
        if tight:
            @pl.when(away)
            def _():
                for item in items:
                    swap(item).wait_recv()
                    for j in range(3):
                        spread(item, j).start()

    def weights_ready(copies, *items):
        if not tight:
            for copy in copies:
                copy.wait()
            return

        @pl.when(home)
        def _():
            for copy in copies:
                copy.wait()

        @pl.when(away)
        def _():
            for item in items:
                for j in range(3):
                    spread_in(item, j).wait_recv()

    if tight:
        @pl.when(away)
        def _():
            swap(0).start()
            for i in range(6):
                raw_copy(i, staged).wait()
            for item in (1, 2, 3, 4, 5):
                swap(item).start()

        pl.when(home)(to_small.start)
    else:
        to_small.start()

    def at_own(c):
        return pl.ds(c * chunk, chunk)

    def at_mate(c):
        return pl.ds(rows + c * chunk, chunk)

    def at_far(c):
        return pl.ds(2 * rows + 2 * c * chunk, chunk)

    def at_last(c):
        return pl.ds(2 * rows + (2 * c + 1) * chunk, chunk)

    def gather_copy(i, buf, c, kind):
        src, dst, device = (
            (at_own(c), at_mate(c), mate), (at_own(c), at_far(c), far), (at_far(c), at_last(c), mate)
        )[kind]
        return copy_to(
            buf.at[src], buf.at[dst], ag_s.at[i, c, kind], ag_r.at[i, c, kind], device
        )

    def ag_own(i, buf, c):
        gather_copy(i, buf, c, 1).start()
        gather_copy(i, buf, c, 0).start()

    def ag_mate(i, buf):
        for c in range(2):
            gather_copy(i, buf, c, 0).wait_recv()

    def ag_unit(i, buf, c):
        gather_copy(i, buf, c, 1).wait_recv()
        gather_copy(i, buf, c, 2).start()
        gather_copy(i, buf, c, 2).wait_recv()

    def rs_copy(i, c, kind):
        src, dst, device = (
            (part_last.at[i, c], land_last.at[i, c], mate),
            (part_mate.at[i, c], land_mate.at[i, c], mate),
            (passed.at[i, c], land_far.at[i, c], far),
        )[kind]
        return copy_to(src, dst, rs_s.at[i, c, kind], rs_r.at[i, c, kind], device)

    def rs_unit(i, c, term):
        part_last[i, c] = term[chunk:].astype(BF16)
        rs_copy(i, c, 0).start()
        own_part[rows + c * chunk:rows + (c + 1) * chunk, :] = term[:chunk]

    def rs_pass(i, c):
        rs_copy(i, c, 0).wait_recv()
        term = own_part[rows + c * chunk:rows + (c + 1) * chunk, :]
        passed[i, c] = (term + land_last[i, c].astype(F32)).astype(BF16)
        rs_copy(i, c, 2).start()

    def rs_mate(i, term):
        for c in range(2):
            part_mate[i, c] = term[rows + c * chunk:rows + (c + 1) * chunk].astype(BF16)
            rs_copy(i, c, 1).start()
        own_part[0:rows, :] = term[:rows]

    def reduced(i, c):
        rs_copy(i, c, 1).wait_recv()
        rs_copy(i, c, 2).wait_recv()
        term = own_part[c * chunk:(c + 1) * chunk, :]
        return term + land_mate[i, c].astype(F32) + land_far[i, c].astype(F32)

    if not tight:
        for c in range(2):
            to_tokens[c].wait()
            ag_own(0, x_all, c)
    else:
        @pl.when(home)
        def _():
            for c in range(2):
                to_tokens[c].wait()
                ag_own(0, x_all, c)

    to_small.wait()
    seg_row = small_v[8:9, :length]
    seg_nat[...] = jnp.transpose(jnp.broadcast_to(seg_row, (128, length)))
    segs = seg_nat[...]
    place = lax.broadcasted_iota(jnp.int32, (length, 128), 0).astype(F32)
    start = jnp.zeros((length, 128), F32)
    for s in range(4):
        before = jnp.sum(jnp.where(seg_row < s, 1.0, 0.0), axis=1, keepdims=True)
        start = jnp.where(segs == s, before, start)
    cos_t[...] = place - start
    order = [(0, slot, 0), (1, slot, 1), (2, mate_slot, 0), (3, mate_slot, 1)]
    order += [(4, far_slot, 0), (5, last_slot, 0), (6, far_slot, 1), (7, last_slot, 1)]
    for to, from_slot, c in order:
        at = pl.ds(pl.multiple_of(from_slot * rows + c * chunk, chunk), chunk)
        seg_cols[to * chunk:(to + 1) * chunk, :] = seg_nat[at, :]
        sin_t[to * chunk:(to + 1) * chunk, :] = cos_t[at, :]
    lane = lax.broadcasted_iota(jnp.int32, (1, 128), 1)
    frequency = jnp.exp(lax.rem(lane, 32).astype(F32) * (-math.log(10000.0) / 32))
    sign = jnp.where(lax.rem(lane, 64) < 32, -1.0, 1.0)
    angle = sin_t[...] * frequency
    cos_t[...] = jnp.cos(angle)
    sin_t[...] = jnp.sin(angle) * sign
    seg_row = jnp.transpose(seg_cols[...])[0:1, :]

    if tight:
        @pl.when(away)
        def _():
            for item, follow in ((1, 6), (2, 7), (3, 8)):
                swap(item).wait_recv()
                for j in range(3):
                    spread(item, j).start()
                swap(follow).start()
            for c, follow in ((0, 9), (1, 10)):
                swap(4 + c).wait_recv()
                ag_own(0, x_all, c)
                swap(follow).start()
            swap(11).start()

    low_lane = lane < 64

    def turn(values):
        return jnp.where(
            lax.rem(lane, 64) < 32, pltpu.roll(values, 96, 1), pltpu.roll(values, 32, 1)
        )

    scale = HD ** (-0.5)

    def project_rows(lo, n):
        here = slice(lo, lo + n)
        x = x_all[here, :]
        pre = nt(x, wqkv[...]) + small_v[B_QKV:B_QKV + 1, :640]
        cosine, sine = cos_t[here, :], sin_t[here, :]

        def rot(block):
            return block * cosine + turn(block) * sine

        query, key, mixed = rot(pre[:, :128]), rot(pre[:, 128:256]), rot(pre[:, 384:512])
        qkv_s[here, 0:128] = (query.astype(BF16) * scale).astype(BF16)
        qkv_s[here, 128:256] = key.astype(BF16)
        qkv_s[here, 256:384] = pre[:, 256:384].astype(BF16)
        qkv_s[here, 384:512] = (jnp.where(low_lane, mixed, 0.0).astype(BF16) * scale).astype(BF16)
        qkv_s[here, 512:640] = pre[:, 512:640].astype(BF16)
        k2_s[here, :] = jnp.where(low_lane, pltpu.roll(mixed, 64, 1), 0.0).astype(BF16)
        x_t[:, here] = jnp.transpose(x)

    weights_ready([raw_copy(i, wqkv) for i in range(6)], 1, 2, 3)
    ag_mate(0, x_all)
    project_rows(*units[0])
    ag_unit(0, x_all, 0)
    project_rows(*units[1])
    ag_unit(0, x_all, 1)
    project_rows(*units[2])
    relay(6, 7)

    def masked(block, head):
        if head == 2:
            return block
        keep = low_lane if head == 0 else ~low_lane
        return jnp.where(keep, block, jnp.zeros_like(block))

    def attend(s, carry):
        here = pl.ds(pl.multiple_of(s * rows, rows), rows)
        same = seg_cols[here, 0:1] == seg_row
        outs = []
        for head in range(3):
            q_at, v_at = (0, 256) if head < 2 else (384, 512)
            query = masked(qkv_s[here, q_at:q_at + 128], head)
            keys = qkv_s[:, 128:256] if head < 2 else k2_s[...]
            scores = jnp.where(same, nt(query, keys), -1e30)
            scores = jnp.exp(scores - jnp.max(scores, axis=1, keepdims=True))
            weight = scores / jnp.sum(scores, axis=1, keepdims=True)
            probs[head, here, :] = weight
            weight_low = weight.astype(BF16)
            probs_low[head, here, :] = weight_low
            outs.append(nn(weight_low, qkv_s[:, v_at:v_at + 128]))
        o_s[here, 0:128] = jnp.where(low_lane, outs[0], outs[1]).astype(BF16)
        o_s[here, 128:256] = outs[2].astype(BF16)
        return carry

    def mix(lo, n):
        return nn(o_s[lo:lo + n, :], wo[...])

    attend(2, 0)
    weights_ready([to_out], 6)
    rs_unit(0, 0, mix(*units[1]))
    relay(8)
    attend(3, 0)
    rs_unit(0, 1, mix(*units[2]))
    rs_pass(0, 0)
    lax.fori_loop(0, 1, attend, 0)
    rs_pass(0, 1)
    relay(9)
    lax.fori_loop(1, 2, attend, 0)
    rs_mate(0, mix(*units[0]))
    factors = []

    def spot(c):
        return slice(c * chunk, (c + 1) * chunk)

    def row_of(at):
        return small_v[at:at + 1, :]

    for c in range(2):
        here = spot(c)
        into = reduced(0, c) + x_all[here, :].astype(F32) + row_of(B_OUT)
        normal1, factor1 = norm_stats(into)
        factors.append(factor1)
        normed = normal1 * row_of(G_MIX) + row_of(S_MIX)
        h_own[0, here, :] = normed
        h_own[1, here, :] = normal1
        h_all[here, :] = normed.astype(BF16)
        ag_own(1, h_all, c)
    relay(10)

    def feed(lo, n):
        here = slice(lo, lo + n)
        h = h_all[here, :]
        z = nn(h, wu[...]) + row_of(B_UP)
        phi = 0.5 * (1.0 + lax.erf(z * (2.0 ** -0.5)))
        act[here, :] = (z * phi).astype(BF16)
        dgelu[here, :] = phi + z * (jnp.exp(-0.5 * z * z) * (1.0 / math.sqrt(2.0 * math.pi)))

    def shrink(lo, n):
        return nn(act[lo:lo + n, :], wd[...])

    weights_ready([to_up], 7, 8)
    ag_mate(1, h_all)
    feed(*units[0])
    ag_unit(1, h_all, 0)
    feed(*units[1])
    weights_ready([to_down], 9, 10)
    rs_unit(1, 0, shrink(*units[1]))
    ag_unit(1, h_all, 1)
    rs_pass(1, 0)
    feed(*units[2])
    rs_unit(1, 1, shrink(*units[2]))
    rs_mate(1, shrink(*units[0]))
    rs_pass(1, 1)
    h_t[...] = jnp.transpose(h_all[...])

    def hand_out(i, src, dst, c):
        src, dst = src.at[pl.ds(c * chunk, chunk)], dst.at[pl.ds(c * chunk, chunk)]
        keep = local(src, dst, out_r.at[i, c])
        send = copy_to(src, dst, out_s.at[i, c], out_r.at[i, c], partner) if tight else None
        return keep, send

    def hand_start(*args):
        keep, send = hand_out(*args)
        if tight:
            pl.when(home)(keep.start)
            pl.when(away)(send.start)
        else:
            keep.start()

    to_cot.wait()
    sums = [0.0, 0.0, 0.0]
    for c in range(2):
        here = spot(c)
        into = reduced(1, c) + h_own[0, here, :] + row_of(B_DOWN)
        normal2, factor2 = norm_stats(into)
        dy = cot_v[here, :].astype(F32)
        grad2 = norm_back(dy, normal2, factor2, row_of(G_FEED))
        g_own[0, here, :] = grad2
        g2_all[here, :] = grad2.astype(BF16)
        ag_own(2, g2_all, c)
        out_rows[0, here, :] = (normal2 * row_of(G_FEED) + row_of(S_FEED)).astype(BF16)
        hand_start(0, out_rows.at[0], result_o, c)
        for i, term in enumerate((grad2, dy * normal2, dy)):
            sums[i] = sums[i] + jnp.sum(term, axis=0, keepdims=True)
    for i in range(3):
        vec[3 + i:4 + i, :] = sums[i]

    def feed_back(lo, n):
        here = slice(lo, lo + n)
        dz_s[here, :] = (nt(g2_all[here, :], wd[...]) * dgelu[here, :]).astype(BF16)

    def widen(lo, n):
        return nt(dz_s[lo:lo + n, :], wu[...])

    ag_mate(2, g2_all)
    feed_back(*units[0])
    ag_unit(2, g2_all, 0)
    feed_back(*units[1])
    rs_unit(2, 0, widen(*units[1]))
    ag_unit(2, g2_all, 1)
    rs_pass(2, 0)
    feed_back(*units[2])
    rs_unit(2, 1, widen(*units[2]))
    rs_mate(2, widen(*units[0]))
    rs_pass(2, 1)

    def weight_grad(i, left, right):
        quarter = width // 4

        def step(q, carry):
            at = pl.ds(pl.multiple_of(q * quarter, quarter), quarter)
            grads[i][q // 2, lax.rem(q, 2)] = nn(left[at, :], right[...]).astype(BF16)
            return carry

        lax.fori_loop(0, 4, step, 0)

    along_x = {DOWN: True, UP: False, OUT: True}

    def first_copy(i):
        if along_x[i]:
            src, device = grads[i].at[:, 1 - col_x], next_x
        else:
            src, device = grads[i].at[1 - col_y], next_y
        return copy_to(src, first_in[i], dx_s.at[i, 0], dx_r.at[i, 0], device)

    def second_copy(i):
        keep, device = (1 - col_y, next_y) if along_x[i] else (1 - col_x, next_x)
        return copy_to(
            grads_mid[i].at[keep], second_in[i], dx_s.at[i, 1], dx_r.at[i, 1], device
        )

    def first_land(i):
        if not tight:
            return
        first_copy(i).wait_recv()
        for j in range(2):
            own = grads[i][j, col_x] if along_x[i] else grads[i][col_y, j]
            grads_mid[i][j] = (own.astype(F32) + first_in[i][j].astype(F32)).astype(BF16)
        second_copy(i).start()

    def second_land(i):
        if not tight:
            return
        second_copy(i).wait_recv()
        own = grads_mid[i][col_y if along_x[i] else col_x]
        total = own.astype(F32) + second_in[i][...].astype(F32)
        finish_sum(i, total)

    def finish_sum(i, total):
        grads_sum[i][...] = total.astype(BF16).reshape(grads_sum[i].shape)

        @pl.when(home)
        def _():
            keep_sum(i).start()
            mate_sum(i).start()

        @pl.when(away)
        def _():
            for copy in away_sums(i):
                copy.start()

    def direct_copy(j):
        to = lax.rem(col + 1 + j, 4)
        return copy_to(
            grads[QKV].at[to // 2, lax.rem(to, 2)], grads_in.at[j], dq_s.at[j], dq_r.at[j], cols[j]
        )

    def keep_sum(i):
        return local(grads_sum[i].at[core], sums_a[i], dz_sem_r.at[i, 0])

    def mate_sum(i):
        return copy_to(
            grads_sum[i].at[1 - core], sums_a[i], dz_sem_s.at[i, 0], dz_sem_r.at[i, 0], mate
        )

    def away_sums(i):
        return (
            copy_to(
                grads_sum[i].at[core], sums_b[i], dz_sem_s.at[i, 0], dz_sem_r.at[i, 1], across
            ),
            copy_to(
                grads_sum[i].at[1 - core], sums_b[i], dz_sem_s.at[i, 1], dz_sem_r.at[i, 1], partner
            ),
        )

    def first_send(i):
        if tight:
            first_copy(i).start()

    g2_t[...] = jnp.transpose(g2_all[...])
    weight_grad(DOWN, g2_t, act)
    first_send(DOWN)
    weight_grad(UP, h_t, dz_s)
    first_send(UP)
    vec[6:7, :] = jnp.sum(dz_s[...].astype(F32), axis=0, keepdims=True)

    sums = [0.0, 0.0, 0.0]
    for c in range(2):
        here = spot(c)
        dh = reduced(2, c) + g_own[0, here, :]
        normal1 = h_own[1, here, :]
        grad1 = norm_back(dh, normal1, factors[c], row_of(G_MIX))
        g_own[1, here, :] = grad1
        g1_all[here, :] = grad1.astype(BF16)
        ag_own(3, g1_all, c)
        for i, term in enumerate((grad1, dh * normal1, dh)):
            sums[i] = sums[i] + jnp.sum(term, axis=0, keepdims=True)
    for i in range(3):
        vec[i:i + 1, :] = sums[i]
    vec[7:8, :] = jnp.zeros((1, width), F32)

    def vec_copy(j):
        return copy_to(vec, vec_in.at[j], vx_s.at[j], vx_r.at[j], cols[j])

    def bias_copy(j):
        return copy_to(bias, bias_in.at[j], bx_s.at[j], bx_r.at[j], cols[j])

    if tight:
        mine = half * 4 + slot
        for j in range(3):
            vec_copy(j).start()

    def column_out(j, ref, send, recv):
        return copy_to(ref.at[mine], ref.at[mine], send.at[j], recv.at[j], column[j])

    def column_in(j, ref, send, recv):
        core_j = core if j < 3 else 1 - core
        ten_j = lax.rem(ten + 3 - j, 4) if j < 3 else lax.rem(ten + 4 - (j - 3), 4)
        at = (ten_j // 2) * 4 + lax.rem(ten_j, 2) + 2 * core_j
        return copy_to(ref.at[at], ref.at[at], send.at[j], recv.at[j], column[j])

    def heads_back(lo, n):
        here = slice(lo, lo + n)
        do_s[here, :] = nt(g1_all[here, :], wo[...]).astype(BF16)

    def back(values, here):
        return values * cos_t[here, :] - turn(values) * sin_t[here, :]

    def attend_back(s, carry):
        here = pl.ds(pl.multiple_of(s * rows, rows), rows)
        outs = []
        for head in range(3):
            v_at, o_at = (256, 0) if head < 2 else (512, 128)
            grad_o = masked(do_s[here, o_at:o_at + 128], head)
            grad_p = nt(grad_o, qkv_s[:, v_at:v_at + 128])
            weight = probs[head, here, :]
            dot = jnp.sum(grad_p * weight, axis=1, keepdims=True)
            ds = (weight * (grad_p - dot)).astype(BF16)
            ds_s[head, here, :] = ds
            keys = qkv_s[:, 128:256] if head < 2 else k2_s[...]
            outs.append(nn(ds, keys) * scale)
        dqkv_s[here, 0:128] = back(jnp.where(low_lane, outs[0], outs[1]), here).astype(BF16)
        dqkv_s[here, 384:512] = back(outs[2], here).astype(BF16)
        return carry

    q_t[0:128, :] = jnp.transpose(qkv_s[:, 0:128])
    q_t[128:256, :] = jnp.transpose(qkv_s[:, 384:512])
    ag_mate(3, g1_all)
    heads_back(*units[0])
    lax.fori_loop(0, 2, attend_back, 0)
    ag_unit(3, g1_all, 0)
    heads_back(*units[1])
    first_land(DOWN)
    lax.fori_loop(2, 3, attend_back, 0)
    ag_unit(3, g1_all, 1)
    heads_back(*units[2])
    first_land(UP)
    lax.fori_loop(3, 4, attend_back, 0)
    g1_t[...] = jnp.transpose(g1_all[...])
    weight_grad(OUT, g1_t, o_s)
    first_send(OUT)
    do_t[0:128, :] = jnp.transpose(do_s[:, 0:128])
    do_t[128:256, :] = jnp.transpose(do_s[:, 128:256])
    for head in range(3):
        at = slice(head * 64, head * 64 + 64)
        dk_t[at, :] = nn(q_t[at, :], ds_s[head])
        dv_t[at, :] = nn(do_t[at, :], probs_low[head])
    dk_t[192:, :] = jnp.zeros((64, length), F32)
    dv_t[192:, :] = jnp.zeros((64, length), F32)

    everything = slice(None)
    dqkv_s[:, 128:256] = back(jnp.transpose(dk_t[0:128, :]), everything).astype(BF16)
    key2 = back(jnp.transpose(dk_t[128:256, :]), everything)
    query2 = dqkv_s[:, 384:512].astype(F32)
    dqkv_s[:, 384:512] = jnp.where(low_lane, query2, pltpu.roll(key2, 64, 1)).astype(BF16)
    dqkv_s[:, 256:384] = jnp.transpose(dv_t[0:128, :]).astype(BF16)
    dqkv_s[:, 512:640] = jnp.transpose(dv_t[128:256, :]).astype(BF16)

    weight_grad(QKV, x_t, dqkv_s)
    if tight:
        for j in range(3):
            direct_copy(j).start()

    def to_input(lo, n):
        return nn(dqkv_s[lo:lo + n, :], wqkv[...])

    rs_unit(3, 0, to_input(*units[1]))
    rs_unit(3, 1, to_input(*units[2]))
    rs_pass(3, 0)
    rs_pass(3, 1)
    rs_mate(3, to_input(*units[0]))
    total = jnp.sum(dqkv_s[...].astype(F32), axis=0, keepdims=True)
    bias[...] = jnp.zeros((8, 128), F32)
    for i in range(5):
        bias[i:i + 1, :] = total[:, i * 128:(i + 1) * 128]
    if tight:
        for j in range(3):
            bias_copy(j).start()
        second_land(DOWN)
        second_land(UP)
        for j in range(3):
            vec_copy(j).wait_recv()
        vec_col[mine] = vec[...] + vec_in[0] + vec_in[1] + vec_in[2]
        for j in range(7):
            column_out(j, vec_col, vc_s, vc_r).start()
        first_land(OUT)

    for c in range(2):
        here = spot(c)
        out_rows[1, here, :] = (reduced(3, c) + g_own[1, here, :]).astype(BF16)
        hand_start(1, out_rows.at[1], grad_o, c)

    if tight:
        for j in range(3):
            bias_copy(j).wait_recv()
        bias_col[mine] = bias[...] + bias_in[0] + bias_in[1] + bias_in[2]
        for j in range(7):
            column_out(j, bias_col, bc_s, bc_r).start()
        second_land(OUT)
        for j in range(3):
            direct_copy(j).wait_recv()
        total = grads[QKV][col_y, col_x].astype(F32)
        for j in range(3):
            total = total + grads_in[j].astype(F32)
        finish_sum(QKV, total)
        for j in range(7):
            column_in(j, vec_col, vc_s, vc_r).wait_recv()
            column_in(j, bias_col, bc_s, bc_r).wait_recv()
        keep = [local(vec_col, vec_o, loc.at[0]), local(bias_col, bias_o, loc.at[1])]
    else:
        keep = [local(vec, vec_o, loc.at[0]), local(bias, bias_o, loc.at[1])]
        keep += [local(grads[i], sums_a[i], loc.at[2 + i]) for i in range(4)]
    for copy in keep:
        copy.start()

    for i, dst in enumerate((result_o, grad_o)):
        for c in range(2):
            hand_out(i, out_rows.at[i], dst, c)[0].wait()
    for i, buf in enumerate((x_all, h_all, g2_all, g1_all)):
        for c in range(2):
            for kind in range(3):
                gather_copy(i, buf, c, kind).wait_send()
                rs_copy(i, c, kind).wait_send()
    for copy in keep:
        copy.wait()
    if tight:
        for i in range(4):
            keep_sum(i).wait()
            away_sums(i)[0].wait_recv()
        for i in (DOWN, UP, OUT):
            first_copy(i).wait_send()
            second_copy(i).wait_send()
        for j in range(3):
            direct_copy(j).wait_send()
            vec_copy(j).wait_send()
            bias_copy(j).wait_send()
        for j in range(7):
            column_out(j, vec_col, vc_s, vc_r).wait_send()
            column_out(j, bias_col, bc_s, bc_r).wait_send()

        @pl.when(home)
        def _():
            for i in range(4):
                mate_sum(i).wait_send()

        @pl.when(away)
        def _():
            for i in range(4):
                for copy in away_sums(i):
                    copy.wait_send()
            for item in weight_items:
                for j in range(3):
                    spread(item, j).wait_send()
            for item in range(12):
                swap(item).wait_send()
            for i, dst in enumerate((result_o, grad_o)):
                for c in range(2):
                    hand_out(i, out_rows.at[i], dst, c)[1].wait_send()


def layer_call(tight, shapes, *args):
    rows, width = shapes
    hidden = width
    length = 4 * rows
    chunk = rows // 2
    heads_wide, qkv_wide = 256, 640
    widths = (hidden, hidden, heads_wide, qkv_wide)
    any_space = pl.BlockSpec(memory_space=pl.ANY)
    vmem = pl.BlockSpec(memory_space=pltpu.VMEM)
    quarter = width // 4
    vec_rows = (8, 8) if tight else (8,)
    if tight:
        sums = [jax.ShapeDtypeStruct((quarter // 2, w), BF16) for w in widths]
    else:
        sums = [jax.ShapeDtypeStruct((2, 2, quarter, w), BF16) for w in widths]
    out_shape = (
        jax.ShapeDtypeStruct((rows, width), BF16),
        jax.ShapeDtypeStruct((rows, width), BF16),
        sums,
        [jax.ShapeDtypeStruct((quarter // 2, w), BF16) for w in widths],
        jax.ShapeDtypeStruct((*vec_rows, width), F32),
        jax.ShapeDtypeStruct((*vec_rows, 128), F32),
    )
    V = pltpu.VMEM
    D = pltpu.SemaphoreType.DMA
    pieces = V((4, 2, chunk, width), BF16)
    scratch = [
        *[V((length, width), BF16)] * 4,
        *[V((width, length), BF16)] * 4,
        *[pieces] * 6, V((2, rows, width), BF16),
        V((16, width), F32), V((16, width), F32), V((rows, width), BF16),
        V((576, width), BF16), V((qkv_wide, width), BF16), V((heads_wide, width), BF16),
        V((width, hidden), BF16), V((hidden, width), BF16),
        *[V((length, 128), F32)] * 4,
        V((length, qkv_wide), BF16), V((length, 128), BF16), V((3, length, length), F32),
        V((3, length, length), BF16), V((3, length, length), BF16), V((length, heads_wide), BF16),
        V((length, hidden), BF16), V((length, hidden), F32), V((length, hidden), BF16),
        V((length, heads_wide), BF16), V((length, qkv_wide), BF16),
        V((heads_wide, length), BF16), V((heads_wide, length), BF16),
        V((heads_wide, length), F32), V((heads_wide, length), F32),
        V((2, rows, width), F32), V((2, rows, width), F32), V((2 * rows, width), F32),
        [V((2, 2, quarter, w), BF16) for w in widths],
        [V((2, quarter, w), BF16) for w in widths[:3]],
        [V((quarter, w), BF16) for w in widths[:3]],
        [V((2, quarter, w), BF16) for w in widths[:3]],
        V((3, quarter, qkv_wide), BF16),
        [V((2, quarter // 2, w), BF16) for w in widths],
        V((8, width), F32), V((3, 8, width), F32), V((8, 8, width), F32),
        V((8, 128), F32), V((3, 8, 128), F32), V((8, 8, 128), F32),
        *[D((4, 2, 3))] * 4, D((12,)), D((12,)), D((8, 3)), D((8, 3)),
        D((3, 2)), D((3, 2)), D((3,)), D((3,)), D((4, 2)), D((4, 2)),
        D((3,)), D((3,)), D((7,)), D((7,)), D((3,)), D((3,)), D((7,)), D((7,)),
        D((2, 2)), D((2, 2)), D((9,)),
    ]
    return pl.pallas_call(
        partial(layer_kernel, tight),
        out_shape=out_shape,
        in_specs=[any_space] * 8 + [vmem] * 11,
        out_specs=jax.tree.map(lambda _: any_space, out_shape),
        scratch_shapes=scratch,
        compiler_params=pltpu.CompilerParams(
            collective_id=0, has_side_effects=True, vmem_limit_bytes=61 << 20
        ),
    )(*args)


def finish_kernel(*refs):
    sources, refs = refs[:12], refs[12:]
    outs, refs = refs[:18], refs[18:]
    held, sem = refs[:12], refs[12]
    (
        o_result, o_tokens, o_query, o_b_query, o_key, o_b_key, o_value, o_b_value, o_out, o_b_out,
        o_gain_mixer, o_shift_mixer, o_up, o_b_up, o_down, o_b_down, o_gain_feed, o_shift_feed,
    ) = outs
    copies = [
        pltpu.make_async_copy(src, dst, sem.at[i]) for i, (src, dst) in enumerate(zip(sources, held))
    ]
    for copy in copies:
        copy.start()

    def take(i):
        copies[i].wait()
        return held[i][...]

    def total(i):
        return take(2 + i).astype(F32) + take(6 + i).astype(F32)

    o_result[...] = take(0)
    o_tokens[...] = take(1).astype(F32)
    o_down[...] = total(DOWN)
    o_up[...] = total(UP)
    o_out[...] = jnp.transpose(total(OUT))[:192, :]
    for ref, part in zip((o_query, o_key, o_value), split_qkv(total(QKV))):
        ref[...] = part
    vec, bias = take(10), take(11)
    everywhere = jnp.sum(vec, axis=0)
    rows = (o_b_out, o_gain_mixer, o_shift_mixer, o_b_down, o_gain_feed, o_shift_feed)
    for i, ref in enumerate(rows):
        ref[...] = everywhere[i]
    by_slot = [vec[k, 6:7, :] + vec[4 + k, 6:7, :] for k in range(4)]
    o_b_up[...] = jnp.concatenate(by_slot, axis=1).reshape(o_b_up.shape)
    blocks = [bias[k] + bias[4 + k] for k in range(4)]
    for ref, (i, at) in zip((o_b_query, o_b_key, o_b_value), ((0, 0), (1, 64), (2, 0))):
        j = 4 if i == 2 else 3
        parts = []
        for b in blocks:
            parts += [b[i:i + 1, :], b[j:j + 1, at:at + 64]]
        ref[...] = jnp.concatenate(parts, axis=1).reshape(ref.shape)


def finish_call(shapes, *args):
    vmem = pl.BlockSpec(memory_space=pltpu.VMEM)
    return pl.pallas_call(
        finish_kernel,
        out_shape=shapes,
        in_specs=[pl.BlockSpec(memory_space=pl.ANY)] * len(args),
        out_specs=tuple(vmem for _ in shapes),
        scratch_shapes=[
            *[pltpu.VMEM(a.shape, a.dtype) for a in args], pltpu.SemaphoreType.DMA((len(args),))
        ],
        compiler_params=pltpu.CompilerParams(vmem_limit_bytes=61 << 20),
    )(*args)


def split_qkv(block):
    query = jnp.concatenate([block[..., :128], block[..., 384:448]], axis=-1)
    key = jnp.concatenate([block[..., 128:256], block[..., 448:512]], axis=-1)
    value = jnp.concatenate([block[..., 256:384], block[..., 512:576]], axis=-1)
    return query, key, value


def on_device(
    tight,
    tokens,
    segment_ids,
    w_query,
    b_query,
    w_key,
    b_key,
    w_value,
    b_value,
    w_out,
    b_out,
    gain_mixer,
    shift_mixer,
    w_up,
    b_up,
    w_down,
    b_down,
    gain_feed,
    shift_feed,
    cotangent,
):
    rows, width = tokens.shape
    result, grad_rows, sums_a, sums_b, vec, bias = layer_call(
        tight, (rows, width), tokens, cotangent, w_query.T, w_key.T, w_value.T, w_out, w_up, w_down,
        segment_ids, b_query, b_key, b_value, b_up, b_out, gain_mixer, shift_mixer, b_down,
        gain_feed, shift_feed,
    )
    if tight:
        ranks = lax.axis_size("tensor")
        share, here = width // lax.axis_size("dp"), w_query.shape[1]
        hidden = w_up.shape[1]

        def shape(*dims):
            return jax.ShapeDtypeStruct(dims, F32)

        head = (shape(share, here), shape(width)) * 3
        shapes = (
            jax.ShapeDtypeStruct((rows, width), BF16), shape(rows, width), *head,
            shape(here, share), shape(width), shape(width), shape(width),
            shape(share, hidden), shape(hidden * ranks), shape(share, hidden),
            shape(width), shape(width), shape(width),
        )
        outs = finish_call(shapes, result, grad_rows, *sums_a, *sums_b, vec, bias)
        return (*outs[:14], outs[14].T, *outs[15:])
    flat = [a.reshape(width, a.shape[-1]).astype(F32) for a in sums_a]
    scatter = partial(lax.psum_scatter, axis_name="dp", scatter_dimension=0, tiled=True)
    sum_query, sum_key, sum_value = (scatter(b) for b in split_qkv(flat[QKV]))
    sum_out, sum_down = scatter(flat[OUT][:, :192]).T, scatter(flat[DOWN]).T
    totals = lax.psum(vec, ("dp", "tensor"))
    bias_up = lax.all_gather(lax.psum(vec[6], "dp"), "tensor").reshape(-1)
    rows_qkv = lax.all_gather(lax.psum(bias[:5], "dp"), "tensor").reshape(-1, 640)
    biases = [b.reshape(-1) for b in split_qkv(rows_qkv)]
    return (
        result,
        grad_rows.astype(F32),
        sum_query,
        biases[0],
        sum_key,
        biases[1],
        sum_value,
        biases[2],
        sum_out,
        totals[0],
        totals[1],
        totals[2],
        scatter(flat[UP]),
        bias_up,
        sum_down,
        totals[3],
        totals[4],
        totals[5],
    )


def solution(mesh):
    in_specs = (
        P(("dp", "tensor"), None),
        P("dp", None),
        P(None, "tensor"),
        P("tensor"),
        P(None, "tensor"),
        P("tensor"),
        P(None, "tensor"),
        P("tensor"),
        P("tensor", None),
        P(),
        P(),
        P(),
        P(None, "tensor"),
        P("tensor"),
        P("tensor", None),
        P(),
        P(),
        P(),
        P(("dp", "tensor"), None),
    )
    out_specs = (
        P(("dp", "tensor"), None),
        P(("dp", "tensor"), None),
        P("dp", "tensor"),
        P(),
        P("dp", "tensor"),
        P(),
        P("dp", "tensor"),
        P(),
        P("tensor", "dp"),
        P(),
        P(),
        P(),
        P("dp", "tensor"),
        P(),
        P("tensor", "dp"),
        P(),
        P(),
        P(),
    )
    tight = mesh.shape["dp"] == 8
    return jax.shard_map(
        partial(on_device, tight), mesh=mesh, in_specs=in_specs, out_specs=out_specs,
        check_vma=False,
    )
```

```python
from functools import partial
import math

import jax
import jax.numpy as jnp
from jax import lax
from jax.experimental import pallas as pl
from jax.experimental.pallas import tpu as pltpu
from jax.sharding import PartitionSpec as P

HD = 64
MESH = pl.DeviceIdType.MESH
F32 = jnp.float32
BF16 = jnp.bfloat16
LN_EPS = 1e-12
B_QKV, B_UP, B_OUT, G_MIX, S_MIX, B_DOWN, G_FEED, S_FEED = range(8)
DOWN, UP, OV, QK = range(4)


def nn(left, right):
    return lax.dot_general(left, right, (((1,), (0,)), ((), ())), preferred_element_type=F32)


def nt(left, right):
    return lax.dot_general(left, right, (((1,), (1,)), ((), ())), preferred_element_type=F32)


def norm_stats(values):
    centered = values - jnp.mean(values, axis=-1, keepdims=True)
    factor = lax.rsqrt(jnp.mean(centered * centered, axis=-1, keepdims=True) + LN_EPS)
    return centered * factor, factor


def norm_back(grads, normalized, factor, gain):
    scaled = grads * gain
    first = jnp.mean(scaled, axis=-1, keepdims=True)
    second = jnp.mean(scaled * normalized, axis=-1, keepdims=True)
    return factor * (scaled - first - normalized * second)


def copy_to(src, dst, send, recv, device):
    return pltpu.make_async_remote_copy(
        src_ref=src, dst_ref=dst, send_sem=send, recv_sem=recv, device_id=device,
        device_id_type=MESH,
    )


def layer_kernel(
    tight,
    tokens, cotangent, wq_t, wk_t, wv_t, w_out, w_up, w_down,
    segment_ids, *rest,
):
    b_refs, rest = rest[:10], rest[10:]
    layer_body(tight, tokens, cotangent, wq_t, wk_t, wv_t, w_out, w_up, w_down, segment_ids,
               b_refs, *rest)


def layer_body(
    tight,
    tokens, cotangent, wq_t, wk_t, wv_t, w_out, w_up, w_down, segment_ids, b_refs,
    result_o, grad_o, sums_a, sums_b, vec_o, bias_o,
    x_all, h_all, g2_all, g1_all, x_t, h_t, g2_t, g1_t,
    part_last, part_mate, land_last, land_mate, land_far, passed, out_rows,
    small_own, small_v, cot_v, staged, wqkv, wo, wu, wd,
    seg_nat, seg_cols, cos_t, sin_t,
    qkv_s, k2_s, probs, probs_low, ds_s, o_s, act, dgelu, dz_s, do_s, dqk_s, dv_s,
    q_t, do_t, dk_t, dv_t, h_own, g_own, own_part,
    grads, first_in, second_in, grads_mid, grads_in, grads_sum,
    vec, vec_x, vec_in, bias, bias_x, bias_in, seg_v, b_v,
    ag_s, ag_r, rs_s, rs_r, sw_s, sw_r, wx_s, wx_r, dx_s, dx_r, dq_s, dq_r, dz_sem_s, dz_sem_r,
    vec_s, vec_r, bias_s, bias_r, out_s, out_r, loc, b_sem,
):
    dp, ten = lax.axis_index("dp"), lax.axis_index("tensor")
    low = lax.rem(ten, 2)
    if tight:
        col, core, half = dp // 2, lax.rem(dp, 2), ten // 2
        col_x, col_y = lax.rem(col, 2), col // 2
        slot = low + 2 * core
        mate_slot = low + 2 * (1 - core)
        far_slot = 1 - low + 2 * core
        last_slot = 1 - low + 2 * (1 - core)
        mate = {"dp": col * 2 + 1 - core, "tensor": ten}
        far = {"dp": dp, "tensor": ten + 1 - 2 * low}
        other = lax.rem(ten + 2, 4)
        partner = {"dp": col * 2 + 1 - core, "tensor": other}
        across = {"dp": dp, "tensor": other}
        cols = [{"dp": lax.rem(col + j, 4) * 2 + core, "tensor": ten} for j in (1, 2, 3)]
        next_x = {"dp": (col_y * 2 + 1 - col_x) * 2 + core, "tensor": ten}
        next_y = {"dp": ((1 - col_y) * 2 + col_x) * 2 + core, "tensor": ten}
        home = core == half
        away = core != half
        met = [mate, far, across, partner, *cols]
    else:
        slot = ten
        mate_slot = ten + 1 - 2 * low
        far_slot = lax.rem(ten + 2, 4)
        last_slot = 3 - ten
        mate = {"dp": dp, "tensor": mate_slot}
        far = {"dp": dp, "tensor": far_slot}
        met = [mate, far]

    rows, width = tokens.shape
    length = 4 * rows
    chunk = rows // 2
    units = ((0, 2 * rows), (2 * rows, rows), (3 * rows, rows))

    def local(src, dst, sem):
        return pltpu.make_async_copy(src, dst, sem)

    barrier = pltpu.get_barrier_semaphore()
    for device in met:
        pl.semaphore_signal(barrier, inc=1, device_id=device, device_id_type=MESH)

    b_copies = [local(src, dst, b_sem.at[i]) for i, (src, dst) in enumerate(zip(b_refs, b_v))]
    b_copies.append(local(segment_ids, seg_v, b_sem.at[10]))
    for copy in b_copies:
        copy.start()
    raw = []
    for i, w in enumerate((wq_t, wk_t, wv_t)):
        raw.append((w.at[pl.ds(0, 128)], (0, 128, 384)[i], 128))
        raw.append((w.at[pl.ds(128, 64)], (256, 320, 512)[i], 64))

    def raw_copy(i, ref):
        src, at, size = raw[i]
        return local(src, ref.at[pl.ds(at, size)], loc.at[i])

    to_tokens = [
        local(tokens.at[pl.ds(c * chunk, chunk)], x_all.at[pl.ds(c * chunk, chunk)], sw_r.at[4 + c])
        for c in range(2)
    ]
    to_small = local(small_own, small_v, sw_r.at[0])
    to_cot = local(cotangent, cot_v, sw_r.at[11])
    wo_rows = w_out.shape[0]
    to_out = local(w_out, wo.at[pl.ds(0, wo_rows)], loc.at[6])
    to_up = local(w_up, wu, loc.at[7])
    to_down = local(w_down, wd, loc.at[8])

    def load_own():
        for copy in to_tokens:
            copy.start()
        for i in range(6):
            raw_copy(i, wqkv).start()
        for copy in (to_out, to_up, to_down, to_cot):
            copy.start()

    def stage_own():
        for i in range(6):
            raw_copy(i, staged).start()

    if tight:
        pl.when(home)(load_own)
        pl.when(away)(stage_own)
    else:
        load_own()

    wo[wo_rows:, :] = jnp.zeros((wo.shape[0] - wo_rows, width), BF16)
    wqkv[576:, :] = jnp.zeros((wqkv.shape[0] - 576, width), BF16)

    def vector(ref):
        return ref[...].astype(F32).reshape(1, ref.shape[0])

    for copy in b_copies:
        copy.wait()
    bq, bk, bv = (vector(b_v[i]) for i in range(3))
    for at, b in ((0, bq), (128, bk), (384, bv)):
        small_own[0:1, at:at + 128] = b[:, :128]
    small_own[0:1, 256:384] = jnp.concatenate([bq[:, 128:], bk[:, 128:]], axis=1)
    small_own[0:1, 512:640] = jnp.concatenate([bv[:, 128:], jnp.zeros((1, 64), F32)], axis=1)
    small_own[0:1, 640:] = jnp.zeros((1, width - 640), F32)
    for i in range(7):
        small_own[B_UP + i:B_UP + i + 1, :] = vector(b_v[3 + i])
    small_own[8:16, :] = jnp.zeros((8, width), F32)
    small_own[8:9, :length] = seg_v[...].astype(F32)
    pl.semaphore_wait(barrier, len(met))

    weight_items = {
        1: (wqkv, staged, 576, 0, 3), 2: (wqkv, staged, 576, 1, 3), 3: (wqkv, staged, 576, 2, 3),
        6: (wo, w_out, wo_rows, 0, 1),
        7: (wu, w_up, width, 0, 2), 8: (wu, w_up, width, 1, 2),
        9: (wd, w_down, width, 0, 2), 10: (wd, w_down, width, 1, 2),
    }
    item_rank = {item: i for i, item in enumerate(weight_items)}

    def item_rows(item, q):
        _, _, total, part, count = weight_items[item]
        size = total // 4 // count
        return pl.ds(q * (total // 4) + part * size, size)

    def swap(item):
        if item in weight_items:
            dst, src = weight_items[item][:2]
            at = item_rows(item, col)
            src, dst = src.at[at], dst.at[at]
        elif item == 0:
            src, dst = small_own, small_v
        elif item == 11:
            src, dst = cotangent, cot_v
        else:
            at = pl.ds((item - 4) * chunk, chunk)
            src, dst = tokens.at[at], x_all.at[at]
        return copy_to(src, dst, sw_s.at[item], sw_r.at[item], partner)

    def spread(item, j):
        ref = weight_items[item][0].at[item_rows(item, col)]
        rank = item_rank[item]
        return copy_to(ref, ref, wx_s.at[rank, j], wx_r.at[rank, j], cols[j])

    def spread_in(item, j):
        ref = weight_items[item][0].at[item_rows(item, lax.rem(col + 3 - j, 4))]
        rank = item_rank[item]
        return copy_to(ref, ref, wx_s.at[rank, j], wx_r.at[rank, j], cols[j])

    def relay(item, follow=None):
        if tight:
            @pl.when(away)
            def _():
                swap(item).wait_recv()
                for j in range(3):
                    spread(item, j).start()
                if follow is not None:
                    swap(follow).start()

    def weights_ready(copies, *items):
        if not tight:
            for copy in copies:
                copy.wait()
            return

        @pl.when(home)
        def _():
            for copy in copies:
                copy.wait()

        @pl.when(away)
        def _():
            for item in items:
                for j in range(3):
                    spread_in(item, j).wait_recv()

    if tight:
        @pl.when(away)
        def _():
            swap(0).start()
            for i in range(6):
                raw_copy(i, staged).wait()
            for item in (1, 2, 3, 4, 5):
                swap(item).start()

        pl.when(home)(to_small.start)
    else:
        to_small.start()

    def at_own(c):
        return pl.ds(c * chunk, chunk)

    def at_mate(c):
        return pl.ds(rows + c * chunk, chunk)

    def at_far(c):
        return pl.ds(2 * rows + 2 * c * chunk, chunk)

    def at_last(c):
        return pl.ds(2 * rows + (2 * c + 1) * chunk, chunk)

    def gather_copy(i, buf, c, kind):
        src, dst, device = (
            (at_own(c), at_mate(c), mate), (at_own(c), at_far(c), far), (at_far(c), at_last(c), mate)
        )[kind]
        return copy_to(
            buf.at[src], buf.at[dst], ag_s.at[i, c, kind], ag_r.at[i, c, kind], device
        )

    def ag_own(i, buf, c):
        gather_copy(i, buf, c, 1).start()
        gather_copy(i, buf, c, 0).start()

    def ag_mate(i, buf):
        for c in range(2):
            gather_copy(i, buf, c, 0).wait_recv()

    def ag_unit(i, buf, c):
        gather_copy(i, buf, c, 1).wait_recv()
        gather_copy(i, buf, c, 2).start()
        gather_copy(i, buf, c, 2).wait_recv()

    def rs_copy(i, c, kind):
        src, dst, device = (
            (part_last.at[i, c], land_last.at[i, c], mate),
            (part_mate.at[i, c], land_mate.at[i, c], mate),
            (passed.at[i, c], land_far.at[i, c], far),
        )[kind]
        return copy_to(src, dst, rs_s.at[i, c, kind], rs_r.at[i, c, kind], device)

    def rs_unit(i, c, term):
        part_last[i, c] = term[chunk:].astype(BF16)
        rs_copy(i, c, 0).start()
        own_part[rows + c * chunk:rows + (c + 1) * chunk, :] = term[:chunk]

    def rs_pass(i, c):
        rs_copy(i, c, 0).wait_recv()
        term = own_part[rows + c * chunk:rows + (c + 1) * chunk, :]
        passed[i, c] = (term + land_last[i, c].astype(F32)).astype(BF16)
        rs_copy(i, c, 2).start()

    def rs_mate(i, term):
        for c in range(2):
            part_mate[i, c] = term[rows + c * chunk:rows + (c + 1) * chunk].astype(BF16)
            rs_copy(i, c, 1).start()
        own_part[0:rows, :] = term[:rows]

    def reduced(i, c):
        rs_copy(i, c, 1).wait_recv()
        rs_copy(i, c, 2).wait_recv()
        term = own_part[c * chunk:(c + 1) * chunk, :]
        return term + land_mate[i, c].astype(F32) + land_far[i, c].astype(F32)

    if not tight:
        for c in range(2):
            to_tokens[c].wait()
            ag_own(0, x_all, c)
    else:
        @pl.when(home)
        def _():
            for c in range(2):
                to_tokens[c].wait()
                ag_own(0, x_all, c)

    to_small.wait()
    seg_row = small_v[8:9, :length]
    seg_nat[...] = jnp.transpose(jnp.broadcast_to(seg_row, (128, length)))
    segs = seg_nat[...]
    place = lax.broadcasted_iota(jnp.int32, (length, 128), 0).astype(F32)
    start = jnp.zeros((length, 128), F32)
    for s in range(4):
        before = jnp.sum(jnp.where(seg_row < s, 1.0, 0.0), axis=1, keepdims=True)
        start = jnp.where(segs == s, before, start)
    cos_t[...] = place - start
    order = [(0, slot, 0), (1, slot, 1), (2, mate_slot, 0), (3, mate_slot, 1)]
    order += [(4, far_slot, 0), (5, last_slot, 0), (6, far_slot, 1), (7, last_slot, 1)]
    for to, from_slot, c in order:
        at = pl.ds(pl.multiple_of(from_slot * rows + c * chunk, chunk), chunk)
        seg_cols[to * chunk:(to + 1) * chunk, :] = seg_nat[at, :]
        sin_t[to * chunk:(to + 1) * chunk, :] = cos_t[at, :]
    lane = lax.broadcasted_iota(jnp.int32, (1, 128), 1)
    frequency = jnp.exp(lax.rem(lane, 32).astype(F32) * (-math.log(10000.0) / 32))
    sign = jnp.where(lax.rem(lane, 64) < 32, -1.0, 1.0)
    angle = sin_t[...] * frequency
    cos_t[...] = jnp.cos(angle)
    sin_t[...] = jnp.sin(angle) * sign
    seg_row = jnp.transpose(seg_cols[...])[0:1, :]

    if tight:
        @pl.when(away)
        def _():
            for item in (1, 2, 3):
                swap(item).wait_recv()
                for j in range(3):
                    spread(item, j).start()
            swap(6).start()
            swap(7).start()
            for c, follow in ((0, 8), (1, 9)):
                swap(4 + c).wait_recv()
                ag_own(0, x_all, c)
                swap(follow).start()
            swap(6).wait_recv()
            for j in range(3):
                spread(6, j).start()
            swap(10).start()

    low_lane = lane < 64

    def turn(values):
        return jnp.where(
            lax.rem(lane, 64) < 32, pltpu.roll(values, 96, 1), pltpu.roll(values, 32, 1)
        )

    scale = HD ** (-0.5)

    def project_rows(lo, n):
        here = slice(lo, lo + n)
        x = x_all[here, :]
        pre = nt(x, wqkv[...]) + small_v[B_QKV:B_QKV + 1, :640]
        cosine, sine = cos_t[here, :], sin_t[here, :]

        def rot(block):
            return block * cosine + turn(block) * sine

        query, key, mixed = rot(pre[:, :128]), rot(pre[:, 128:256]), rot(pre[:, 256:384])
        qkv_s[here, 0:128] = (query.astype(BF16) * scale).astype(BF16)
        qkv_s[here, 128:256] = key.astype(BF16)
        qkv_s[here, 256:384] = (jnp.where(low_lane, mixed, 0.0).astype(BF16) * scale).astype(BF16)
        qkv_s[here, 384:640] = pre[:, 384:640].astype(BF16)
        k2_s[here, :] = jnp.where(low_lane, pltpu.roll(mixed, 64, 1), 0.0).astype(BF16)
        x_t[:, here] = jnp.transpose(x)

    weights_ready([raw_copy(i, wqkv) for i in range(6)], 1, 2, 3)
    ag_mate(0, x_all)
    project_rows(*units[0])
    ag_unit(0, x_all, 0)
    project_rows(*units[1])
    ag_unit(0, x_all, 1)
    project_rows(*units[2])
    relay(7, 11)

    def masked(block, head):
        if head == 2:
            return block
        keep = low_lane if head == 0 else ~low_lane
        return jnp.where(keep, block, jnp.zeros_like(block))

    def attend(s, carry):
        here = pl.ds(pl.multiple_of(s * rows, rows), rows)
        same = seg_cols[here, 0:1] == seg_row
        outs = []
        for head in range(3):
            q_at, v_at = (0, 384) if head < 2 else (256, 512)
            query = masked(qkv_s[here, q_at:q_at + 128], head)
            keys = qkv_s[:, 128:256] if head < 2 else k2_s[...]
            scores = jnp.where(same, nt(query, keys), -1e30)
            scores = jnp.exp(scores - jnp.max(scores, axis=1, keepdims=True))
            weight = scores * (1.0 / jnp.sum(scores, axis=1, keepdims=True))
            probs[head, here, :] = weight
            weight_low = weight.astype(BF16)
            probs_low[head, here, :] = weight_low
            outs.append(nn(weight_low, qkv_s[:, v_at:v_at + 128]))
        o_s[here, 0:128] = jnp.where(low_lane, outs[0], outs[1]).astype(BF16)
        o_s[here, 128:256] = outs[2].astype(BF16)
        return carry

    def mix(lo, n):
        return nn(o_s[lo:lo + n, :], wo[...])

    attend(2, 0)
    relay(8)
    weights_ready([to_out], 6)
    rs_unit(0, 0, mix(*units[1]))
    attend(3, 0)
    rs_unit(0, 1, mix(*units[2]))
    rs_pass(0, 0)
    lax.fori_loop(0, 1, attend, 0)
    rs_pass(0, 1)
    relay(9)
    lax.fori_loop(1, 2, attend, 0)
    rs_mate(0, mix(*units[0]))
    relay(10)
    factors = []

    def spot(c):
        return slice(c * chunk, (c + 1) * chunk)

    def row_of(at):
        return small_v[at:at + 1, :]

    for c in range(2):
        here = spot(c)
        into = reduced(0, c) + x_all[here, :].astype(F32) + row_of(B_OUT)
        normal1, factor1 = norm_stats(into)
        factors.append(factor1)
        normed = normal1 * row_of(G_MIX) + row_of(S_MIX)
        h_own[0, here, :] = normed
        h_own[1, here, :] = normal1
        h_all[here, :] = normed.astype(BF16)
        ag_own(1, h_all, c)

    def feed(lo, n):
        here = slice(lo, lo + n)
        h = h_all[here, :]
        z = nn(h, wu[...]) + row_of(B_UP)
        phi = 0.5 * (1.0 + lax.erf(z * (2.0 ** -0.5)))
        act[here, :] = (z * phi).astype(BF16)
        dgelu[here, :] = phi + z * (jnp.exp(-0.5 * z * z) * (1.0 / math.sqrt(2.0 * math.pi)))

    def shrink(lo, n):
        return nn(act[lo:lo + n, :], wd[...])

    weights_ready([to_up], 7, 8)
    ag_mate(1, h_all)
    feed(*units[0])
    ag_unit(1, h_all, 0)
    feed(*units[1])
    weights_ready([to_down], 9, 10)
    rs_unit(1, 0, shrink(*units[1]))
    ag_unit(1, h_all, 1)
    rs_pass(1, 0)
    feed(*units[2])
    rs_unit(1, 1, shrink(*units[2]))
    rs_pass(1, 1)
    rs_mate(1, shrink(*units[0]))
    h_t[...] = jnp.transpose(h_all[...])

    def hand_out(i, src, dst, c):
        src, dst = src.at[pl.ds(c * chunk, chunk)], dst.at[pl.ds(c * chunk, chunk)]
        keep = local(src, dst, out_r.at[i, c])
        send = copy_to(src, dst, out_s.at[i, c], out_r.at[i, c], partner) if tight else None
        return keep, send

    def hand_start(*args):
        keep, send = hand_out(*args)
        if tight:
            pl.when(home)(keep.start)
            pl.when(away)(send.start)
        else:
            keep.start()

    to_cot.wait()
    sums = [0.0, 0.0, 0.0]
    for c in range(2):
        here = spot(c)
        into = reduced(1, c) + h_own[0, here, :] + row_of(B_DOWN)
        normal2, factor2 = norm_stats(into)
        dy = cot_v[here, :].astype(F32)
        grad2 = norm_back(dy, normal2, factor2, row_of(G_FEED))
        g_own[0, here, :] = grad2
        g2_all[here, :] = grad2.astype(BF16)
        ag_own(2, g2_all, c)
        out_rows[0, here, :] = (normal2 * row_of(G_FEED) + row_of(S_FEED)).astype(BF16)
        hand_start(0, out_rows.at[0], result_o, c)
        for i, term in enumerate((grad2, dy * normal2, dy)):
            sums[i] = sums[i] + jnp.sum(term, axis=0, keepdims=True)
    vec[...] = jnp.zeros(vec.shape, F32)
    for i in range(3):
        vec[0, 3 + i:4 + i, :] = sums[i]

    def feed_back(lo, n):
        here = slice(lo, lo + n)
        dz_s[here, :] = (nt(g2_all[here, :], wd[...]) * dgelu[here, :]).astype(BF16)

    def widen(lo, n):
        return nt(dz_s[lo:lo + n, :], wu[...])

    ag_mate(2, g2_all)
    feed_back(*units[0])
    g2_t[:, :2 * rows] = jnp.transpose(g2_all[:2 * rows, :])
    ag_unit(2, g2_all, 0)
    feed_back(*units[1])
    rs_unit(2, 0, widen(*units[1]))
    ag_unit(2, g2_all, 1)
    rs_pass(2, 0)
    feed_back(*units[2])
    rs_unit(2, 1, widen(*units[2]))
    rs_pass(2, 1)
    rs_mate(2, widen(*units[0]))

    def weight_grad(at_piece, value):
        quarter = width // 4

        def step(q, carry):
            at = pl.ds(pl.multiple_of(q * quarter, quarter), quarter)
            found = value(at).astype(BF16)
            for h in range(found.shape[1] // 384):
                part = found[:, h * 384:(h + 1) * 384]
                grads[at_piece + h][q // 2, lax.rem(q, 2)] = part
            return carry

        lax.fori_loop(0, 4, step, 0)

    def first_copy(i, h):
        if h == 0:
            src, device = grads[2 * i].at[:, 1 - col_x], next_x
        else:
            src, device = grads[2 * i + 1].at[1 - col_y], next_y
        return copy_to(
            src, first_in.at[2 * i + h], dx_s.at[i, h, 0], dx_r.at[i, h, 0], device
        )

    def second_copy(i, h):
        keep, device = (1 - col_y, next_y) if h == 0 else (1 - col_x, next_x)
        return copy_to(
            grads_mid.at[2 * i + h, keep], second_in.at[2 * i + h], dx_s.at[i, h, 1],
            dx_r.at[i, h, 1], device,
        )

    def first_send(i):
        if tight:
            for h in range(2):
                first_copy(i, h).start()

    def first_land(i):
        if not tight:
            return
        for h in range(2):
            first_copy(i, h).wait_recv()
            for j in range(2):
                own = grads[2 * i][j, col_x] if h == 0 else grads[2 * i + 1][col_y, j]
                came = first_in[2 * i + h, j].astype(F32)
                grads_mid[2 * i + h, j] = (own.astype(F32) + came).astype(BF16)
            second_copy(i, h).start()

    def second_land(i):
        if not tight:
            return
        totals = []
        for h in range(2):
            second_copy(i, h).wait_recv()
            own = grads_mid[2 * i + h, col_y if h == 0 else col_x]
            totals.append(own.astype(F32) + second_in[2 * i + h].astype(F32))
        finish_sum(i, jnp.concatenate(totals, axis=1))

    def finish_sum(i, total):
        grads_sum[i][...] = total.astype(BF16).reshape(grads_sum[i].shape)

        @pl.when(home)
        def _():
            keep_sum(i).start()
            mate_sum(i).start()

        @pl.when(away)
        def _():
            for copy in away_sums(i):
                copy.start()

    def direct_copy(i, j):
        to = lax.rem(col + 1 + j, 4)
        return copy_to(
            grads[i + 2].at[to // 2, lax.rem(to, 2)], grads_in.at[i - OV, j],
            dq_s.at[i - OV, j], dq_r.at[i - OV, j], cols[j],
        )

    def direct_send(i):
        if tight:
            for j in range(3):
                direct_copy(i, j).start()

    def direct_land(i):
        if not tight:
            return
        total = grads[i + 2][col_y, col_x].astype(F32)
        for j in range(3):
            direct_copy(i, j).wait_recv()
            total = total + grads_in[i - OV, j].astype(F32)
        finish_sum(i, total)

    def keep_sum(i):
        return local(grads_sum[i].at[core], sums_a[i], dz_sem_r.at[i, 0])

    def mate_sum(i):
        return copy_to(
            grads_sum[i].at[1 - core], sums_a[i], dz_sem_s.at[i, 0], dz_sem_r.at[i, 0], mate
        )

    def away_sums(i):
        return (
            copy_to(
                grads_sum[i].at[core], sums_b[i], dz_sem_s.at[i, 0], dz_sem_r.at[i, 1], across
            ),
            copy_to(
                grads_sum[i].at[1 - core], sums_b[i], dz_sem_s.at[i, 1], dz_sem_r.at[i, 1], partner
            ),
        )

    g2_t[:, 2 * rows:] = jnp.transpose(g2_all[2 * rows:, :])
    weight_grad(0, lambda at: nn(g2_t[at, :], act[...]))
    first_send(DOWN)
    weight_grad(2, lambda at: nn(h_t[at, :], dz_s[...]))
    vec[1, pl.ds(slot, 1), :] = jnp.sum(dz_s[...].astype(F32), axis=0, keepdims=True)

    sums = [0.0, 0.0, 0.0]
    for c in range(2):
        here = spot(c)
        dh = reduced(2, c) + g_own[0, here, :]
        normal1 = h_own[1, here, :]
        grad1 = norm_back(dh, normal1, factors[c], row_of(G_MIX))
        g_own[1, here, :] = grad1
        g1_all[here, :] = grad1.astype(BF16)
        ag_own(3, g1_all, c)
        for i, term in enumerate((grad1, dh * normal1, dh)):
            sums[i] = sums[i] + jnp.sum(term, axis=0, keepdims=True)
    for i in range(3):
        vec[0, i:i + 1, :] = sums[i]

    class Total:
        def __init__(self, own, sent, landing, send, recv):
            self.own, self.sent, self.landing, self.send, self.recv = own, sent, landing, send, recv

        def copy(self, j):
            src = self.own if j < 3 else self.sent.at[j - 3]
            device = (*cols, mate, far, across)[j]
            return copy_to(src, self.landing.at[j], self.send.at[j], self.recv.at[j], device)

        def begin(self):
            if tight:
                for j in range(3):
                    self.copy(j).start()

        def columns(self):
            if tight:
                for j in range(3):
                    self.copy(j).wait_recv()
                self.sent[0] = self.own[...] + self.landing[0] + self.landing[1] + self.landing[2]
                self.copy(3).start()

        def step(self, k):
            if tight:
                self.copy(2 + k).wait_recv()
                self.sent[k] = self.sent[k - 1] + self.landing[2 + k]
                if k < 3:
                    self.copy(3 + k).start()

        def sends_done(self):
            for j in range(6):
                self.copy(j).wait_send()

    vec_total = Total(vec, vec_x, vec_in, vec_s, vec_r)
    bias_total = Total(bias, bias_x, bias_in, bias_s, bias_r)
    vec_total.begin()
    first_send(UP)

    def heads_back(lo, n):
        here = slice(lo, lo + n)
        do_s[here, :] = nt(g1_all[here, :], wo[...]).astype(BF16)

    def back(values, here):
        return values * cos_t[here, :] - turn(values) * sin_t[here, :]

    def attend_back(s, carry):
        here = pl.ds(pl.multiple_of(s * rows, rows), rows)
        outs = []
        for head in range(3):
            v_at, o_at = (384, 0) if head < 2 else (512, 128)
            grad_o = masked(do_s[here, o_at:o_at + 128], head)
            grad_p = nt(grad_o, qkv_s[:, v_at:v_at + 128])
            weight = probs[head, here, :]
            dot = jnp.sum(grad_p * weight, axis=1, keepdims=True)
            ds = (weight * (grad_p - dot)).astype(BF16)
            ds_s[head, here, :] = ds
            keys = qkv_s[:, 128:256] if head < 2 else k2_s[...]
            outs.append(nn(ds, keys) * scale)
        dqk_s[here, 0:128] = back(jnp.where(low_lane, outs[0], outs[1]), here).astype(BF16)
        dqk_s[here, 256:384] = back(outs[2], here).astype(BF16)
        return carry

    q_t[0:128, :] = jnp.transpose(qkv_s[:, 0:128])
    q_t[128:256, :] = jnp.transpose(qkv_s[:, 256:384])
    ag_mate(3, g1_all)
    heads_back(*units[0])
    g1_t[:, :2 * rows] = jnp.transpose(g1_all[:2 * rows, :])
    lax.fori_loop(0, 2, attend_back, 0)
    first_land(DOWN)
    vec_total.columns()
    ag_unit(3, g1_all, 0)
    heads_back(*units[1])
    ag_unit(3, g1_all, 1)
    heads_back(*units[2])
    vec_total.step(1)
    g1_t[:, 2 * rows:] = jnp.transpose(g1_all[2 * rows:, :])
    do_t[0:128, :] = jnp.transpose(do_s[:, 0:128])
    do_t[128:256, :] = jnp.transpose(do_s[:, 128:256])
    for head in range(2):
        at = slice(head * 64, head * 64 + 64)
        dv_t[at, :] = nn(do_t[at, :], probs_low[head])
    dv_t[128:192, :] = jnp.zeros((64, length), F32)
    dv_t[192:256, :] = nn(do_t[128:192, :], probs_low[2])
    dv_s[:, 0:128] = jnp.transpose(dv_t[0:128, :]).astype(BF16)
    dv_s[:, 128:256] = jnp.transpose(dv_t[128:256, :]).astype(BF16)

    def out_value(at):
        out = nn(g1_t[at, :], o_s[...])
        value = nn(x_t[at, :], dv_s[...])
        return jnp.concatenate(
            [out[:, :128], value[:, :128], out[:, 128:] + value[:, 128:]], axis=1
        )

    weight_grad(4, out_value)
    lax.fori_loop(2, 4, attend_back, 0)
    first_land(UP)
    vec_total.step(2)
    for head in range(3):
        at = slice(head * 64, head * 64 + 64)
        dk_t[at, :] = nn(q_t[at, :], ds_s[head])
    dk_t[192:, :] = jnp.zeros((64, length), F32)
    everything = slice(None)
    dqk_s[:, 128:256] = back(jnp.transpose(dk_t[0:128, :]), everything).astype(BF16)
    key2 = back(jnp.transpose(dk_t[128:256, :]), everything)
    query2 = dqk_s[:, 256:384].astype(F32)
    dqk_s[:, 256:384] = jnp.where(low_lane, query2, pltpu.roll(key2, 64, 1)).astype(BF16)

    query_key = jnp.sum(dqk_s[...].astype(F32), axis=0, keepdims=True)
    values = jnp.sum(dv_s[...].astype(F32), axis=0, keepdims=True)
    bias[...] = jnp.zeros(bias.shape, F32)
    for i in range(3):
        bias[slot, i:i + 1, :] = query_key[:, i * 128:(i + 1) * 128]
    for i in range(2):
        bias[slot, 3 + i:4 + i, :] = values[:, i * 128:(i + 1) * 128]
    bias_total.begin()
    direct_send(OV)
    weight_grad(5, lambda at: nn(x_t[at, :], dqk_s[...]))
    direct_send(QK)
    second_land(DOWN)
    value_low = jnp.where(
        low_lane, pltpu.roll(dv_s[:, 128:256].astype(F32), 64, 1), 0.0
    ).astype(BF16)

    def to_input(lo, n):
        term = nn(dqk_s[lo:lo + n, :], wqkv[0:384, :])
        term = term + nn(dv_s[lo:lo + n, 0:128], wqkv[384:512, :])
        return term + nn(value_low[lo:lo + n, :], wqkv[512:640, :])

    rs_unit(3, 0, to_input(*units[1]))
    rs_unit(3, 1, to_input(*units[2]))
    rs_pass(3, 0)
    rs_pass(3, 1)
    rs_mate(3, to_input(*units[0]))
    bias_total.columns()
    second_land(UP)
    bias_total.step(1)
    for c in range(2):
        here = spot(c)
        out_rows[1, here, :] = (reduced(3, c) + g_own[1, here, :]).astype(BF16)
        hand_start(1, out_rows.at[1], grad_o, c)
    bias_total.step(2)
    direct_land(OV)
    direct_land(QK)
    vec_total.step(3)
    bias_total.step(3)
    if tight:
        keep = [local(vec_x.at[3], vec_o, loc.at[0]), local(bias_x.at[3], bias_o, loc.at[1])]
    else:
        keep = [local(vec, vec_o, loc.at[0]), local(bias, bias_o, loc.at[1])]
        keep += [local(grads[i], sums_a[i], loc.at[2 + i]) for i in range(6)]
    for copy in keep:
        copy.start()

    for i, dst in enumerate((result_o, grad_o)):
        for c in range(2):
            hand_out(i, out_rows.at[i], dst, c)[0].wait()
    for i, buf in enumerate((x_all, h_all, g2_all, g1_all)):
        for c in range(2):
            for kind in range(3):
                gather_copy(i, buf, c, kind).wait_send()
                rs_copy(i, c, kind).wait_send()
    for copy in keep:
        copy.wait()
    if tight:
        for i in range(4):
            keep_sum(i).wait()
            away_sums(i)[0].wait_recv()
        for i in (DOWN, UP):
            for h in range(2):
                first_copy(i, h).wait_send()
                second_copy(i, h).wait_send()
        for i in (OV, QK):
            for j in range(3):
                direct_copy(i, j).wait_send()
        vec_total.sends_done()
        bias_total.sends_done()

        @pl.when(home)
        def _():
            for i in range(4):
                mate_sum(i).wait_send()

        @pl.when(away)
        def _():
            for i in range(4):
                for copy in away_sums(i):
                    copy.wait_send()
            for item in weight_items:
                for j in range(3):
                    spread(item, j).wait_send()
            for item in range(12):
                swap(item).wait_send()
            for i, dst in enumerate((result_o, grad_o)):
                for c in range(2):
                    hand_out(i, out_rows.at[i], dst, c)[1].wait_send()


def layer_call(tight, shapes, *args):
    rows, width = shapes
    hidden = width
    length = 4 * rows
    chunk = rows // 2
    heads_wide, qkv_wide = 256, 640
    widths = (hidden, hidden, 384, 384)
    any_space = pl.BlockSpec(memory_space=pl.ANY)
    quarter = width // 4
    if tight:
        sums = [jax.ShapeDtypeStruct((quarter // 2, w), BF16) for w in widths]
    else:
        sums = [jax.ShapeDtypeStruct((2, 2, quarter, 384), BF16)] * 6
    out_shape = (
        jax.ShapeDtypeStruct((rows, width), BF16),
        jax.ShapeDtypeStruct((rows, width), BF16),
        sums,
        [jax.ShapeDtypeStruct((quarter // 2, w), BF16) for w in widths],
        jax.ShapeDtypeStruct((2, 8, width), F32),
        jax.ShapeDtypeStruct((4, 8, 128), F32),
    )
    V = pltpu.VMEM
    D = pltpu.SemaphoreType.DMA
    pieces = V((4, 2, chunk, width), BF16)
    scratch = [
        *[V((length, width), BF16)] * 4,
        *[V((width, length), BF16)] * 4,
        *[pieces] * 6, V((2, rows, width), BF16),
        V((16, width), F32), V((16, width), F32), V((rows, width), BF16),
        V((576, width), BF16), V((qkv_wide, width), BF16), V((heads_wide, width), BF16),
        V((width, hidden), BF16), V((hidden, width), BF16),
        *[V((length, 128), F32)] * 4,
        V((length, qkv_wide), BF16), V((length, 128), BF16), V((3, length, length), F32),
        V((3, length, length), BF16), V((3, length, length), BF16), V((length, heads_wide), BF16),
        V((length, hidden), BF16), V((length, hidden), F32), V((length, hidden), BF16),
        V((length, heads_wide), BF16), V((length, 384), BF16), V((length, heads_wide), BF16),
        V((heads_wide, length), BF16), V((heads_wide, length), BF16),
        V((heads_wide, length), F32), V((heads_wide, length), F32),
        V((2, rows, width), F32), V((2, rows, width), F32), V((2 * rows, width), F32),
        [V((2, 2, quarter, 384), BF16)] * 6,
        V((4, 2, quarter, 384), BF16), V((4, quarter, 384), BF16), V((4, 2, quarter, 384), BF16),
        V((2, 3, quarter, 384), BF16),
        [V((2, quarter // 2, w), BF16) for w in widths],
        V((2, 8, width), F32), V((4, 2, 8, width), F32), V((6, 2, 8, width), F32),
        V((4, 8, 128), F32), V((4, 4, 8, 128), F32), V((6, 4, 8, 128), F32),
        V((1, length), jnp.int32), [V(b.shape, BF16) for b in args[9:]],
        *[D((4, 2, 3))] * 4, D((12,)), D((12,)), D((8, 3)), D((8, 3)),
        D((2, 2, 2)), D((2, 2, 2)), D((2, 3)), D((2, 3)), D((4, 2)), D((4, 2)),
        D((6,)), D((6,)), D((6,)), D((6,)), D((2, 2)), D((2, 2)), D((9,)), D((11,)),
    ]
    return pl.pallas_call(
        partial(layer_kernel, tight),
        out_shape=out_shape,
        in_specs=[any_space] * 19,
        out_specs=jax.tree.map(lambda _: any_space, out_shape),
        scratch_shapes=scratch,
        compiler_params=pltpu.CompilerParams(
            collective_id=0, has_side_effects=True, vmem_limit_bytes=61 << 20
        ),
    )(*args)


def finish_kernel(*refs):
    sources, refs = refs[:12], refs[12:]
    outs, refs = refs[:18], refs[18:]
    held, sem = refs[:12], refs[12]
    (
        o_result, o_tokens, o_query, o_b_query, o_key, o_b_key, o_value, o_b_value, o_out, o_b_out,
        o_gain_mixer, o_shift_mixer, o_up, o_b_up, o_down, o_b_down, o_gain_feed, o_shift_feed,
    ) = outs
    copies = [
        pltpu.make_async_copy(src, dst, sem.at[i]) for i, (src, dst) in enumerate(zip(sources, held))
    ]
    for copy in copies:
        copy.start()

    def take(i):
        copies[i].wait()
        return held[i][...]

    def total(i):
        return take(2 + i).astype(F32) + take(6 + i).astype(F32)

    o_result[...] = take(0)
    o_tokens[...] = take(1).astype(F32)
    o_down[...] = total(DOWN)
    o_up[...] = total(UP)
    out, query, key, value = split_pieces(total(OV), total(QK))
    o_out[...] = jnp.transpose(out)
    for ref, part in zip((o_query, o_key, o_value), (query, key, value)):
        ref[...] = part
    vec, bias = take(10), take(11)
    rows = (o_b_out, o_gain_mixer, o_shift_mixer, o_b_down, o_gain_feed, o_shift_feed)
    for i, ref in enumerate(rows):
        ref[...] = vec[0, i]
    o_b_up[...] = jnp.concatenate([vec[1, k:k + 1, :] for k in range(4)], axis=1).reshape(
        o_b_up.shape
    )
    for ref, (i, j, at) in zip(
        (o_b_query, o_b_key, o_b_value), ((0, 2, 0), (1, 2, 64), (3, 4, 64))
    ):
        parts = []
        for k in range(4):
            parts += [bias[k, i:i + 1, :], bias[k, j:j + 1, at:at + 64]]
        ref[...] = jnp.concatenate(parts, axis=1).reshape(ref.shape)


def finish_call(shapes, *args):
    vmem = pl.BlockSpec(memory_space=pltpu.VMEM)
    return pl.pallas_call(
        finish_kernel,
        out_shape=shapes,
        in_specs=[pl.BlockSpec(memory_space=pl.ANY)] * len(args),
        out_specs=tuple(vmem for _ in shapes),
        scratch_shapes=[
            *[pltpu.VMEM(a.shape, a.dtype) for a in args], pltpu.SemaphoreType.DMA((len(args),))
        ],
        compiler_params=pltpu.CompilerParams(vmem_limit_bytes=61 << 20),
    )(*args)


def split_pieces(out_value, query_key):
    def pick(block, at, tail):
        return jnp.concatenate([block[..., at:at + 128], block[..., tail:tail + 64]], axis=-1)

    return (
        pick(out_value, 0, 256), pick(query_key, 0, 256), pick(query_key, 128, 320),
        pick(out_value, 128, 320),
    )


def on_device(
    tight,
    tokens,
    segment_ids,
    w_query,
    b_query,
    w_key,
    b_key,
    w_value,
    b_value,
    w_out,
    b_out,
    gain_mixer,
    shift_mixer,
    w_up,
    b_up,
    w_down,
    b_down,
    gain_feed,
    shift_feed,
    cotangent,
):
    rows, width = tokens.shape
    result, grad_rows, sums_a, sums_b, vec, bias = layer_call(
        tight, (rows, width), tokens, cotangent, w_query.T, w_key.T, w_value.T, w_out, w_up, w_down,
        segment_ids, b_query, b_key, b_value, b_up, b_out, gain_mixer, shift_mixer, b_down,
        gain_feed, shift_feed,
    )
    if tight:
        ranks = lax.axis_size("tensor")
        share, here = width // lax.axis_size("dp"), w_query.shape[1]
        hidden = w_up.shape[1]

        def shape(*dims):
            return jax.ShapeDtypeStruct(dims, F32)

        head = (shape(share, here), shape(width)) * 3
        shapes = (
            jax.ShapeDtypeStruct((rows, width), BF16), shape(rows, width), *head,
            shape(here, share), shape(width), shape(width), shape(width),
            shape(share, hidden), shape(hidden * ranks), shape(share, hidden),
            shape(width), shape(width), shape(width),
        )
        outs = finish_call(shapes, result, grad_rows, *sums_a, *sums_b, vec, bias)
        return (*outs[:14], outs[14].T, *outs[15:])
    flat = [a.reshape(width, a.shape[-1]).astype(F32) for a in sums_a]
    flat = [jnp.concatenate(flat[:2], axis=1), jnp.concatenate(flat[2:4], axis=1), *flat[4:]]
    scatter = partial(lax.psum_scatter, axis_name="dp", scatter_dimension=0, tiled=True)
    sum_out, sum_query, sum_key, sum_value = (
        scatter(b) for b in split_pieces(flat[OV], flat[QK])
    )
    sum_out, sum_down = sum_out.T, scatter(flat[DOWN]).T
    vec = lax.psum(vec, ("dp", "tensor"))
    bias = lax.psum(bias, ("dp", "tensor"))
    totals, bias_up = vec[0], vec[1, :4].reshape(-1)
    biases = [
        jnp.concatenate([bias[:, i], bias[:, j, at:at + 64]], axis=1).reshape(-1)
        for i, j, at in ((0, 2, 0), (1, 2, 64), (3, 4, 64))
    ]
    return (
        result,
        grad_rows.astype(F32),
        sum_query,
        biases[0],
        sum_key,
        biases[1],
        sum_value,
        biases[2],
        sum_out,
        totals[0],
        totals[1],
        totals[2],
        scatter(flat[UP]),
        bias_up,
        sum_down,
        totals[3],
        totals[4],
        totals[5],
    )


def solution(mesh):
    in_specs = (
        P(("dp", "tensor"), None),
        P("dp", None),
        P(None, "tensor"),
        P("tensor"),
        P(None, "tensor"),
        P("tensor"),
        P(None, "tensor"),
        P("tensor"),
        P("tensor", None),
        P(),
        P(),
        P(),
        P(None, "tensor"),
        P("tensor"),
        P("tensor", None),
        P(),
        P(),
        P(),
        P(("dp", "tensor"), None),
    )
    out_specs = (
        P(("dp", "tensor"), None),
        P(("dp", "tensor"), None),
        P("dp", "tensor"),
        P(),
        P("dp", "tensor"),
        P(),
        P("dp", "tensor"),
        P(),
        P("tensor", "dp"),
        P(),
        P(),
        P(),
        P("dp", "tensor"),
        P(),
        P("tensor", "dp"),
        P(),
        P(),
        P(),
    )
    tight = mesh.shape["dp"] == 8
    return jax.shard_map(
        partial(on_device, tight), mesh=mesh, in_specs=in_specs, out_specs=out_specs,
        check_vma=False,
    )
```

```python
from functools import partial
import math

import jax
import jax.numpy as jnp
from jax import lax
from jax.experimental import pallas as pl
from jax.experimental.pallas import tpu as pltpu
from jax.sharding import PartitionSpec as P

HD = 64
MESH = pl.DeviceIdType.MESH
F32 = jnp.float32
BF16 = jnp.bfloat16
LN_EPS = 1e-12
B_QKV, B_UP, B_OUT, G_MIX, S_MIX, B_DOWN, G_FEED, S_FEED = range(8)
DOWN, UP, OV, QK = range(4)


def nn(left, right):
    return lax.dot_general(left, right, (((1,), (0,)), ((), ())), preferred_element_type=F32)


def tn(left, right):
    return lax.dot_general(left, right, (((0,), (0,)), ((), ())), preferred_element_type=F32)


def nt(left, right):
    return lax.dot_general(left, right, (((1,), (1,)), ((), ())), preferred_element_type=F32)


def norm_stats(values):
    centered = values - jnp.mean(values, axis=-1, keepdims=True)
    factor = lax.rsqrt(jnp.mean(centered * centered, axis=-1, keepdims=True) + LN_EPS)
    return centered * factor, factor


def norm_back(grads, normalized, factor, gain):
    scaled = grads * gain
    first = jnp.mean(scaled, axis=-1, keepdims=True)
    second = jnp.mean(scaled * normalized, axis=-1, keepdims=True)
    return factor * (scaled - first - normalized * second)


def copy_to(src, dst, send, recv, device):
    return pltpu.make_async_remote_copy(
        src_ref=src, dst_ref=dst, send_sem=send, recv_sem=recv, device_id=device,
        device_id_type=MESH,
    )


def layer_kernel(
    tight,
    tokens, cotangent, wq_t, wk_t, wv_t, w_out, w_up, w_down,
    segment_ids, *rest,
):
    b_refs, rest = rest[:10], rest[10:]
    layer_body(tight, tokens, cotangent, wq_t, wk_t, wv_t, w_out, w_up, w_down, segment_ids,
               b_refs, *rest)


def layer_body(
    tight,
    tokens, cotangent, wq_t, wk_t, wv_t, w_out, w_up, w_down, segment_ids, b_refs,
    result_o, grad_o, sums_a, sums_b, vec_o, bias_o,
    x_all, h_all, g2_all, g1_all, wu_t, wd_t, wo_t,
    part_last, part_mate, land_last, land_mate, land_far, passed, out_rows,
    small_own, small_v, cot_v, staged, wqkv, wo, wu, wd,
    seg_nat, seg_cols, cos_t, sin_t,
    qkv_s, k2_s, probs, probs_low, ds_s, o_s, act, dgelu, dz_s, do_s, dqk_s, dv_s,
    q_t, do_t, dk_t, dv_t, h_own, g_own, own_part,
    grads, first_in, second_in, grads_mid, grads_in, grads_sum,
    vec, vec_x, vec_in, bias, bias_x, bias_in, seg_v, b_v,
    ag_s, ag_r, rs_s, rs_r, sw_s, sw_r, wx_s, wx_r, dx_s, dx_r, dq_s, dq_r, dz_sem_s, dz_sem_r,
    vec_s, vec_r, bias_s, bias_r, out_s, out_r, loc, b_sem,
):
    dp, ten = lax.axis_index("dp"), lax.axis_index("tensor")
    low = lax.rem(ten, 2)
    if tight:
        col, core, half = dp // 2, lax.rem(dp, 2), ten // 2
        col_x, col_y = lax.rem(col, 2), col // 2
        slot = low + 2 * core
        mate_slot = low + 2 * (1 - core)
        far_slot = 1 - low + 2 * core
        last_slot = 1 - low + 2 * (1 - core)
        mate = {"dp": col * 2 + 1 - core, "tensor": ten}
        far = {"dp": dp, "tensor": ten + 1 - 2 * low}
        other = lax.rem(ten + 2, 4)
        partner = {"dp": col * 2 + 1 - core, "tensor": other}
        across = {"dp": dp, "tensor": other}
        cols = [{"dp": lax.rem(col + j, 4) * 2 + core, "tensor": ten} for j in (1, 2, 3)]
        next_x = {"dp": (col_y * 2 + 1 - col_x) * 2 + core, "tensor": ten}
        next_y = {"dp": ((1 - col_y) * 2 + col_x) * 2 + core, "tensor": ten}
        home = core == half
        away = core != half
        met = [mate, far, across, partner, *cols]
    else:
        slot = ten
        mate_slot = ten + 1 - 2 * low
        far_slot = lax.rem(ten + 2, 4)
        last_slot = 3 - ten
        mate = {"dp": dp, "tensor": mate_slot}
        far = {"dp": dp, "tensor": far_slot}
        met = [mate, far]

    rows, width = tokens.shape
    length = 4 * rows
    chunk = rows // 2
    units = ((0, 2 * rows), (2 * rows, rows), (3 * rows, rows))

    def local(src, dst, sem):
        return pltpu.make_async_copy(src, dst, sem)

    barrier = pltpu.get_barrier_semaphore()
    for device in met:
        pl.semaphore_signal(barrier, inc=1, device_id=device, device_id_type=MESH)

    b_copies = [local(src, dst, b_sem.at[i]) for i, (src, dst) in enumerate(zip(b_refs, b_v))]
    b_copies.append(local(segment_ids, seg_v, b_sem.at[10]))
    for copy in b_copies:
        copy.start()
    raw = []
    for i, w in enumerate((wq_t, wk_t, wv_t)):
        raw.append((w.at[pl.ds(0, 128)], (0, 128, 384)[i], 128))
        raw.append((w.at[pl.ds(128, 64)], (256, 320, 512)[i], 64))

    def raw_copy(i, ref):
        src, at, size = raw[i]
        return local(src, ref.at[pl.ds(at, size)], loc.at[i])

    to_tokens = [
        local(tokens.at[pl.ds(c * chunk, chunk)], x_all.at[pl.ds(c * chunk, chunk)], sw_r.at[4 + c])
        for c in range(2)
    ]
    to_small = local(small_own, small_v, sw_r.at[0])
    to_cot = local(cotangent, cot_v, sw_r.at[11])
    wo_rows = w_out.shape[0]
    to_out = local(w_out, wo.at[pl.ds(0, wo_rows)], loc.at[6])
    to_up = local(w_up, wu, loc.at[7])
    to_down = local(w_down, wd, loc.at[8])

    def load_own():
        for copy in to_tokens:
            copy.start()
        for i in range(6):
            raw_copy(i, wqkv).start()
        for copy in (to_out, to_up, to_down, to_cot):
            copy.start()

    def stage_own():
        for i in range(6):
            raw_copy(i, staged).start()

    if tight:
        pl.when(home)(load_own)
        pl.when(away)(stage_own)
    else:
        load_own()

    wo[wo_rows:, :] = jnp.zeros((wo.shape[0] - wo_rows, width), BF16)
    wqkv[576:, :] = jnp.zeros((wqkv.shape[0] - 576, width), BF16)

    def vector(ref):
        return ref[...].astype(F32).reshape(1, ref.shape[0])

    for copy in b_copies:
        copy.wait()
    bq, bk, bv = (vector(b_v[i]) for i in range(3))
    for at, b in ((0, bq), (128, bk), (384, bv)):
        small_own[0:1, at:at + 128] = b[:, :128]
    small_own[0:1, 256:384] = jnp.concatenate([bq[:, 128:], bk[:, 128:]], axis=1)
    small_own[0:1, 512:640] = jnp.concatenate([bv[:, 128:], jnp.zeros((1, 64), F32)], axis=1)
    small_own[0:1, 640:] = jnp.zeros((1, width - 640), F32)
    for i in range(7):
        small_own[B_UP + i:B_UP + i + 1, :] = vector(b_v[3 + i])
    small_own[8:16, :] = jnp.zeros((8, width), F32)
    small_own[8:9, :length] = seg_v[...].astype(F32)
    pl.semaphore_wait(barrier, len(met))

    weight_items = {
        1: (wqkv, staged, 576, 0, 3), 2: (wqkv, staged, 576, 1, 3), 3: (wqkv, staged, 576, 2, 3),
        6: (wo, w_out, wo_rows, 0, 1),
        7: (wu, w_up, width, 0, 2), 8: (wu, w_up, width, 1, 2),
        9: (wd, w_down, width, 0, 2), 10: (wd, w_down, width, 1, 2),
    }
    item_rank = {item: i for i, item in enumerate(weight_items)}

    def item_rows(item, q):
        _, _, total, part, count = weight_items[item]
        size = total // 4 // count
        return pl.ds(q * (total // 4) + part * size, size)

    def swap(item):
        if item in weight_items:
            dst, src = weight_items[item][:2]
            at = item_rows(item, col)
            src, dst = src.at[at], dst.at[at]
        elif item == 0:
            src, dst = small_own, small_v
        elif item == 11:
            src, dst = cotangent, cot_v
        else:
            at = pl.ds((item - 4) * chunk, chunk)
            src, dst = tokens.at[at], x_all.at[at]
        return copy_to(src, dst, sw_s.at[item], sw_r.at[item], partner)

    def spread(item, j):
        ref = weight_items[item][0].at[item_rows(item, col)]
        rank = item_rank[item]
        return copy_to(ref, ref, wx_s.at[rank, j], wx_r.at[rank, j], cols[j])

    def spread_in(item, j):
        ref = weight_items[item][0].at[item_rows(item, lax.rem(col + 3 - j, 4))]
        rank = item_rank[item]
        return copy_to(ref, ref, wx_s.at[rank, j], wx_r.at[rank, j], cols[j])

    def relay(item, follow=None):
        if tight:
            @pl.when(away)
            def _():
                swap(item).wait_recv()
                for j in range(3):
                    spread(item, j).start()
                if follow is not None:
                    swap(follow).start()

    def weights_ready(copies, *items):
        if not tight:
            for copy in copies:
                copy.wait()
            return

        @pl.when(home)
        def _():
            for copy in copies:
                copy.wait()

        @pl.when(away)
        def _():
            for item in items:
                for j in range(3):
                    spread_in(item, j).wait_recv()

    if tight:
        @pl.when(away)
        def _():
            swap(0).start()
            for i in range(6):
                raw_copy(i, staged).wait()
            for item in (1, 2, 3, 4, 5):
                swap(item).start()

        pl.when(home)(to_small.start)
    else:
        to_small.start()

    def at_own(c):
        return pl.ds(c * chunk, chunk)

    def at_mate(c):
        return pl.ds(rows + c * chunk, chunk)

    def at_far(c):
        return pl.ds(2 * rows + 2 * c * chunk, chunk)

    def at_last(c):
        return pl.ds(2 * rows + (2 * c + 1) * chunk, chunk)

    def gather_copy(i, buf, c, kind):
        src, dst, device = (
            (at_own(c), at_mate(c), mate), (at_own(c), at_far(c), far), (at_far(c), at_last(c), mate)
        )[kind]
        return copy_to(
            buf.at[src], buf.at[dst], ag_s.at[i, c, kind], ag_r.at[i, c, kind], device
        )

    def ag_own(i, buf, c):
        gather_copy(i, buf, c, 1).start()
        gather_copy(i, buf, c, 0).start()

    def ag_mate(i, buf):
        for c in range(2):
            gather_copy(i, buf, c, 0).wait_recv()

    def ag_unit(i, buf, c):
        gather_copy(i, buf, c, 1).wait_recv()
        gather_copy(i, buf, c, 2).start()
        gather_copy(i, buf, c, 2).wait_recv()

    def rs_copy(i, c, kind):
        src, dst, device = (
            (part_last.at[i, c], land_last.at[i, c], mate),
            (part_mate.at[i, c], land_mate.at[i, c], mate),
            (passed.at[i, c], land_far.at[i, c], far),
        )[kind]
        return copy_to(src, dst, rs_s.at[i, c, kind], rs_r.at[i, c, kind], device)

    def rs_unit(i, c, term):
        part_last[i, c] = term[chunk:].astype(BF16)
        rs_copy(i, c, 0).start()
        own_part[rows + c * chunk:rows + (c + 1) * chunk, :] = term[:chunk]

    def rs_pass(i, c):
        rs_copy(i, c, 0).wait_recv()
        term = own_part[rows + c * chunk:rows + (c + 1) * chunk, :]
        passed[i, c] = (term + land_last[i, c].astype(F32)).astype(BF16)
        rs_copy(i, c, 2).start()

    def rs_mate(i, term):
        for c in range(2):
            part_mate[i, c] = term[rows + c * chunk:rows + (c + 1) * chunk].astype(BF16)
            rs_copy(i, c, 1).start()
        own_part[0:rows, :] = term[:rows]

    def reduced(i, c):
        rs_copy(i, c, 1).wait_recv()
        rs_copy(i, c, 2).wait_recv()
        term = own_part[c * chunk:(c + 1) * chunk, :]
        return term + land_mate[i, c].astype(F32) + land_far[i, c].astype(F32)

    if not tight:
        for c in range(2):
            to_tokens[c].wait()
            ag_own(0, x_all, c)
    else:
        @pl.when(home)
        def _():
            for c in range(2):
                to_tokens[c].wait()
                ag_own(0, x_all, c)

    to_small.wait()
    seg_row = small_v[8:9, :length]
    seg_nat[...] = jnp.transpose(jnp.broadcast_to(seg_row, (128, length)))
    segs = seg_nat[...]
    place = lax.broadcasted_iota(jnp.int32, (length, 128), 0).astype(F32)
    start = jnp.zeros((length, 128), F32)
    for s in range(4):
        before = jnp.sum(jnp.where(seg_row < s, 1.0, 0.0), axis=1, keepdims=True)
        start = jnp.where(segs == s, before, start)
    cos_t[...] = place - start
    order = [(0, slot, 0), (1, slot, 1), (2, mate_slot, 0), (3, mate_slot, 1)]
    order += [(4, far_slot, 0), (5, last_slot, 0), (6, far_slot, 1), (7, last_slot, 1)]
    for to, from_slot, c in order:
        at = pl.ds(pl.multiple_of(from_slot * rows + c * chunk, chunk), chunk)
        seg_cols[to * chunk:(to + 1) * chunk, :] = seg_nat[at, :]
        sin_t[to * chunk:(to + 1) * chunk, :] = cos_t[at, :]
    lane = lax.broadcasted_iota(jnp.int32, (1, 128), 1)
    frequency = jnp.exp(lax.rem(lane, 32).astype(F32) * (-math.log(10000.0) / 32))
    sign = jnp.where(lax.rem(lane, 64) < 32, -1.0, 1.0)
    angle = sin_t[...] * frequency
    cos_t[...] = jnp.cos(angle)
    sin_t[...] = jnp.sin(angle) * sign
    seg_row = jnp.transpose(seg_cols[...])[0:1, :]

    if tight:
        @pl.when(away)
        def _():
            for item in (1, 2, 3):
                swap(item).wait_recv()
                for j in range(3):
                    spread(item, j).start()
            swap(6).start()
            for c, follow in ((0, 7), (1, 8)):
                swap(4 + c).wait_recv()
                ag_own(0, x_all, c)
                swap(follow).start()
            swap(6).wait_recv()
            for j in range(3):
                spread(6, j).start()
            swap(9).start()
            swap(10).start()

    low_lane = lane < 64

    def turn(values):
        return jnp.where(
            lax.rem(lane, 64) < 32, pltpu.roll(values, 96, 1), pltpu.roll(values, 32, 1)
        )

    scale = HD ** (-0.5)

    def project_rows(lo, n):
        here = slice(lo, lo + n)
        x = x_all[here, :]
        pre = nt(x, wqkv[...]) + small_v[B_QKV:B_QKV + 1, :640]
        cosine, sine = cos_t[here, :], sin_t[here, :]

        def rot(block):
            return block * cosine + turn(block) * sine

        query, key, mixed = rot(pre[:, :128]), rot(pre[:, 128:256]), rot(pre[:, 256:384])
        qkv_s[here, 0:128] = (query.astype(BF16) * scale).astype(BF16)
        qkv_s[here, 128:256] = key.astype(BF16)
        qkv_s[here, 256:384] = (jnp.where(low_lane, mixed, 0.0).astype(BF16) * scale).astype(BF16)
        qkv_s[here, 384:640] = pre[:, 384:640].astype(BF16)
        k2_s[here, :] = jnp.where(low_lane, pltpu.roll(mixed, 64, 1), 0.0).astype(BF16)

    weights_ready([raw_copy(i, wqkv) for i in range(6)], 1, 2, 3)
    ag_mate(0, x_all)
    project_rows(*units[0])
    ag_unit(0, x_all, 0)
    project_rows(*units[1])
    ag_unit(0, x_all, 1)
    project_rows(*units[2])

    def masked(block, head):
        if head == 2:
            return block
        keep = low_lane if head == 0 else ~low_lane
        return jnp.where(keep, block, jnp.zeros_like(block))

    def attend(s, carry):
        here = pl.ds(pl.multiple_of(s * rows, rows), rows)
        same = seg_cols[here, 0:1] == seg_row
        outs = []
        for head in range(3):
            q_at, v_at = (0, 384) if head < 2 else (256, 512)
            query = masked(qkv_s[here, q_at:q_at + 128], head)
            keys = qkv_s[:, 128:256] if head < 2 else k2_s[...]
            scores = jnp.where(same, nt(query, keys), -1e30)
            scores = jnp.exp(scores - jnp.max(scores, axis=1, keepdims=True))
            weight = scores * (1.0 / jnp.sum(scores, axis=1, keepdims=True))
            probs[head, here, :] = weight
            weight_low = weight.astype(BF16)
            probs_low[head, here, :] = weight_low
            outs.append(nn(weight_low, qkv_s[:, v_at:v_at + 128]))
        o_s[here, 0:128] = jnp.where(low_lane, outs[0], outs[1]).astype(BF16)
        o_s[here, 128:256] = outs[2].astype(BF16)
        return carry

    def mix(lo, n):
        return nn(o_s[lo:lo + n, :], wo[...])

    attend(2, 0)
    relay(7)
    weights_ready([to_out], 6)
    rs_unit(0, 0, mix(*units[1]))
    attend(3, 0)
    relay(8)
    rs_unit(0, 1, mix(*units[2]))
    rs_pass(0, 0)
    lax.fori_loop(0, 1, attend, 0)
    rs_pass(0, 1)
    relay(9)
    lax.fori_loop(1, 2, attend, 0)
    rs_mate(0, mix(*units[0]))
    relay(10, 11)
    factors = []

    def spot(c):
        return slice(c * chunk, (c + 1) * chunk)

    def row_of(at):
        return small_v[at:at + 1, :]

    for c in range(2):
        here = spot(c)
        into = reduced(0, c) + x_all[here, :].astype(F32) + row_of(B_OUT)
        normal1, factor1 = norm_stats(into)
        factors.append(factor1)
        normed = normal1 * row_of(G_MIX) + row_of(S_MIX)
        h_own[0, here, :] = normed
        h_own[1, here, :] = normal1
        h_all[here, :] = normed.astype(BF16)
        ag_own(1, h_all, c)

    def feed(lo, n):
        here = slice(lo, lo + n)
        h = h_all[here, :]
        z = nn(h, wu[...]) + row_of(B_UP)
        phi = 0.5 * (1.0 + lax.erf(z * (2.0 ** -0.5)))
        act[here, :] = (z * phi).astype(BF16)
        dgelu[here, :] = phi + z * (jnp.exp(-0.5 * z * z) * (1.0 / math.sqrt(2.0 * math.pi)))

    def shrink(lo, n):
        return nn(act[lo:lo + n, :], wd[...])

    weights_ready([to_up], 7, 8)
    ag_mate(1, h_all)
    feed(*units[0])
    wu_t[...] = jnp.transpose(wu[...])
    wo_t[...] = jnp.transpose(wo[...])
    ag_unit(1, h_all, 0)
    feed(*units[1])
    weights_ready([to_down], 9, 10)
    rs_unit(1, 0, shrink(*units[1]))
    ag_unit(1, h_all, 1)
    rs_pass(1, 0)
    feed(*units[2])
    rs_unit(1, 1, shrink(*units[2]))
    rs_pass(1, 1)
    rs_mate(1, shrink(*units[0]))
    wd_t[...] = jnp.transpose(wd[...])

    def hand_out(i, src, dst, c):
        src, dst = src.at[pl.ds(c * chunk, chunk)], dst.at[pl.ds(c * chunk, chunk)]
        keep = local(src, dst, out_r.at[i, c])
        send = copy_to(src, dst, out_s.at[i, c], out_r.at[i, c], partner) if tight else None
        return keep, send

    def hand_start(*args):
        keep, send = hand_out(*args)
        if tight:
            pl.when(home)(keep.start)
            pl.when(away)(send.start)
        else:
            keep.start()

    to_cot.wait()
    sums = [0.0, 0.0, 0.0]
    for c in range(2):
        here = spot(c)
        into = reduced(1, c) + h_own[0, here, :] + row_of(B_DOWN)
        normal2, factor2 = norm_stats(into)
        dy = cot_v[here, :].astype(F32)
        grad2 = norm_back(dy, normal2, factor2, row_of(G_FEED))
        g_own[0, here, :] = grad2
        g2_all[here, :] = grad2.astype(BF16)
        ag_own(2, g2_all, c)
        out_rows[0, here, :] = (normal2 * row_of(G_FEED) + row_of(S_FEED)).astype(BF16)
        hand_start(0, out_rows.at[0], result_o, c)
        for i, term in enumerate((grad2, dy * normal2, dy)):
            sums[i] = sums[i] + jnp.sum(term, axis=0, keepdims=True)
    vec[...] = jnp.zeros(vec.shape, F32)
    for i in range(3):
        vec[0, 3 + i:4 + i, :] = sums[i]

    def weight_grad(at_piece, value):
        quarter = width // 4
        for y in range(2):
            found = value(slice(2 * y * quarter, 2 * (y + 1) * quarter)).astype(BF16)
            for x in range(2):
                for h in range(found.shape[1] // 384):
                    part = found[x * quarter:(x + 1) * quarter, h * 384:(h + 1) * 384]
                    grads[at_piece + h][y, x] = part

    def first_copy(i, h):
        if h == 0:
            src, device = grads[2 * i].at[:, 1 - col_x], next_x
        else:
            src, device = grads[2 * i + 1].at[1 - col_y], next_y
        return copy_to(
            src, first_in.at[2 * i + h], dx_s.at[i, h, 0], dx_r.at[i, h, 0], device
        )

    def second_copy(i, h):
        keep, device = (1 - col_y, next_y) if h == 0 else (1 - col_x, next_x)
        return copy_to(
            grads_mid.at[2 * i + h, keep], second_in.at[2 * i + h], dx_s.at[i, h, 1],
            dx_r.at[i, h, 1], device,
        )

    def first_send(i):
        if tight:
            for h in range(2):
                first_copy(i, h).start()

    def first_land(i):
        if not tight:
            return
        for h in range(2):
            first_copy(i, h).wait_recv()
            for j in range(2):
                own = grads[2 * i][j, col_x] if h == 0 else grads[2 * i + 1][col_y, j]
                came = first_in[2 * i + h, j].astype(F32)
                grads_mid[2 * i + h, j] = (own.astype(F32) + came).astype(BF16)
            second_copy(i, h).start()

    def second_land(i):
        if not tight:
            return
        totals = []
        for h in range(2):
            second_copy(i, h).wait_recv()
            own = grads_mid[2 * i + h, col_y if h == 0 else col_x]
            totals.append(own.astype(F32) + second_in[2 * i + h].astype(F32))
        finish_sum(i, jnp.concatenate(totals, axis=1))

    def finish_sum(i, total):
        grads_sum[i][...] = total.astype(BF16).reshape(grads_sum[i].shape)

        @pl.when(home)
        def _():
            keep_sum(i).start()
            mate_sum(i).start()

        @pl.when(away)
        def _():
            for copy in away_sums(i):
                copy.start()

    def direct_copy(i, j):
        to = lax.rem(col + 1 + j, 4)
        return copy_to(
            grads[i + 2].at[to // 2, lax.rem(to, 2)], grads_in.at[i - OV, j],
            dq_s.at[i - OV, j], dq_r.at[i - OV, j], cols[j],
        )

    def direct_send(i):
        if tight:
            for j in range(3):
                direct_copy(i, j).start()

    def direct_land(i):
        if not tight:
            return
        total = grads[i + 2][col_y, col_x].astype(F32)
        for j in range(3):
            direct_copy(i, j).wait_recv()
            total = total + grads_in[i - OV, j].astype(F32)
        finish_sum(i, total)

    def keep_sum(i):
        return local(grads_sum[i].at[core], sums_a[i], dz_sem_r.at[i, 0])

    def mate_sum(i):
        return copy_to(
            grads_sum[i].at[1 - core], sums_a[i], dz_sem_s.at[i, 0], dz_sem_r.at[i, 0], mate
        )

    def away_sums(i):
        return (
            copy_to(
                grads_sum[i].at[core], sums_b[i], dz_sem_s.at[i, 0], dz_sem_r.at[i, 1], across
            ),
            copy_to(
                grads_sum[i].at[1 - core], sums_b[i], dz_sem_s.at[i, 1], dz_sem_r.at[i, 1], partner
            ),
        )

    def feed_back(lo, n):
        here = slice(lo, lo + n)
        dz_s[here, :] = (nn(g2_all[here, :], wd_t[...]) * dgelu[here, :]).astype(BF16)

    def widen(lo, n):
        return nn(dz_s[lo:lo + n, :], wu_t[...])

    ag_mate(2, g2_all)
    feed_back(*units[0])
    ag_unit(2, g2_all, 0)
    feed_back(*units[1])
    rs_unit(2, 0, widen(*units[1]))
    ag_unit(2, g2_all, 1)
    rs_pass(2, 0)
    weight_grad(0, lambda at: tn(g2_all[:, at], act[...]))
    first_send(DOWN)
    feed_back(*units[2])
    rs_unit(2, 1, widen(*units[2]))
    rs_pass(2, 1)
    rs_mate(2, widen(*units[0]))

    weight_grad(2, lambda at: tn(h_all[:, at], dz_s[...]))
    vec[1, pl.ds(slot, 1), :] = jnp.sum(dz_s[...].astype(F32), axis=0, keepdims=True)

    sums = [0.0, 0.0, 0.0]
    for c in range(2):
        here = spot(c)
        dh = reduced(2, c) + g_own[0, here, :]
        normal1 = h_own[1, here, :]
        grad1 = norm_back(dh, normal1, factors[c], row_of(G_MIX))
        g_own[1, here, :] = grad1
        g1_all[here, :] = grad1.astype(BF16)
        ag_own(3, g1_all, c)
        for i, term in enumerate((grad1, dh * normal1, dh)):
            sums[i] = sums[i] + jnp.sum(term, axis=0, keepdims=True)
    for i in range(3):
        vec[0, i:i + 1, :] = sums[i]

    class Total:
        def __init__(self, own, sent, landing, send, recv):
            self.own, self.sent, self.landing, self.send, self.recv = own, sent, landing, send, recv

        def copy(self, j):
            src = self.own if j < 3 else self.sent.at[j - 3]
            device = (*cols, mate, far, across)[j]
            return copy_to(src, self.landing.at[j], self.send.at[j], self.recv.at[j], device)

        def begin(self):
            if tight:
                for j in range(3):
                    self.copy(j).start()

        def columns(self):
            if tight:
                for j in range(3):
                    self.copy(j).wait_recv()
                self.sent[0] = self.own[...] + self.landing[0] + self.landing[1] + self.landing[2]
                self.copy(3).start()

        def step(self, k):
            if tight:
                self.copy(2 + k).wait_recv()
                self.sent[k] = self.sent[k - 1] + self.landing[2 + k]
                if k < 3:
                    self.copy(3 + k).start()

        def sends_done(self):
            for j in range(6):
                self.copy(j).wait_send()

    vec_total = Total(vec, vec_x, vec_in, vec_s, vec_r)
    bias_total = Total(bias, bias_x, bias_in, bias_s, bias_r)
    vec_total.begin()

    def heads_back(lo, n):
        here = slice(lo, lo + n)
        do_s[here, :] = nn(g1_all[here, :], wo_t[...]).astype(BF16)

    def back(values, here):
        return values * cos_t[here, :] - turn(values) * sin_t[here, :]

    def attend_back(s, carry):
        here = pl.ds(pl.multiple_of(s * rows, rows), rows)
        outs = []
        for head in range(3):
            v_at, o_at = (384, 0) if head < 2 else (512, 128)
            grad_o = masked(do_s[here, o_at:o_at + 128], head)
            grad_p = nt(grad_o, qkv_s[:, v_at:v_at + 128])
            weight = probs[head, here, :]
            dot = jnp.sum(grad_p * weight, axis=1, keepdims=True)
            ds = (weight * (grad_p - dot)).astype(BF16)
            ds_s[head, here, :] = ds
            keys = qkv_s[:, 128:256] if head < 2 else k2_s[...]
            outs.append(nn(ds, keys) * scale)
        dqk_s[here, 0:128] = back(jnp.where(low_lane, outs[0], outs[1]), here).astype(BF16)
        dqk_s[here, 256:384] = back(outs[2], here).astype(BF16)
        return carry

    q_t[0:128, :] = jnp.transpose(qkv_s[:, 0:128])
    q_t[128:256, :] = jnp.transpose(qkv_s[:, 256:384])
    ag_mate(3, g1_all)
    heads_back(*units[0])
    first_land(DOWN)
    lax.fori_loop(0, 1, attend_back, 0)
    first_send(UP)
    lax.fori_loop(1, 2, attend_back, 0)
    vec_total.columns()
    ag_unit(3, g1_all, 0)
    heads_back(*units[1])
    ag_unit(3, g1_all, 1)
    heads_back(*units[2])
    vec_total.step(1)
    second_land(DOWN)
    do_t[0:128, :] = jnp.transpose(do_s[:, 0:128])
    do_t[128:256, :] = jnp.transpose(do_s[:, 128:256])
    for head in range(2):
        at = slice(head * 64, head * 64 + 64)
        dv_t[at, :] = nn(do_t[at, :], probs_low[head])
    dv_t[128:192, :] = jnp.zeros((64, length), F32)
    dv_t[192:256, :] = nn(do_t[128:192, :], probs_low[2])
    dv_s[:, 0:128] = jnp.transpose(dv_t[0:128, :]).astype(BF16)
    dv_s[:, 128:256] = jnp.transpose(dv_t[128:256, :]).astype(BF16)

    def out_value(at):
        out = tn(g1_all[:, at], o_s[...])
        value = tn(x_all[:, at], dv_s[...])
        return jnp.concatenate(
            [out[:, :128], value[:, :128], out[:, 128:] + value[:, 128:]], axis=1
        )

    weight_grad(4, out_value)
    lax.fori_loop(2, 4, attend_back, 0)
    first_land(UP)
    vec_total.step(2)
    for head in range(3):
        at = slice(head * 64, head * 64 + 64)
        dk_t[at, :] = nn(q_t[at, :], ds_s[head])
    dk_t[192:, :] = jnp.zeros((64, length), F32)
    everything = slice(None)
    dqk_s[:, 128:256] = back(jnp.transpose(dk_t[0:128, :]), everything).astype(BF16)
    key2 = back(jnp.transpose(dk_t[128:256, :]), everything)
    query2 = dqk_s[:, 256:384].astype(F32)
    dqk_s[:, 256:384] = jnp.where(low_lane, query2, pltpu.roll(key2, 64, 1)).astype(BF16)

    query_key = jnp.sum(dqk_s[...].astype(F32), axis=0, keepdims=True)
    values = jnp.sum(dv_s[...].astype(F32), axis=0, keepdims=True)
    bias[...] = jnp.zeros(bias.shape, F32)
    for i in range(3):
        bias[slot, i:i + 1, :] = query_key[:, i * 128:(i + 1) * 128]
    for i in range(2):
        bias[slot, 3 + i:4 + i, :] = values[:, i * 128:(i + 1) * 128]
    bias_total.begin()
    direct_send(OV)
    weight_grad(5, lambda at: tn(x_all[:, at], dqk_s[...]))
    direct_send(QK)
    value_low = jnp.where(
        low_lane, pltpu.roll(dv_s[:, 128:256].astype(F32), 64, 1), 0.0
    ).astype(BF16)

    def to_input(lo, n):
        term = nn(dqk_s[lo:lo + n, :], wqkv[0:384, :])
        term = term + nn(dv_s[lo:lo + n, 0:128], wqkv[384:512, :])
        return term + nn(value_low[lo:lo + n, :], wqkv[512:640, :])

    rs_unit(3, 0, to_input(*units[1]))
    rs_unit(3, 1, to_input(*units[2]))
    rs_pass(3, 0)
    rs_pass(3, 1)
    rs_mate(3, to_input(*units[0]))
    second_land(UP)
    bias_total.columns()
    for c in range(2):
        here = spot(c)
        out_rows[1, here, :] = (reduced(3, c) + g_own[1, here, :]).astype(BF16)
        hand_start(1, out_rows.at[1], grad_o, c)
    bias_total.step(1)
    vec_total.step(3)
    direct_land(OV)
    bias_total.step(2)
    direct_land(QK)
    bias_total.step(3)
    if tight:
        keep = [local(vec_x.at[3], vec_o, loc.at[0]), local(bias_x.at[3], bias_o, loc.at[1])]
    else:
        keep = [local(vec, vec_o, loc.at[0]), local(bias, bias_o, loc.at[1])]
        keep += [local(grads[i], sums_a[i], loc.at[2 + i]) for i in range(6)]
    for copy in keep:
        copy.start()

    for i, dst in enumerate((result_o, grad_o)):
        for c in range(2):
            hand_out(i, out_rows.at[i], dst, c)[0].wait()
    for i, buf in enumerate((x_all, h_all, g2_all, g1_all)):
        for c in range(2):
            for kind in range(3):
                gather_copy(i, buf, c, kind).wait_send()
                rs_copy(i, c, kind).wait_send()
    for copy in keep:
        copy.wait()
    if tight:
        for i in range(4):
            keep_sum(i).wait()
            away_sums(i)[0].wait_recv()
        for i in (DOWN, UP):
            for h in range(2):
                first_copy(i, h).wait_send()
                second_copy(i, h).wait_send()
        for i in (OV, QK):
            for j in range(3):
                direct_copy(i, j).wait_send()
        vec_total.sends_done()
        bias_total.sends_done()

        @pl.when(home)
        def _():
            for i in range(4):
                mate_sum(i).wait_send()

        @pl.when(away)
        def _():
            for i in range(4):
                for copy in away_sums(i):
                    copy.wait_send()
            for item in weight_items:
                for j in range(3):
                    spread(item, j).wait_send()
            for item in range(12):
                swap(item).wait_send()
            for i, dst in enumerate((result_o, grad_o)):
                for c in range(2):
                    hand_out(i, out_rows.at[i], dst, c)[1].wait_send()


def layer_call(tight, shapes, *args):
    rows, width = shapes
    hidden = width
    length = 4 * rows
    chunk = rows // 2
    heads_wide, qkv_wide = 256, 640
    widths = (hidden, hidden, 384, 384)
    any_space = pl.BlockSpec(memory_space=pl.ANY)
    quarter = width // 4
    if tight:
        sums = [jax.ShapeDtypeStruct((quarter // 2, w), BF16) for w in widths]
    else:
        sums = [jax.ShapeDtypeStruct((2, 2, quarter, 384), BF16)] * 6
    out_shape = (
        jax.ShapeDtypeStruct((rows, width), BF16),
        jax.ShapeDtypeStruct((rows, width), BF16),
        sums,
        [jax.ShapeDtypeStruct((quarter // 2, w), BF16) for w in widths],
        jax.ShapeDtypeStruct((2, 8, width), F32),
        jax.ShapeDtypeStruct((4, 8, 128), F32),
    )
    V = pltpu.VMEM
    D = pltpu.SemaphoreType.DMA
    pieces = V((4, 2, chunk, width), BF16)
    scratch = [
        *[V((length, width), BF16)] * 4,
        V((hidden, width), BF16), V((width, hidden), BF16), V((width, heads_wide), BF16),
        *[pieces] * 6, V((2, rows, width), BF16),
        V((16, width), F32), V((16, width), F32), V((rows, width), BF16),
        V((576, width), BF16), V((qkv_wide, width), BF16), V((heads_wide, width), BF16),
        V((width, hidden), BF16), V((hidden, width), BF16),
        *[V((length, 128), F32)] * 4,
        V((length, qkv_wide), BF16), V((length, 128), BF16), V((3, length, length), F32),
        V((3, length, length), BF16), V((3, length, length), BF16), V((length, heads_wide), BF16),
        V((length, hidden), BF16), V((length, hidden), F32), V((length, hidden), BF16),
        V((length, heads_wide), BF16), V((length, 384), BF16), V((length, heads_wide), BF16),
        V((heads_wide, length), BF16), V((heads_wide, length), BF16),
        V((heads_wide, length), F32), V((heads_wide, length), F32),
        V((2, rows, width), F32), V((2, rows, width), F32), V((2 * rows, width), F32),
        [V((2, 2, quarter, 384), BF16)] * 6,
        V((4, 2, quarter, 384), BF16), V((4, quarter, 384), BF16), V((4, 2, quarter, 384), BF16),
        V((2, 3, quarter, 384), BF16),
        [V((2, quarter // 2, w), BF16) for w in widths],
        V((2, 8, width), F32), V((4, 2, 8, width), F32), V((6, 2, 8, width), F32),
        V((4, 8, 128), F32), V((4, 4, 8, 128), F32), V((6, 4, 8, 128), F32),
        V((1, length), jnp.int32), [V(b.shape, BF16) for b in args[9:]],
        *[D((4, 2, 3))] * 4, D((12,)), D((12,)), D((8, 3)), D((8, 3)),
        D((2, 2, 2)), D((2, 2, 2)), D((2, 3)), D((2, 3)), D((4, 2)), D((4, 2)),
        D((6,)), D((6,)), D((6,)), D((6,)), D((2, 2)), D((2, 2)), D((9,)), D((11,)),
    ]
    return pl.pallas_call(
        partial(layer_kernel, tight),
        out_shape=out_shape,
        in_specs=[any_space] * 19,
        out_specs=jax.tree.map(lambda _: any_space, out_shape),
        scratch_shapes=scratch,
        compiler_params=pltpu.CompilerParams(
            collective_id=0, has_side_effects=True, vmem_limit_bytes=61 << 20
        ),
    )(*args)


def finish_kernel(*refs):
    sources, refs = refs[:12], refs[12:]
    outs, refs = refs[:18], refs[18:]
    held, sem = refs[:12], refs[12]
    (
        o_result, o_tokens, o_query, o_b_query, o_key, o_b_key, o_value, o_b_value, o_out, o_b_out,
        o_gain_mixer, o_shift_mixer, o_up, o_b_up, o_down, o_b_down, o_gain_feed, o_shift_feed,
    ) = outs
    copies = [
        pltpu.make_async_copy(src, dst, sem.at[i]) for i, (src, dst) in enumerate(zip(sources, held))
    ]
    for copy in copies:
        copy.start()

    def take(i):
        copies[i].wait()
        return held[i][...]

    def total(i):
        return take(2 + i).astype(F32) + take(6 + i).astype(F32)

    o_result[...] = take(0)
    o_tokens[...] = take(1).astype(F32)
    o_down[...] = total(DOWN)
    o_up[...] = total(UP)
    out, query, key, value = split_pieces(total(OV), total(QK))
    o_out[...] = jnp.transpose(out)
    for ref, part in zip((o_query, o_key, o_value), (query, key, value)):
        ref[...] = part
    vec, bias = take(10), take(11)
    rows = (o_b_out, o_gain_mixer, o_shift_mixer, o_b_down, o_gain_feed, o_shift_feed)
    for i, ref in enumerate(rows):
        ref[...] = vec[0, i]
    o_b_up[...] = jnp.concatenate([vec[1, k:k + 1, :] for k in range(4)], axis=1).reshape(
        o_b_up.shape
    )
    for ref, (i, j, at) in zip(
        (o_b_query, o_b_key, o_b_value), ((0, 2, 0), (1, 2, 64), (3, 4, 64))
    ):
        parts = []
        for k in range(4):
            parts += [bias[k, i:i + 1, :], bias[k, j:j + 1, at:at + 64]]
        ref[...] = jnp.concatenate(parts, axis=1).reshape(ref.shape)


def finish_call(shapes, *args):
    vmem = pl.BlockSpec(memory_space=pltpu.VMEM)
    return pl.pallas_call(
        finish_kernel,
        out_shape=shapes,
        in_specs=[pl.BlockSpec(memory_space=pl.ANY)] * len(args),
        out_specs=tuple(vmem for _ in shapes),
        scratch_shapes=[
            *[pltpu.VMEM(a.shape, a.dtype) for a in args], pltpu.SemaphoreType.DMA((len(args),))
        ],
        compiler_params=pltpu.CompilerParams(vmem_limit_bytes=61 << 20),
    )(*args)


def split_pieces(out_value, query_key):
    def pick(block, at, tail):
        return jnp.concatenate([block[..., at:at + 128], block[..., tail:tail + 64]], axis=-1)

    return (
        pick(out_value, 0, 256), pick(query_key, 0, 256), pick(query_key, 128, 320),
        pick(out_value, 128, 320),
    )


def on_device(
    tight,
    tokens,
    segment_ids,
    w_query,
    b_query,
    w_key,
    b_key,
    w_value,
    b_value,
    w_out,
    b_out,
    gain_mixer,
    shift_mixer,
    w_up,
    b_up,
    w_down,
    b_down,
    gain_feed,
    shift_feed,
    cotangent,
):
    rows, width = tokens.shape
    result, grad_rows, sums_a, sums_b, vec, bias = layer_call(
        tight, (rows, width), tokens, cotangent, w_query.T, w_key.T, w_value.T, w_out, w_up, w_down,
        segment_ids, b_query, b_key, b_value, b_up, b_out, gain_mixer, shift_mixer, b_down,
        gain_feed, shift_feed,
    )
    if tight:
        ranks = lax.axis_size("tensor")
        share, here = width // lax.axis_size("dp"), w_query.shape[1]
        hidden = w_up.shape[1]

        def shape(*dims):
            return jax.ShapeDtypeStruct(dims, F32)

        head = (shape(share, here), shape(width)) * 3
        shapes = (
            jax.ShapeDtypeStruct((rows, width), BF16), shape(rows, width), *head,
            shape(here, share), shape(width), shape(width), shape(width),
            shape(share, hidden), shape(hidden * ranks), shape(share, hidden),
            shape(width), shape(width), shape(width),
        )
        outs = finish_call(shapes, result, grad_rows, *sums_a, *sums_b, vec, bias)
        return (*outs[:14], outs[14].T, *outs[15:])
    flat = [a.reshape(width, a.shape[-1]).astype(F32) for a in sums_a]
    flat = [jnp.concatenate(flat[:2], axis=1), jnp.concatenate(flat[2:4], axis=1), *flat[4:]]
    scatter = partial(lax.psum_scatter, axis_name="dp", scatter_dimension=0, tiled=True)
    sum_out, sum_query, sum_key, sum_value = (
        scatter(b) for b in split_pieces(flat[OV], flat[QK])
    )
    sum_out, sum_down = sum_out.T, scatter(flat[DOWN]).T
    vec = lax.psum(vec, ("dp", "tensor"))
    bias = lax.psum(bias, ("dp", "tensor"))
    totals, bias_up = vec[0], vec[1, :4].reshape(-1)
    biases = [
        jnp.concatenate([bias[:, i], bias[:, j, at:at + 64]], axis=1).reshape(-1)
        for i, j, at in ((0, 2, 0), (1, 2, 64), (3, 4, 64))
    ]
    return (
        result,
        grad_rows.astype(F32),
        sum_query,
        biases[0],
        sum_key,
        biases[1],
        sum_value,
        biases[2],
        sum_out,
        totals[0],
        totals[1],
        totals[2],
        scatter(flat[UP]),
        bias_up,
        sum_down,
        totals[3],
        totals[4],
        totals[5],
    )


def solution(mesh):
    in_specs = (
        P(("dp", "tensor"), None),
        P("dp", None),
        P(None, "tensor"),
        P("tensor"),
        P(None, "tensor"),
        P("tensor"),
        P(None, "tensor"),
        P("tensor"),
        P("tensor", None),
        P(),
        P(),
        P(),
        P(None, "tensor"),
        P("tensor"),
        P("tensor", None),
        P(),
        P(),
        P(),
        P(("dp", "tensor"), None),
    )
    out_specs = (
        P(("dp", "tensor"), None),
        P(("dp", "tensor"), None),
        P("dp", "tensor"),
        P(),
        P("dp", "tensor"),
        P(),
        P("dp", "tensor"),
        P(),
        P("tensor", "dp"),
        P(),
        P(),
        P(),
        P("dp", "tensor"),
        P(),
        P("tensor", "dp"),
        P(),
        P(),
        P(),
    )
    tight = mesh.shape["dp"] == 8
    return jax.shard_map(
        partial(on_device, tight), mesh=mesh, in_specs=in_specs, out_specs=out_specs,
        check_vma=False,
    )
```

```python
from functools import partial
import math

import jax
import jax.numpy as jnp
from jax import lax
from jax.experimental import pallas as pl
from jax.experimental.pallas import tpu as pltpu
from jax.sharding import PartitionSpec as P

HD = 64
MESH = pl.DeviceIdType.MESH
F32 = jnp.float32
BF16 = jnp.bfloat16
LN_EPS = 1e-12
CHUNKS = 2
B_QKV, B_UP, SEGMENTS = range(3)
B_OUT, G_MIX, S_MIX, B_DOWN, G_FEED, S_FEED = range(8, 14)
DOWN, UP, OV, QK = range(4)


def nn(left, right):
    return lax.dot_general(left, right, (((1,), (0,)), ((), ())), preferred_element_type=F32)


def tn(left, right):
    return lax.dot_general(left, right, (((0,), (0,)), ((), ())), preferred_element_type=F32)


def nt(left, right):
    return lax.dot_general(left, right, (((1,), (1,)), ((), ())), preferred_element_type=F32)


def norm_stats(values):
    centered = values - jnp.mean(values, axis=-1, keepdims=True)
    factor = lax.rsqrt(jnp.mean(centered * centered, axis=-1, keepdims=True) + LN_EPS)
    return centered * factor, factor


def norm_back(grads, normalized, factor, gain):
    scaled = grads * gain
    first = jnp.mean(scaled, axis=-1, keepdims=True)
    second = jnp.mean(scaled * normalized, axis=-1, keepdims=True)
    return factor * (scaled - first - normalized * second)


def copy_to(src, dst, send, recv, device):
    return pltpu.make_async_remote_copy(
        src_ref=src, dst_ref=dst, send_sem=send, recv_sem=recv, device_id=device,
        device_id_type=MESH,
    )


def layer_kernel(
    tight,
    tokens, cotangent, wq_t, wk_t, wv_t, w_out, w_up, w_down,
    segment_ids, *rest,
):
    b_refs, rest = rest[:10], rest[10:]
    layer_body(tight, tokens, cotangent, wq_t, wk_t, wv_t, w_out, w_up, w_down, segment_ids,
               b_refs, *rest)


def layer_body(
    tight,
    tokens, cotangent, wq_t, wk_t, wv_t, w_out, w_up, w_down, segment_ids, b_refs,
    result_o, grad_o, sums_a, sums_b, vec_o, bias_o,
    x_all, h_all, g2_all, g1_all, wu_t, wd_t, wo_t,
    part_last, part_mate, land_last, land_mate, land_far, passed, out_rows,
    small_own, small_v, cot_v, staged, wqkv, wo, wu, wd,
    seg_nat, seg_cols, cos_t, sin_t,
    qkv_s, k2_s, probs, probs_low, ds_s, o_s, act, dgelu, dz_s, do_s, dqk_s, dv_s,
    q_t, do_t, dk_t, dv_t, h_own, g_own, own_part,
    grads, first_in, second_in, grads_mid, grads_in, grads_sum,
    vec, vec_x, vec_in, bias, bias_x, bias_in, seg_v, b_v,
    ag_s, ag_r, rs_s, rs_r, sw_s, sw_r, wx_s, wx_r, dx_s, dx_r, dq_s, dq_r, dz_sem_s, dz_sem_r,
    vec_s, vec_r, bias_s, bias_r, out_s, out_r, loc, b_sem,
):
    dp, ten = lax.axis_index("dp"), lax.axis_index("tensor")
    low = lax.rem(ten, 2)
    if tight:
        col, core, half = dp // 2, lax.rem(dp, 2), ten // 2
        col_x, col_y = lax.rem(col, 2), col // 2
        slot = low + 2 * core
        mate_slot = low + 2 * (1 - core)
        far_slot = 1 - low + 2 * core
        last_slot = 1 - low + 2 * (1 - core)
        mate = {"dp": col * 2 + 1 - core, "tensor": ten}
        far = {"dp": dp, "tensor": ten + 1 - 2 * low}
        other = lax.rem(ten + 2, 4)
        partner = {"dp": col * 2 + 1 - core, "tensor": other}
        across = {"dp": dp, "tensor": other}
        cols = [{"dp": lax.rem(col + j, 4) * 2 + core, "tensor": ten} for j in (1, 2, 3)]
        next_x = {"dp": (col_y * 2 + 1 - col_x) * 2 + core, "tensor": ten}
        next_y = {"dp": ((1 - col_y) * 2 + col_x) * 2 + core, "tensor": ten}
        home = core == half
        away = core != half
        met = [mate, far, across, partner, *cols]
    else:
        slot = ten
        mate_slot = ten + 1 - 2 * low
        far_slot = lax.rem(ten + 2, 4)
        last_slot = 3 - ten
        mate = {"dp": dp, "tensor": mate_slot}
        far = {"dp": dp, "tensor": far_slot}
        met = [mate, far]

    rows, width = tokens.shape
    length = 4 * rows
    chunk = rows // CHUNKS
    token_part = rows // 2
    both = (0, 2 * rows)
    units = [(2 * rows + 2 * c * chunk, 2 * chunk) for c in range(CHUNKS)]

    def local(src, dst, sem):
        return pltpu.make_async_copy(src, dst, sem)

    barrier = pltpu.get_barrier_semaphore()
    for device in met:
        pl.semaphore_signal(barrier, inc=1, device_id=device, device_id_type=MESH)

    b_copies = [local(src, dst, b_sem.at[i]) for i, (src, dst) in enumerate(zip(b_refs, b_v))]
    b_copies.append(local(segment_ids, seg_v, b_sem.at[10]))
    for copy in b_copies:
        copy.start()
    raw = []
    for i, w in enumerate((wq_t, wk_t, wv_t)):
        raw.append((w.at[pl.ds(0, 128)], (0, 128, 384)[i], 128))
        raw.append((w.at[pl.ds(128, 64)], (256, 320, 512)[i], 64))

    def raw_copy(i, ref):
        src, at, size = raw[i]
        return local(src, ref.at[pl.ds(at, size)], loc.at[i])

    to_tokens = [
        local(
            tokens.at[pl.ds(c * token_part, token_part)],
            x_all.at[pl.ds(c * token_part, token_part)], sw_r.at[4 + c],
        )
        for c in range(2)
    ]
    to_small = local(small_own, small_v.at[pl.ds(0, 8)], sw_r.at[0])
    to_cot = local(cotangent, cot_v, sw_r.at[11])
    wo_rows = w_out.shape[0]
    to_out = local(w_out, wo.at[pl.ds(0, wo_rows)], loc.at[6])
    to_up = local(w_up, wu, loc.at[7])
    to_down = local(w_down, wd, loc.at[8])

    def load_own():
        for copy in to_tokens:
            copy.start()
        for i in range(6):
            raw_copy(i, wqkv).start()
        for copy in (to_out, to_up, to_down, to_cot):
            copy.start()

    def stage_own():
        for i in range(6):
            raw_copy(i, staged).start()

    if tight:
        pl.when(home)(load_own)
        pl.when(away)(stage_own)
    else:
        load_own()

    wo[wo_rows:, :] = jnp.zeros((wo.shape[0] - wo_rows, width), BF16)
    wqkv[576:, :] = jnp.zeros((wqkv.shape[0] - 576, width), BF16)

    def vector(ref):
        return ref[...].astype(F32).reshape(1, ref.shape[0])

    for copy in b_copies:
        copy.wait()
    bq, bk, bv = (vector(b_v[i]) for i in range(3))
    for at, b in ((0, bq), (128, bk), (384, bv)):
        small_own[0:1, at:at + 128] = b[:, :128]
    small_own[0:1, 256:384] = jnp.concatenate([bq[:, 128:], bk[:, 128:]], axis=1)
    small_own[0:1, 512:640] = jnp.concatenate([bv[:, 128:], jnp.zeros((1, 64), F32)], axis=1)
    small_own[0:1, 640:] = jnp.zeros((1, width - 640), F32)
    small_own[B_UP:B_UP + 1, :] = vector(b_v[3])
    small_own[SEGMENTS:8, :] = jnp.zeros((8 - SEGMENTS, width), F32)
    small_own[SEGMENTS:SEGMENTS + 1, :length] = seg_v[...].astype(F32)
    for i in range(6):
        small_v[B_OUT + i:B_OUT + i + 1, :] = vector(b_v[4 + i])
    pl.semaphore_wait(barrier, len(met))

    weight_items = {
        1: (wqkv, staged, 576, 0, 3), 2: (wqkv, staged, 576, 1, 3), 3: (wqkv, staged, 576, 2, 3),
        6: (wo, w_out, wo_rows, 0, 1),
        7: (wu, w_up, width, 0, 2), 8: (wu, w_up, width, 1, 2),
        9: (wd, w_down, width, 0, 2), 10: (wd, w_down, width, 1, 2),
    }
    item_rank = {item: i for i, item in enumerate(weight_items)}

    def item_rows(item, q):
        _, _, total, part, count = weight_items[item]
        size = total // 4 // count
        return pl.ds(q * (total // 4) + part * size, size)

    def swap(item):
        if item in weight_items:
            dst, src = weight_items[item][:2]
            at = item_rows(item, col)
            src, dst = src.at[at], dst.at[at]
        elif item == 0:
            src, dst = small_own, small_v.at[pl.ds(0, 8)]
        elif item == 11:
            src, dst = cotangent, cot_v
        else:
            at = pl.ds((item - 4) * token_part, token_part)
            src, dst = tokens.at[at], x_all.at[at]
        return copy_to(src, dst, sw_s.at[item], sw_r.at[item], partner)

    def spread(item, j):
        ref = weight_items[item][0].at[item_rows(item, col)]
        rank = item_rank[item]
        return copy_to(ref, ref, wx_s.at[rank, j], wx_r.at[rank, j], cols[j])

    def spread_in(item, j):
        ref = weight_items[item][0].at[item_rows(item, lax.rem(col + 3 - j, 4))]
        rank = item_rank[item]
        return copy_to(ref, ref, wx_s.at[rank, j], wx_r.at[rank, j], cols[j])

    def relay(item, follow=None):
        if tight:
            @pl.when(away)
            def _():
                swap(item).wait_recv()
                for j in range(3):
                    spread(item, j).start()
                if follow is not None:
                    swap(follow).start()

    def weights_ready(copies, *items):
        if not tight:
            for copy in copies:
                copy.wait()
            return

        @pl.when(home)
        def _():
            for copy in copies:
                copy.wait()

        @pl.when(away)
        def _():
            for item in items:
                for j in range(3):
                    spread_in(item, j).wait_recv()

    if tight:
        @pl.when(away)
        def _():
            swap(0).start()
            for i in range(6):
                raw_copy(i, staged).wait()
            for item in (1, 2, 3, 4, 5):
                swap(item).start()

        pl.when(home)(to_small.start)
    else:
        to_small.start()

    def at_own(c):
        return pl.ds(c * chunk, chunk)

    def at_mate(c):
        return pl.ds(rows + c * chunk, chunk)

    def at_far(c):
        return pl.ds(2 * rows + 2 * c * chunk, chunk)

    def at_last(c):
        return pl.ds(2 * rows + (2 * c + 1) * chunk, chunk)

    def gather_copy(i, buf, c, kind):
        src, dst, device = (
            (at_own(c), at_mate(c), mate), (at_own(c), at_far(c), far), (at_far(c), at_last(c), mate)
        )[kind]
        return copy_to(
            buf.at[src], buf.at[dst], ag_s.at[i, c, kind], ag_r.at[i, c, kind], device
        )

    def ag_own(i, buf, c):
        gather_copy(i, buf, c, 1).start()
        gather_copy(i, buf, c, 0).start()

    def own_tokens(part):
        for c in range(CHUNKS // 2):
            ag_own(0, x_all, part * (CHUNKS // 2) + c)

    def ag_mate(i, buf):
        for c in range(CHUNKS):
            gather_copy(i, buf, c, 0).wait_recv()

    def ag_unit(i, buf, c):
        gather_copy(i, buf, c, 1).wait_recv()
        gather_copy(i, buf, c, 2).start()
        gather_copy(i, buf, c, 2).wait_recv()

    def rs_copy(i, c, kind):
        src, dst, device = (
            (part_last.at[i, c], land_last.at[i, c], mate),
            (part_mate.at[i, c], land_mate.at[i, c], mate),
            (passed.at[i, c], land_far.at[i, c], far),
        )[kind]
        return copy_to(src, dst, rs_s.at[i, c, kind], rs_r.at[i, c, kind], device)

    def rs_whole(i):
        return copy_to(part_mate.at[i], land_mate.at[i], rs_s.at[i, 0, 1], rs_r.at[i, 0, 1], mate)

    def rs_unit(i, c, term):
        part_last[i, c] = term[chunk:].astype(BF16)
        rs_copy(i, c, 0).start()
        own_part[rows + c * chunk:rows + (c + 1) * chunk, :] = term[:chunk]

    def rs_pass(i, c):
        rs_copy(i, c, 0).wait_recv()
        term = own_part[rows + c * chunk:rows + (c + 1) * chunk, :]
        passed[i, c] = (term + land_last[i, c].astype(F32)).astype(BF16)
        rs_copy(i, c, 2).start()

    def rs_mate(i, term):
        for c in range(CHUNKS):
            part_mate[i, c] = term[rows + c * chunk:rows + (c + 1) * chunk].astype(BF16)
        rs_whole(i).start()
        own_part[0:rows, :] = term[:rows]

    def reduced(i, c):
        if c == 0:
            rs_whole(i).wait_recv()
        rs_copy(i, c, 2).wait_recv()
        term = own_part[c * chunk:(c + 1) * chunk, :]
        return term + land_mate[i, c].astype(F32) + land_far[i, c].astype(F32)

    if not tight:
        for c in range(2):
            to_tokens[c].wait()
            own_tokens(c)
    else:
        @pl.when(home)
        def _():
            for c in range(2):
                to_tokens[c].wait()
                own_tokens(c)

    to_small.wait()
    seg_row = small_v[SEGMENTS:SEGMENTS + 1, :length]
    seg_nat[...] = jnp.transpose(jnp.broadcast_to(seg_row, (128, length)))
    segs = seg_nat[...]
    place = lax.broadcasted_iota(jnp.int32, (length, 128), 0).astype(F32)
    start = jnp.zeros((length, 128), F32)
    for s in range(4):
        before = jnp.sum(jnp.where(seg_row < s, 1.0, 0.0), axis=1, keepdims=True)
        start = jnp.where(segs == s, before, start)
    cos_t[...] = place - start
    order = [(c, slot, c) for c in range(CHUNKS)]
    order += [(CHUNKS + c, mate_slot, c) for c in range(CHUNKS)]
    for c in range(CHUNKS):
        order += [(2 * (CHUNKS + c), far_slot, c), (2 * (CHUNKS + c) + 1, last_slot, c)]
    for to, from_slot, c in order:
        at = pl.ds(pl.multiple_of(from_slot * rows + c * chunk, chunk), chunk)
        seg_cols[to * chunk:(to + 1) * chunk, :] = seg_nat[at, :]
        sin_t[to * chunk:(to + 1) * chunk, :] = cos_t[at, :]
    lane = lax.broadcasted_iota(jnp.int32, (1, 128), 1)
    frequency = jnp.exp(lax.rem(lane, 32).astype(F32) * (-math.log(10000.0) / 32))
    sign = jnp.where(lax.rem(lane, 64) < 32, -1.0, 1.0)
    angle = sin_t[...] * frequency
    cos_t[...] = jnp.cos(angle)
    sin_t[...] = jnp.sin(angle) * sign
    seg_row = jnp.transpose(seg_cols[...])[0:1, :]


    low_lane = lane < 64

    def turn(values):
        return jnp.where(
            lax.rem(lane, 64) < 32, pltpu.roll(values, 96, 1), pltpu.roll(values, 32, 1)
        )

    scale = HD ** (-0.5)

    def project_rows(lo, n):
        here = slice(lo, lo + n)
        x = x_all[here, :]
        pre = nt(x, wqkv[...]) + small_v[B_QKV:B_QKV + 1, :640]
        cosine, sine = cos_t[here, :], sin_t[here, :]

        def rot(block):
            return block * cosine + turn(block) * sine

        query, key, mixed = rot(pre[:, :128]), rot(pre[:, 128:256]), rot(pre[:, 256:384])
        qkv_s[here, 0:128] = (query.astype(BF16) * scale).astype(BF16)
        qkv_s[here, 128:256] = key.astype(BF16)
        qkv_s[here, 256:384] = (jnp.where(low_lane, mixed, 0.0).astype(BF16) * scale).astype(BF16)
        qkv_s[here, 384:640] = pre[:, 384:640].astype(BF16)
        k2_s[here, :] = jnp.where(low_lane, pltpu.roll(mixed, 64, 1), 0.0).astype(BF16)

    if tight:
        @pl.when(away)
        def _():
            swap(1).wait_recv()
            for j in range(3):
                spread(1, j).start()
            swap(2).wait_recv()
            for j in range(3):
                spread(2, j).start()
            swap(6).start()
            swap(4 + 0).wait_recv()
            own_tokens(0)
            swap(7).start()
            swap(4 + 1).wait_recv()
            own_tokens(1)
            swap(3).wait_recv()
            for j in range(3):
                spread(3, j).start()
            swap(8).start()
            swap(6).wait_recv()
            for j in range(3):
                spread(6, j).start()
            swap(9).start()
            swap(10).start()
    weights_ready([raw_copy(i, wqkv) for i in range(6)], 1, 2, 3)
    ag_mate(0, x_all)
    project_rows(*both)
    for c in range(CHUNKS):
        ag_unit(0, x_all, c)
    project_rows(2 * rows, 2 * rows)

    def masked(block, head):
        if head == 2:
            return block
        keep = low_lane if head == 0 else ~low_lane
        return jnp.where(keep, block, jnp.zeros_like(block))

    def attend(s, carry):
        here = pl.ds(pl.multiple_of(s * rows, rows), rows)
        same = seg_cols[here, 0:1] == seg_row
        outs = []
        for head in range(3):
            q_at, v_at = (0, 384) if head < 2 else (256, 512)
            query = masked(qkv_s[here, q_at:q_at + 128], head)
            keys = qkv_s[:, 128:256] if head < 2 else k2_s[...]
            scores = jnp.where(same, nt(query, keys), -1e30)
            scores = jnp.exp(scores - jnp.max(scores, axis=1, keepdims=True))
            weight = scores * (1.0 / jnp.sum(scores, axis=1, keepdims=True))
            probs[head, here, :] = weight
            weight_low = weight.astype(BF16)
            probs_low[head, here, :] = weight_low
            outs.append(nn(weight_low, qkv_s[:, v_at:v_at + 128]))
        o_s[here, 0:128] = jnp.where(low_lane, outs[0], outs[1]).astype(BF16)
        o_s[here, 128:256] = outs[2].astype(BF16)
        return carry

    def mix(lo, n):
        return nn(o_s[lo:lo + n, :], wo[...])

    attend(2, 0)
    if tight:
        @pl.when(away)
        def _():
            swap(7).wait_recv()
            for j in range(3):
                spread(7, j).start()
    weights_ready([to_out], 6)
    for c in range(CHUNKS // 2):
        rs_unit(0, c, mix(*units[c]))
    attend(3, 0)
    if tight:
        @pl.when(away)
        def _():
            swap(8).wait_recv()
            for j in range(3):
                spread(8, j).start()
    for c in range(CHUNKS // 2, CHUNKS):
        rs_unit(0, c, mix(*units[c]))
    for c in range(CHUNKS // 2):
        rs_pass(0, c)
    lax.fori_loop(0, 1, attend, 0)
    for c in range(CHUNKS // 2, CHUNKS):
        rs_pass(0, c)
    if tight:
        @pl.when(away)
        def _():
            swap(9).wait_recv()
            for j in range(3):
                spread(9, j).start()
    lax.fori_loop(1, 2, attend, 0)
    rs_mate(0, mix(*both))
    if tight:
        @pl.when(away)
        def _():
            swap(10).wait_recv()
            for j in range(3):
                spread(10, j).start()
            swap(11).start()
    factors = []

    def spot(c):
        return slice(c * chunk, (c + 1) * chunk)

    def row_of(at):
        return small_v[at:at + 1, :]

    for c in range(CHUNKS):
        here = spot(c)
        into = reduced(0, c) + x_all[here, :].astype(F32) + row_of(B_OUT)
        normal1, factor1 = norm_stats(into)
        factors.append(factor1)
        normed = normal1 * row_of(G_MIX) + row_of(S_MIX)
        h_own[0, here, :] = normed
        h_own[1, here, :] = normal1
        h_all[here, :] = normed.astype(BF16)
        ag_own(1, h_all, c)


    def feed(lo, n):
        here = slice(lo, lo + n)
        h = h_all[here, :]
        z = nn(h, wu[...]) + row_of(B_UP)
        phi = 0.5 * (1.0 + lax.erf(z * (2.0 ** -0.5)))
        act[here, :] = (z * phi).astype(BF16)
        dgelu[here, :] = phi + z * (jnp.exp(-0.5 * z * z) * (1.0 / math.sqrt(2.0 * math.pi)))

    def shrink(lo, n):
        return nn(act[lo:lo + n, :], wd[...])

    weights_ready([to_up], 7, 8)
    ag_mate(1, h_all)
    feed(*both)
    wu_t[...] = jnp.transpose(wu[...])
    wo_t[...] = jnp.transpose(wo[...])
    for c in range(CHUNKS):
        ag_unit(1, h_all, c)
        if c > 0:
            rs_pass(1, c - 1)
        feed(*units[c])
        if c == 0:
            weights_ready([to_down], 9, 10)
        rs_unit(1, c, shrink(*units[c]))
    rs_pass(1, CHUNKS - 1)
    rs_mate(1, shrink(*both))
    wd_t[...] = jnp.transpose(wd[...])

    def hand_out(i, src, dst, c):
        src, dst = src.at[pl.ds(c * chunk, chunk)], dst.at[pl.ds(c * chunk, chunk)]
        keep = local(src, dst, out_r.at[i, c])
        send = copy_to(src, dst, out_s.at[i, c], out_r.at[i, c], partner) if tight else None
        return keep, send

    def hand_start(*args):
        keep, send = hand_out(*args)
        if tight:
            pl.when(home)(keep.start)
            pl.when(away)(send.start)
        else:
            keep.start()

    to_cot.wait()
    sums = [0.0, 0.0, 0.0]
    for c in range(CHUNKS):
        here = spot(c)
        into = reduced(1, c) + h_own[0, here, :] + row_of(B_DOWN)
        normal2, factor2 = norm_stats(into)
        dy = cot_v[here, :].astype(F32)
        grad2 = norm_back(dy, normal2, factor2, row_of(G_FEED))
        g_own[0, here, :] = grad2
        g2_all[here, :] = grad2.astype(BF16)
        ag_own(2, g2_all, c)
        out_rows[0, here, :] = (normal2 * row_of(G_FEED) + row_of(S_FEED)).astype(BF16)
        hand_start(0, out_rows.at[0], result_o, c)
        for i, term in enumerate((grad2, dy * normal2, dy)):
            sums[i] = sums[i] + jnp.sum(term, axis=0, keepdims=True)
    vec[...] = jnp.zeros(vec.shape, F32)
    for i in range(3):
        vec[0, 3 + i:4 + i, :] = sums[i]

    def weight_grad(at_piece, value):
        quarter = width // 4
        for y in range(2):
            found = value(slice(2 * y * quarter, 2 * (y + 1) * quarter)).astype(BF16)
            for x in range(2):
                for h in range(found.shape[1] // 384):
                    part = found[x * quarter:(x + 1) * quarter, h * 384:(h + 1) * 384]
                    grads[at_piece + h][y, x] = part

    def first_copy(i, h):
        if h == 0:
            src, device = grads[2 * i].at[:, 1 - col_x], next_x
        else:
            src, device = grads[2 * i + 1].at[1 - col_y], next_y
        return copy_to(
            src, first_in.at[2 * i + h], dx_s.at[i, h, 0], dx_r.at[i, h, 0], device
        )

    def second_copy(i, h):
        keep, device = (1 - col_y, next_y) if h == 0 else (1 - col_x, next_x)
        return copy_to(
            grads_mid.at[2 * i + h, keep], second_in.at[2 * i + h], dx_s.at[i, h, 1],
            dx_r.at[i, h, 1], device,
        )

    def first_send(i):
        if tight:
            for h in range(2):
                first_copy(i, h).start()

    def first_land(i):
        if not tight:
            return
        for h in range(2):
            first_copy(i, h).wait_recv()
            for j in range(2):
                own = grads[2 * i][j, col_x] if h == 0 else grads[2 * i + 1][col_y, j]
                came = first_in[2 * i + h, j].astype(F32)
                grads_mid[2 * i + h, j] = (own.astype(F32) + came).astype(BF16)
            second_copy(i, h).start()

    def second_land(i):
        if not tight:
            return
        totals = []
        for h in range(2):
            second_copy(i, h).wait_recv()
            own = grads_mid[2 * i + h, col_y if h == 0 else col_x]
            totals.append(own.astype(F32) + second_in[2 * i + h].astype(F32))
        finish_sum(i, jnp.concatenate(totals, axis=1))

    def finish_sum(i, total):
        grads_sum[i][...] = total.astype(BF16).reshape(grads_sum[i].shape)

        @pl.when(home)
        def _():
            keep_sum(i).start()
            mate_sum(i).start()

        @pl.when(away)
        def _():
            for copy in away_sums(i):
                copy.start()

    def direct_copy(i, j):
        to = lax.rem(col + 1 + j, 4)
        return copy_to(
            grads[i + 2].at[to // 2, lax.rem(to, 2)], grads_in.at[i - OV, j],
            dq_s.at[i - OV, j], dq_r.at[i - OV, j], cols[j],
        )

    def direct_send(i):
        if tight:
            for j in range(3):
                direct_copy(i, j).start()

    def direct_land(i):
        if not tight:
            return
        total = grads[i + 2][col_y, col_x].astype(F32)
        for j in range(3):
            direct_copy(i, j).wait_recv()
            total = total + grads_in[i - OV, j].astype(F32)
        finish_sum(i, total)

    def keep_sum(i):
        return local(grads_sum[i].at[core], sums_a[i], dz_sem_r.at[i, 0])

    def mate_sum(i):
        return copy_to(
            grads_sum[i].at[1 - core], sums_a[i], dz_sem_s.at[i, 0], dz_sem_r.at[i, 0], mate
        )

    def away_sums(i):
        return (
            copy_to(
                grads_sum[i].at[core], sums_b[i], dz_sem_s.at[i, 0], dz_sem_r.at[i, 1], across
            ),
            copy_to(
                grads_sum[i].at[1 - core], sums_b[i], dz_sem_s.at[i, 1], dz_sem_r.at[i, 1], partner
            ),
        )

    def feed_back(lo, n):
        here = slice(lo, lo + n)
        dz_s[here, :] = (nn(g2_all[here, :], wd_t[...]) * dgelu[here, :]).astype(BF16)

    def widen(lo, n):
        return nn(dz_s[lo:lo + n, :], wu_t[...])

    ag_mate(2, g2_all)
    feed_back(*both)
    for c in range(CHUNKS):
        ag_unit(2, g2_all, c)
        if c > 0:
            rs_pass(2, c - 1)
        if c == CHUNKS - 1:
            weight_grad(0, lambda at: tn(g2_all[:, at], act[...]))
            first_send(DOWN)
        feed_back(*units[c])
        rs_unit(2, c, widen(*units[c]))
    rs_pass(2, CHUNKS - 1)
    rs_mate(2, widen(*both))

    weight_grad(2, lambda at: tn(h_all[:, at], dz_s[...]))
    vec[1, pl.ds(slot, 1), :] = jnp.sum(dz_s[...].astype(F32), axis=0, keepdims=True)

    sums = [0.0, 0.0, 0.0]
    for c in range(CHUNKS):
        here = spot(c)
        dh = reduced(2, c) + g_own[0, here, :]
        normal1 = h_own[1, here, :]
        grad1 = norm_back(dh, normal1, factors[c], row_of(G_MIX))
        g_own[1, here, :] = grad1
        g1_all[here, :] = grad1.astype(BF16)
        ag_own(3, g1_all, c)
        for i, term in enumerate((grad1, dh * normal1, dh)):
            sums[i] = sums[i] + jnp.sum(term, axis=0, keepdims=True)
    for i in range(3):
        vec[0, i:i + 1, :] = sums[i]

    class Total:
        def __init__(self, own, sent, landing, send, recv):
            self.own, self.sent, self.landing, self.send, self.recv = own, sent, landing, send, recv

        def copy(self, j):
            src = self.own if j < 3 else self.sent.at[j - 3]
            device = (*cols, mate, far, across)[j]
            return copy_to(src, self.landing.at[j], self.send.at[j], self.recv.at[j], device)

        def begin(self):
            if tight:
                for j in range(3):
                    self.copy(j).start()

        def columns(self):
            if tight:
                for j in range(3):
                    self.copy(j).wait_recv()
                self.sent[0] = self.own[...] + self.landing[0] + self.landing[1] + self.landing[2]
                self.copy(3).start()

        def step(self, k):
            if tight:
                self.copy(2 + k).wait_recv()
                self.sent[k] = self.sent[k - 1] + self.landing[2 + k]
                if k < 3:
                    self.copy(3 + k).start()

        def sends_done(self):
            for j in range(6):
                self.copy(j).wait_send()

    vec_total = Total(vec, vec_x, vec_in, vec_s, vec_r)
    bias_total = Total(bias, bias_x, bias_in, bias_s, bias_r)
    vec_total.begin()

    def heads_back(lo, n):
        here = slice(lo, lo + n)
        do_s[here, :] = nn(g1_all[here, :], wo_t[...]).astype(BF16)

    def back(values, here):
        return values * cos_t[here, :] - turn(values) * sin_t[here, :]

    def attend_back(s, carry):
        here = pl.ds(pl.multiple_of(s * rows, rows), rows)
        outs = []
        for head in range(3):
            v_at, o_at = (384, 0) if head < 2 else (512, 128)
            grad_o = masked(do_s[here, o_at:o_at + 128], head)
            grad_p = nt(grad_o, qkv_s[:, v_at:v_at + 128])
            weight = probs[head, here, :]
            dot = jnp.sum(grad_p * weight, axis=1, keepdims=True)
            ds = (weight * (grad_p - dot)).astype(BF16)
            ds_s[head, here, :] = ds
            keys = qkv_s[:, 128:256] if head < 2 else k2_s[...]
            outs.append(nn(ds, keys) * scale)
        dqk_s[here, 0:128] = back(jnp.where(low_lane, outs[0], outs[1]), here).astype(BF16)
        dqk_s[here, 256:384] = back(outs[2], here).astype(BF16)
        return carry

    q_t[0:128, :] = jnp.transpose(qkv_s[:, 0:128])
    q_t[128:256, :] = jnp.transpose(qkv_s[:, 256:384])
    ag_mate(3, g1_all)
    heads_back(*both)
    first_land(DOWN)
    lax.fori_loop(0, 1, attend_back, 0)
    first_send(UP)
    lax.fori_loop(1, 2, attend_back, 0)
    vec_total.columns()
    for c in range(CHUNKS):
        ag_unit(3, g1_all, c)
    heads_back(2 * rows, 2 * rows)
    vec_total.step(1)
    second_land(DOWN)
    do_t[0:128, :] = jnp.transpose(do_s[:, 0:128])
    do_t[128:256, :] = jnp.transpose(do_s[:, 128:256])
    for head in range(2):
        at = slice(head * 64, head * 64 + 64)
        dv_t[at, :] = nn(do_t[at, :], probs_low[head])
    dv_t[128:192, :] = jnp.zeros((64, length), F32)
    dv_t[192:256, :] = nn(do_t[128:192, :], probs_low[2])
    dv_s[:, 0:128] = jnp.transpose(dv_t[0:128, :]).astype(BF16)
    dv_s[:, 128:256] = jnp.transpose(dv_t[128:256, :]).astype(BF16)

    def out_value(at):
        out = tn(g1_all[:, at], o_s[...])
        value = tn(x_all[:, at], dv_s[...])
        return jnp.concatenate(
            [out[:, :128], value[:, :128], out[:, 128:] + value[:, 128:]], axis=1
        )

    weight_grad(4, out_value)
    lax.fori_loop(2, 3, attend_back, 0)
    lax.fori_loop(3, 4, attend_back, 0)
    first_land(UP)
    vec_total.step(2)
    for head in range(3):
        at = slice(head * 64, head * 64 + 64)
        dk_t[at, :] = nn(q_t[at, :], ds_s[head])
    dk_t[192:, :] = jnp.zeros((64, length), F32)
    everything = slice(None)
    dqk_s[:, 128:256] = back(jnp.transpose(dk_t[0:128, :]), everything).astype(BF16)
    key2 = back(jnp.transpose(dk_t[128:256, :]), everything)
    query2 = dqk_s[:, 256:384].astype(F32)
    dqk_s[:, 256:384] = jnp.where(low_lane, query2, pltpu.roll(key2, 64, 1)).astype(BF16)

    query_key = jnp.sum(dqk_s[...].astype(F32), axis=0, keepdims=True)
    values = jnp.sum(dv_s[...].astype(F32), axis=0, keepdims=True)
    bias[...] = jnp.zeros(bias.shape, F32)
    for i in range(3):
        bias[slot, i:i + 1, :] = query_key[:, i * 128:(i + 1) * 128]
    for i in range(2):
        bias[slot, 3 + i:4 + i, :] = values[:, i * 128:(i + 1) * 128]
    value_low = jnp.where(
        low_lane, pltpu.roll(dv_s[:, 128:256].astype(F32), 64, 1), 0.0
    ).astype(BF16)

    def to_input(lo, n):
        term = nn(dqk_s[lo:lo + n, :], wqkv[0:384, :])
        term = term + nn(dv_s[lo:lo + n, 0:128], wqkv[384:512, :])
        return term + nn(value_low[lo:lo + n, :], wqkv[512:640, :])

    bias_total.begin()
    direct_send(OV)
    weight_grad(5, lambda at: tn(x_all[:, at], dqk_s[...]))
    direct_send(QK)
    for c in range(CHUNKS):
        rs_unit(3, c, to_input(*units[c]))
    for c in range(CHUNKS):
        rs_pass(3, c)
    rs_mate(3, to_input(*both))
    second_land(UP)
    bias_total.columns()
    for c in range(CHUNKS):
        here = spot(c)
        out_rows[1, here, :] = (reduced(3, c) + g_own[1, here, :]).astype(BF16)
        hand_start(1, out_rows.at[1], grad_o, c)
    bias_total.step(1)
    vec_total.step(3)
    for i, buf in enumerate((x_all, h_all, g2_all, g1_all)):
        for c in range(CHUNKS):
            for kind in range(3):
                gather_copy(i, buf, c, kind).wait_send()
                if kind != 1:
                    rs_copy(i, c, kind).wait_send()
        rs_whole(i).wait_send()

    def out_waits(i, dst):
        for c in range(CHUNKS):
            hand_out(i, out_rows.at[i], dst, c)[0].wait()
        if tight:
            @pl.when(away)
            def _():
                for c in range(CHUNKS):
                    hand_out(i, out_rows.at[i], dst, c)[1].wait_send()

    out_waits(0, result_o)
    if tight:
        for i in (DOWN, UP):
            for h in range(2):
                first_copy(i, h).wait_send()
                second_copy(i, h).wait_send()
        vec_total.sends_done()

        @pl.when(away)
        def _():
            for item in weight_items:
                for j in range(3):
                    spread(item, j).wait_send()
            for item in range(12):
                swap(item).wait_send()

    direct_land(OV)
    if tight:
        for j in range(3):
            direct_copy(OV, j).wait_send()
    bias_total.step(2)
    direct_land(QK)
    bias_total.step(3)
    if tight:
        keep = [local(vec_x.at[3], vec_o, loc.at[0]), local(bias_x.at[3], bias_o, loc.at[1])]
    else:
        keep = [local(vec, vec_o, loc.at[0]), local(bias, bias_o, loc.at[1])]
        keep += [local(grads[i], sums_a[i], loc.at[2 + i]) for i in range(6)]
    for copy in keep:
        copy.start()

    out_waits(1, grad_o)
    for copy in keep:
        copy.wait()
    if tight:
        for i in range(4):
            keep_sum(i).wait()
            away_sums(i)[0].wait_recv()
        for j in range(3):
            direct_copy(QK, j).wait_send()
        bias_total.sends_done()

        @pl.when(home)
        def _():
            for i in range(4):
                mate_sum(i).wait_send()

        @pl.when(away)
        def _():
            for i in range(4):
                for copy in away_sums(i):
                    copy.wait_send()


def layer_call(tight, shapes, *args):
    rows, width = shapes
    hidden = width
    length = 4 * rows
    chunk = rows // CHUNKS
    heads_wide, qkv_wide = 256, 640
    widths = (hidden, hidden, 384, 384)
    any_space = pl.BlockSpec(memory_space=pl.ANY)
    quarter = width // 4
    if tight:
        sums = [jax.ShapeDtypeStruct((quarter // 2, w), BF16) for w in widths]
    else:
        sums = [jax.ShapeDtypeStruct((2, 2, quarter, 384), BF16)] * 6
    out_shape = (
        jax.ShapeDtypeStruct((rows, width), BF16),
        jax.ShapeDtypeStruct((rows, width), BF16),
        sums,
        [jax.ShapeDtypeStruct((quarter // 2, w), BF16) for w in widths],
        jax.ShapeDtypeStruct((2, 8, width), F32),
        jax.ShapeDtypeStruct((4, 8, 128), F32),
    )
    V = pltpu.VMEM
    D = pltpu.SemaphoreType.DMA
    pieces = V((4, CHUNKS, chunk, width), BF16)
    scratch = [
        *[V((length, width), BF16)] * 4,
        V((hidden, width), BF16), V((width, hidden), BF16), V((width, heads_wide), BF16),
        *[pieces] * 6, V((2, rows, width), BF16),
        V((8, width), F32), V((16, width), F32), V((rows, width), BF16),
        V((576, width), BF16), V((qkv_wide, width), BF16), V((heads_wide, width), BF16),
        V((width, hidden), BF16), V((hidden, width), BF16),
        *[V((length, 128), F32)] * 4,
        V((length, qkv_wide), BF16), V((length, 128), BF16), V((3, length, length), F32),
        V((3, length, length), BF16), V((3, length, length), BF16), V((length, heads_wide), BF16),
        V((length, hidden), BF16), V((length, hidden), F32), V((length, hidden), BF16),
        V((length, heads_wide), BF16), V((length, 384), BF16), V((length, heads_wide), BF16),
        V((heads_wide, length), BF16), V((heads_wide, length), BF16),
        V((heads_wide, length), F32), V((heads_wide, length), F32),
        V((2, rows, width), F32), V((2, rows, width), F32), V((2 * rows, width), F32),
        [V((2, 2, quarter, 384), BF16)] * 6,
        V((4, 2, quarter, 384), BF16), V((4, quarter, 384), BF16), V((4, 2, quarter, 384), BF16),
        V((2, 3, quarter, 384), BF16),
        [V((2, quarter // 2, w), BF16) for w in widths],
        V((2, 8, width), F32), V((4, 2, 8, width), F32), V((6, 2, 8, width), F32),
        V((4, 8, 128), F32), V((4, 4, 8, 128), F32), V((6, 4, 8, 128), F32),
        V((1, length), jnp.int32), [V(b.shape, BF16) for b in args[9:]],
        *[D((4, CHUNKS, 3))] * 4, D((12,)), D((12,)), D((8, 3)), D((8, 3)),
        D((2, 2, 2)), D((2, 2, 2)), D((2, 3)), D((2, 3)), D((4, 2)), D((4, 2)),
        D((6,)), D((6,)), D((6,)), D((6,)), D((2, CHUNKS)), D((2, CHUNKS)), D((9,)), D((11,)),
    ]
    return pl.pallas_call(
        partial(layer_kernel, tight),
        out_shape=out_shape,
        in_specs=[any_space] * 19,
        out_specs=jax.tree.map(lambda _: any_space, out_shape),
        scratch_shapes=scratch,
        compiler_params=pltpu.CompilerParams(
            collective_id=0, has_side_effects=True, vmem_limit_bytes=61 << 20
        ),
    )(*args)


def finish_kernel(*refs):
    sources, refs = refs[:12], refs[12:]
    outs, refs = refs[:18], refs[18:]
    held, made, sem, out_sem = refs[:12], refs[12:30], refs[30], refs[31]
    (
        o_result, o_tokens, o_query, o_b_query, o_key, o_b_key, o_value, o_b_value, o_out, o_b_out,
        o_gain_mixer, o_shift_mixer, o_up, o_b_up, o_down, o_b_down, o_gain_feed, o_shift_feed,
    ) = made
    writes = [
        pltpu.make_async_copy(src, dst, out_sem.at[i]) for i, (src, dst) in enumerate(zip(made, outs))
    ]
    copies = [
        pltpu.make_async_copy(src, dst, sem.at[i]) for i, (src, dst) in enumerate(zip(sources, held))
    ]
    for copy in copies:
        copy.start()

    def take(i):
        copies[i].wait()
        return held[i][...]

    def total(i):
        return take(2 + i).astype(F32) + take(6 + i).astype(F32)

    o_result[...] = take(0)
    writes[0].start()
    o_tokens[...] = take(1).astype(F32)
    writes[1].start()
    o_down[...] = total(DOWN)
    writes[14].start()
    o_up[...] = total(UP)
    writes[12].start()
    out, query, key, value = split_pieces(total(OV), total(QK))
    o_out[...] = jnp.transpose(out)
    for ref, part in zip((o_query, o_key, o_value), (query, key, value)):
        ref[...] = part
    for i in (8, 2, 4, 6):
        writes[i].start()
    vec, bias = take(10), take(11)
    rows = (o_b_out, o_gain_mixer, o_shift_mixer, o_b_down, o_gain_feed, o_shift_feed)
    for i, ref in enumerate(rows):
        ref[...] = vec[0, i]
    o_b_up[...] = jnp.concatenate([vec[1, k:k + 1, :] for k in range(4)], axis=1).reshape(
        o_b_up.shape
    )
    for ref, (i, j, at) in zip(
        (o_b_query, o_b_key, o_b_value), ((0, 2, 0), (1, 2, 64), (3, 4, 64))
    ):
        parts = []
        for k in range(4):
            parts += [bias[k, i:i + 1, :], bias[k, j:j + 1, at:at + 64]]
        ref[...] = jnp.concatenate(parts, axis=1).reshape(ref.shape)
    for i in (3, 5, 7, 9, 10, 11, 13, 15, 16, 17):
        writes[i].start()
    for write in writes:
        write.wait()


def finish_call(shapes, *args):
    any_space = pl.BlockSpec(memory_space=pl.ANY)
    return pl.pallas_call(
        finish_kernel,
        out_shape=shapes,
        in_specs=[any_space] * len(args),
        out_specs=tuple(any_space for _ in shapes),
        scratch_shapes=[
            *[pltpu.VMEM(a.shape, a.dtype) for a in args],
            *[pltpu.VMEM(a.shape, a.dtype) for a in shapes],
            pltpu.SemaphoreType.DMA((len(args),)), pltpu.SemaphoreType.DMA((len(shapes),)),
        ],
        compiler_params=pltpu.CompilerParams(vmem_limit_bytes=61 << 20),
    )(*args)


def split_pieces(out_value, query_key):
    def pick(block, at, tail):
        return jnp.concatenate([block[..., at:at + 128], block[..., tail:tail + 64]], axis=-1)

    return (
        pick(out_value, 0, 256), pick(query_key, 0, 256), pick(query_key, 128, 320),
        pick(out_value, 128, 320),
    )


def on_device(
    tight,
    tokens,
    segment_ids,
    w_query,
    b_query,
    w_key,
    b_key,
    w_value,
    b_value,
    w_out,
    b_out,
    gain_mixer,
    shift_mixer,
    w_up,
    b_up,
    w_down,
    b_down,
    gain_feed,
    shift_feed,
    cotangent,
):
    rows, width = tokens.shape
    result, grad_rows, sums_a, sums_b, vec, bias = layer_call(
        tight, (rows, width), tokens, cotangent, w_query.T, w_key.T, w_value.T, w_out, w_up, w_down,
        segment_ids, b_query, b_key, b_value, b_up, b_out, gain_mixer, shift_mixer, b_down,
        gain_feed, shift_feed,
    )
    if tight:
        ranks = lax.axis_size("tensor")
        share, here = width // lax.axis_size("dp"), w_query.shape[1]
        hidden = w_up.shape[1]

        def shape(*dims):
            return jax.ShapeDtypeStruct(dims, F32)

        head = (shape(share, here), shape(width)) * 3
        shapes = (
            jax.ShapeDtypeStruct((rows, width), BF16), shape(rows, width), *head,
            shape(here, share), shape(width), shape(width), shape(width),
            shape(share, hidden), shape(hidden * ranks), shape(share, hidden),
            shape(width), shape(width), shape(width),
        )
        outs = finish_call(shapes, result, grad_rows, *sums_a, *sums_b, vec, bias)
        return (*outs[:14], outs[14].T, *outs[15:])
    flat = [a.reshape(width, a.shape[-1]).astype(F32) for a in sums_a]
    flat = [jnp.concatenate(flat[:2], axis=1), jnp.concatenate(flat[2:4], axis=1), *flat[4:]]
    scatter = partial(lax.psum_scatter, axis_name="dp", scatter_dimension=0, tiled=True)
    sum_out, sum_query, sum_key, sum_value = (
        scatter(b) for b in split_pieces(flat[OV], flat[QK])
    )
    sum_out, sum_down = sum_out.T, scatter(flat[DOWN]).T
    vec = lax.psum(vec, ("dp", "tensor"))
    bias = lax.psum(bias, ("dp", "tensor"))
    totals, bias_up = vec[0], vec[1, :4].reshape(-1)
    biases = [
        jnp.concatenate([bias[:, i], bias[:, j, at:at + 64]], axis=1).reshape(-1)
        for i, j, at in ((0, 2, 0), (1, 2, 64), (3, 4, 64))
    ]
    return (
        result,
        grad_rows.astype(F32),
        sum_query,
        biases[0],
        sum_key,
        biases[1],
        sum_value,
        biases[2],
        sum_out,
        totals[0],
        totals[1],
        totals[2],
        scatter(flat[UP]),
        bias_up,
        sum_down,
        totals[3],
        totals[4],
        totals[5],
    )


def solution(mesh):
    in_specs = (
        P(("dp", "tensor"), None),
        P("dp", None),
        P(None, "tensor"),
        P("tensor"),
        P(None, "tensor"),
        P("tensor"),
        P(None, "tensor"),
        P("tensor"),
        P("tensor", None),
        P(),
        P(),
        P(),
        P(None, "tensor"),
        P("tensor"),
        P("tensor", None),
        P(),
        P(),
        P(),
        P(("dp", "tensor"), None),
    )
    out_specs = (
        P(("dp", "tensor"), None),
        P(("dp", "tensor"), None),
        P("dp", "tensor"),
        P(),
        P("dp", "tensor"),
        P(),
        P("dp", "tensor"),
        P(),
        P("tensor", "dp"),
        P(),
        P(),
        P(),
        P("dp", "tensor"),
        P(),
        P("tensor", "dp"),
        P(),
        P(),
        P(),
    )
    tight = mesh.shape["dp"] == 8
    return jax.shard_map(
        partial(on_device, tight), mesh=mesh, in_specs=in_specs, out_specs=out_specs,
        check_vma=False,
    )
```

```python
from functools import partial
import math

import jax
import jax.numpy as jnp
from jax import lax
from jax.experimental import pallas as pl
from jax.experimental.pallas import tpu as pltpu
from jax.sharding import PartitionSpec as P

HD = 64
MESH = pl.DeviceIdType.MESH
F32 = jnp.float32
BF16 = jnp.bfloat16
LN_EPS = 1e-12
CHUNKS = 2
B_QKV, B_UP, SEGMENTS = range(3)
B_OUT, G_MIX, S_MIX, B_DOWN, G_FEED, S_FEED = range(8, 14)
DOWN, UP, OV, QK = range(4)


def nn(left, right):
    return lax.dot_general(left, right, (((1,), (0,)), ((), ())), preferred_element_type=F32)


def tn(left, right):
    return lax.dot_general(left, right, (((0,), (0,)), ((), ())), preferred_element_type=F32)


def nt(left, right):
    return lax.dot_general(left, right, (((1,), (1,)), ((), ())), preferred_element_type=F32)


def norm_stats(values):
    centered = values - jnp.mean(values, axis=-1, keepdims=True)
    factor = lax.rsqrt(jnp.mean(centered * centered, axis=-1, keepdims=True) + LN_EPS)
    return centered * factor, factor


def norm_back(grads, normalized, factor, gain):
    scaled = grads * gain
    first = jnp.mean(scaled, axis=-1, keepdims=True)
    second = jnp.mean(scaled * normalized, axis=-1, keepdims=True)
    return factor * (scaled - first - normalized * second)


def copy_to(src, dst, send, recv, device):
    return pltpu.make_async_remote_copy(
        src_ref=src, dst_ref=dst, send_sem=send, recv_sem=recv, device_id=device,
        device_id_type=MESH,
    )


def layer_kernel(
    tight,
    tokens, cotangent, wq_t, wk_t, wv_t, w_out, w_up, w_down,
    segment_ids, *rest,
):
    b_refs, rest = rest[:10], rest[10:]
    layer_body(tight, tokens, cotangent, wq_t, wk_t, wv_t, w_out, w_up, w_down, segment_ids,
               b_refs, *rest)


def layer_body(
    tight,
    tokens, cotangent, wq_t, wk_t, wv_t, w_out, w_up, w_down, segment_ids, b_refs,
    result_o, grad_o, sums_a, sums_b, vec_o, bias_o,
    x_all, h_all, g2_all, g1_all, wu_t, wd_t, wo_t,
    part_last, part_mate, land_last, land_mate, land_far, passed, out_rows,
    small_own, small_v, cot_v, staged, wqkv, wo, wu, wd,
    seg_nat, seg_cols, cos_t, sin_t,
    qkv_s, k2_s, probs, probs_low, ds_s, o_s, act, dgelu, dz_s, do_s, dqk_s, dv_s,
    q_t, do_t, dk_t, dv_t, h_own, g_own, own_part,
    grads, first_in, second_in, grads_mid, grads_in, grads_sum,
    vec, vec_x, vec_in, bias, bias_x, bias_in, seg_v, b_v,
    ag_s, ag_r, rs_s, rs_r, sw_s, sw_r, wx_s, wx_r, dx_s, dx_r, dq_s, dq_r, dz_sem_s, dz_sem_r,
    vec_s, vec_r, bias_s, bias_r, out_s, out_r, loc, b_sem,
):
    dp, ten = lax.axis_index("dp"), lax.axis_index("tensor")
    low = lax.rem(ten, 2)
    if tight:
        col, core, half = dp // 2, lax.rem(dp, 2), ten // 2
        col_x, col_y = lax.rem(col, 2), col // 2
        slot = low + 2 * core
        mate_slot = low + 2 * (1 - core)
        far_slot = 1 - low + 2 * core
        last_slot = 1 - low + 2 * (1 - core)
        mate = {"dp": col * 2 + 1 - core, "tensor": ten}
        far = {"dp": dp, "tensor": ten + 1 - 2 * low}
        other = lax.rem(ten + 2, 4)
        partner = {"dp": col * 2 + 1 - core, "tensor": other}
        across = {"dp": dp, "tensor": other}
        cols = [{"dp": lax.rem(col + j, 4) * 2 + core, "tensor": ten} for j in (1, 2, 3)]
        next_x = {"dp": (col_y * 2 + 1 - col_x) * 2 + core, "tensor": ten}
        next_y = {"dp": ((1 - col_y) * 2 + col_x) * 2 + core, "tensor": ten}
        home = core == half
        away = core != half
        met = [mate, far, across, partner, *cols]
    else:
        slot = ten
        mate_slot = ten + 1 - 2 * low
        far_slot = lax.rem(ten + 2, 4)
        last_slot = 3 - ten
        mate = {"dp": dp, "tensor": mate_slot}
        far = {"dp": dp, "tensor": far_slot}
        met = [mate, far]

    rows, width = tokens.shape
    length = 4 * rows
    chunk = rows // CHUNKS
    token_part = rows // 2
    both = (0, 2 * rows)
    units = [(2 * rows + 2 * c * chunk, 2 * chunk) for c in range(CHUNKS)]

    def local(src, dst, sem):
        return pltpu.make_async_copy(src, dst, sem)

    barrier = pltpu.get_barrier_semaphore()
    for device in met:
        pl.semaphore_signal(barrier, inc=1, device_id=device, device_id_type=MESH)

    b_copies = [local(src, dst, b_sem.at[i]) for i, (src, dst) in enumerate(zip(b_refs, b_v))]
    b_copies.append(local(segment_ids, seg_v, b_sem.at[10]))
    for copy in b_copies:
        copy.start()
    raw = []
    for i, w in enumerate((wq_t, wk_t, wv_t)):
        raw.append((w.at[pl.ds(0, 128)], (0, 128, 384)[i], 128))
        raw.append((w.at[pl.ds(128, 64)], (256, 320, 512)[i], 64))

    def raw_copy(i, ref):
        src, at, size = raw[i]
        return local(src, ref.at[pl.ds(at, size)], loc.at[i])

    to_tokens = [
        local(
            tokens.at[pl.ds(c * token_part, token_part)],
            x_all.at[pl.ds(c * token_part, token_part)], sw_r.at[4 + c],
        )
        for c in range(2)
    ]
    to_small = local(small_own, small_v.at[pl.ds(0, 8)], sw_r.at[0])
    to_cot = local(cotangent, cot_v, sw_r.at[11])
    wo_rows = w_out.shape[0]
    to_out = local(w_out, wo.at[pl.ds(0, wo_rows)], loc.at[6])
    to_up = local(w_up, wu, loc.at[7])
    to_down = local(w_down, wd, loc.at[8])

    def load_own():
        for copy in to_tokens:
            copy.start()
        for i in range(6):
            raw_copy(i, wqkv).start()
        for copy in (to_out, to_up, to_down, to_cot):
            copy.start()

    def stage_own():
        for i in range(6):
            raw_copy(i, staged).start()

    if tight:
        pl.when(home)(load_own)
        pl.when(away)(stage_own)
    else:
        load_own()

    wo[wo_rows:, :] = jnp.zeros((wo.shape[0] - wo_rows, width), BF16)
    wqkv[576:, :] = jnp.zeros((wqkv.shape[0] - 576, width), BF16)

    def vector(ref):
        return ref[...].astype(F32).reshape(1, ref.shape[0])

    for copy in b_copies:
        copy.wait()
    bq, bk, bv = (vector(b_v[i]) for i in range(3))
    for at, b in ((0, bq), (128, bk), (384, bv)):
        small_own[0:1, at:at + 128] = b[:, :128]
    small_own[0:1, 256:384] = jnp.concatenate([bq[:, 128:], bk[:, 128:]], axis=1)
    small_own[0:1, 512:640] = jnp.concatenate([bv[:, 128:], jnp.zeros((1, 64), F32)], axis=1)
    small_own[0:1, 640:] = jnp.zeros((1, width - 640), F32)
    small_own[B_UP:B_UP + 1, :] = vector(b_v[3])
    small_own[SEGMENTS:8, :] = jnp.zeros((8 - SEGMENTS, width), F32)
    small_own[SEGMENTS:SEGMENTS + 1, :length] = seg_v[...].astype(F32)
    for i in range(6):
        small_v[B_OUT + i:B_OUT + i + 1, :] = vector(b_v[4 + i])
    pl.semaphore_wait(barrier, len(met))

    weight_items = {
        1: (wqkv, staged, 576, 0, 3), 2: (wqkv, staged, 576, 1, 3), 3: (wqkv, staged, 576, 2, 3),
        6: (wo, w_out, wo_rows, 0, 1),
        7: (wu, w_up, width, 0, 2), 8: (wu, w_up, width, 1, 2),
        9: (wd, w_down, width, 0, 2), 10: (wd, w_down, width, 1, 2),
    }
    item_rank = {item: i for i, item in enumerate(weight_items)}

    def item_rows(item, q):
        _, _, total, part, count = weight_items[item]
        size = total // 4 // count
        return pl.ds(q * (total // 4) + part * size, size)

    def swap(item):
        if item in weight_items:
            dst, src = weight_items[item][:2]
            at = item_rows(item, col)
            src, dst = src.at[at], dst.at[at]
        elif item == 0:
            src, dst = small_own, small_v.at[pl.ds(0, 8)]
        elif item == 11:
            src, dst = cotangent, cot_v
        else:
            at = pl.ds((item - 4) * token_part, token_part)
            src, dst = tokens.at[at], x_all.at[at]
        return copy_to(src, dst, sw_s.at[item], sw_r.at[item], partner)

    def spread(item, j):
        ref = weight_items[item][0].at[item_rows(item, col)]
        rank = item_rank[item]
        return copy_to(ref, ref, wx_s.at[rank, j], wx_r.at[rank, j], cols[j])

    def spread_in(item, j):
        ref = weight_items[item][0].at[item_rows(item, lax.rem(col + 3 - j, 4))]
        rank = item_rank[item]
        return copy_to(ref, ref, wx_s.at[rank, j], wx_r.at[rank, j], cols[j])

    def relay(item, follow=None):
        if tight:
            @pl.when(away)
            def _():
                swap(item).wait_recv()
                for j in range(3):
                    spread(item, j).start()
                if follow is not None:
                    swap(follow).start()

    def weights_ready(copies, *items):
        if not tight:
            for copy in copies:
                copy.wait()
            return

        @pl.when(home)
        def _():
            for copy in copies:
                copy.wait()

        @pl.when(away)
        def _():
            for item in items:
                for j in range(3):
                    spread_in(item, j).wait_recv()

    if tight:
        @pl.when(away)
        def _():
            swap(0).start()
            for i in range(6):
                raw_copy(i, staged).wait()
            for item in (1, 2, 3, 4, 5):
                swap(item).start()

        pl.when(home)(to_small.start)
    else:
        to_small.start()

    def at_own(c):
        return pl.ds(c * chunk, chunk)

    def at_mate(c):
        return pl.ds(rows + c * chunk, chunk)

    def at_far(c):
        return pl.ds(2 * rows + 2 * c * chunk, chunk)

    def at_last(c):
        return pl.ds(2 * rows + (2 * c + 1) * chunk, chunk)

    def gather_copy(i, buf, c, kind):
        src, dst, device = (
            (at_own(c), at_mate(c), mate), (at_own(c), at_far(c), far), (at_far(c), at_last(c), mate)
        )[kind]
        return copy_to(
            buf.at[src], buf.at[dst], ag_s.at[i, c, kind], ag_r.at[i, c, kind], device
        )

    def ag_own(i, buf, c):
        gather_copy(i, buf, c, 1).start()
        gather_copy(i, buf, c, 0).start()

    def own_tokens(part):
        for c in range(CHUNKS // 2):
            ag_own(0, x_all, part * (CHUNKS // 2) + c)

    def ag_mate(i, buf):
        for c in range(CHUNKS):
            gather_copy(i, buf, c, 0).wait_recv()

    def ag_unit(i, buf, c):
        gather_copy(i, buf, c, 1).wait_recv()
        gather_copy(i, buf, c, 2).start()
        gather_copy(i, buf, c, 2).wait_recv()

    def rs_copy(i, c, kind):
        src, dst, device = (
            (part_last.at[i, c], land_last.at[i, c], mate),
            (part_mate.at[i, c], land_mate.at[i, c], mate),
            (passed.at[i, c], land_far.at[i, c], far),
        )[kind]
        return copy_to(src, dst, rs_s.at[i, c, kind], rs_r.at[i, c, kind], device)

    def rs_whole(i):
        return copy_to(part_mate.at[i], land_mate.at[i], rs_s.at[i, 0, 1], rs_r.at[i, 0, 1], mate)

    def rs_unit(i, c, term):
        part_last[i, c] = term[chunk:].astype(BF16)
        rs_copy(i, c, 0).start()
        own_part[rows + c * chunk:rows + (c + 1) * chunk, :] = term[:chunk]

    def rs_pass(i, c):
        rs_copy(i, c, 0).wait_recv()
        term = own_part[rows + c * chunk:rows + (c + 1) * chunk, :]
        passed[i, c] = (term + land_last[i, c].astype(F32)).astype(BF16)
        rs_copy(i, c, 2).start()

    def rs_mate(i, term):
        for c in range(CHUNKS):
            part_mate[i, c] = term[rows + c * chunk:rows + (c + 1) * chunk].astype(BF16)
        rs_whole(i).start()
        own_part[0:rows, :] = term[:rows]

    def reduced(i, c):
        if c == 0:
            rs_whole(i).wait_recv()
        rs_copy(i, c, 2).wait_recv()
        term = own_part[c * chunk:(c + 1) * chunk, :]
        return term + land_mate[i, c].astype(F32) + land_far[i, c].astype(F32)

    if not tight:
        for c in range(2):
            to_tokens[c].wait()
            own_tokens(c)
    else:
        @pl.when(home)
        def _():
            for c in range(2):
                to_tokens[c].wait()
                own_tokens(c)

    to_small.wait()
    seg_row = small_v[SEGMENTS:SEGMENTS + 1, :length]
    seg_nat[...] = jnp.transpose(jnp.broadcast_to(seg_row, (128, length)))
    segs = seg_nat[...]
    place = lax.broadcasted_iota(jnp.int32, (length, 128), 0).astype(F32)
    start = jnp.zeros((length, 128), F32)
    for s in range(4):
        before = jnp.sum(jnp.where(seg_row < s, 1.0, 0.0), axis=1, keepdims=True)
        start = jnp.where(segs == s, before, start)
    cos_t[...] = place - start
    order = [(c, slot, c) for c in range(CHUNKS)]
    order += [(CHUNKS + c, mate_slot, c) for c in range(CHUNKS)]
    for c in range(CHUNKS):
        order += [(2 * (CHUNKS + c), far_slot, c), (2 * (CHUNKS + c) + 1, last_slot, c)]
    for to, from_slot, c in order:
        at = pl.ds(pl.multiple_of(from_slot * rows + c * chunk, chunk), chunk)
        seg_cols[to * chunk:(to + 1) * chunk, :] = seg_nat[at, :]
        sin_t[to * chunk:(to + 1) * chunk, :] = cos_t[at, :]
    lane = lax.broadcasted_iota(jnp.int32, (1, 128), 1)
    frequency = jnp.exp(lax.rem(lane, 32).astype(F32) * (-math.log(10000.0) / 32))
    sign = jnp.where(lax.rem(lane, 64) < 32, -1.0, 1.0)
    angle = sin_t[...] * frequency
    cos_t[...] = jnp.cos(angle)
    sin_t[...] = jnp.sin(angle) * sign
    seg_row = jnp.transpose(seg_cols[...])[0:1, :]


    low_lane = lane < 64

    def turn(values):
        return jnp.where(
            lax.rem(lane, 64) < 32, pltpu.roll(values, 96, 1), pltpu.roll(values, 32, 1)
        )

    scale = HD ** (-0.5)

    def project_rows(lo, n):
        here = slice(lo, lo + n)
        x = x_all[here, :]
        pre = nt(x, wqkv[...]) + small_v[B_QKV:B_QKV + 1, :640]
        cosine, sine = cos_t[here, :], sin_t[here, :]

        def rot(block):
            return block * cosine + turn(block) * sine

        query, key, mixed = rot(pre[:, :128]), rot(pre[:, 128:256]), rot(pre[:, 256:384])
        qkv_s[here, 0:128] = (query.astype(BF16) * scale).astype(BF16)
        qkv_s[here, 128:256] = key.astype(BF16)
        qkv_s[here, 256:384] = (jnp.where(low_lane, mixed, 0.0).astype(BF16) * scale).astype(BF16)
        qkv_s[here, 384:640] = pre[:, 384:640].astype(BF16)
        k2_s[here, :] = jnp.where(low_lane, pltpu.roll(mixed, 64, 1), 0.0).astype(BF16)

    if tight:
        @pl.when(away)
        def _():
            swap(1).wait_recv()
            for j in range(3):
                spread(1, j).start()
            swap(2).wait_recv()
            for j in range(3):
                spread(2, j).start()
            swap(6).start()
            swap(4 + 0).wait_recv()
            own_tokens(0)
            swap(7).start()
            swap(4 + 1).wait_recv()
            own_tokens(1)
            swap(3).wait_recv()
            for j in range(3):
                spread(3, j).start()
            swap(8).start()
            swap(6).wait_recv()
            for j in range(3):
                spread(6, j).start()
            swap(9).start()
            swap(10).start()
    weights_ready([raw_copy(i, wqkv) for i in range(6)], 1, 2, 3)
    ag_mate(0, x_all)
    project_rows(*both)
    for c in range(CHUNKS):
        ag_unit(0, x_all, c)
    project_rows(2 * rows, 2 * rows)

    def masked(block, head):
        if head == 2:
            return block
        keep = low_lane if head == 0 else ~low_lane
        return jnp.where(keep, block, jnp.zeros_like(block))

    def attend(s, carry):
        here = pl.ds(pl.multiple_of(s * rows, rows), rows)
        same = seg_cols[here, 0:1] == seg_row
        outs = []
        for head in range(3):
            q_at, v_at = (0, 384) if head < 2 else (256, 512)
            query = masked(qkv_s[here, q_at:q_at + 128], head)
            keys = qkv_s[:, 128:256] if head < 2 else k2_s[...]
            scores = jnp.where(same, nt(query, keys), -1e30)
            scores = jnp.exp(scores - jnp.max(scores, axis=1, keepdims=True))
            weight = scores * (1.0 / jnp.sum(scores, axis=1, keepdims=True))
            probs[head, here, :] = weight
            weight_low = weight.astype(BF16)
            probs_low[head, here, :] = weight_low
            outs.append(nn(weight_low, qkv_s[:, v_at:v_at + 128]))
        o_s[here, 0:128] = jnp.where(low_lane, outs[0], outs[1]).astype(BF16)
        o_s[here, 128:256] = outs[2].astype(BF16)
        return carry

    def mix(lo, n):
        return nn(o_s[lo:lo + n, :], wo[...])

    attend(2, 0)
    if tight:
        @pl.when(away)
        def _():
            swap(7).wait_recv()
            for j in range(3):
                spread(7, j).start()
    weights_ready([to_out], 6)
    for c in range(CHUNKS // 2):
        rs_unit(0, c, mix(*units[c]))
    attend(3, 0)
    if tight:
        @pl.when(away)
        def _():
            swap(8).wait_recv()
            for j in range(3):
                spread(8, j).start()
    for c in range(CHUNKS // 2, CHUNKS):
        rs_unit(0, c, mix(*units[c]))
    for c in range(CHUNKS // 2):
        rs_pass(0, c)
    lax.fori_loop(0, 1, attend, 0)
    for c in range(CHUNKS // 2, CHUNKS):
        rs_pass(0, c)
    if tight:
        @pl.when(away)
        def _():
            swap(9).wait_recv()
            for j in range(3):
                spread(9, j).start()
    lax.fori_loop(1, 2, attend, 0)
    rs_mate(0, mix(*both))
    if tight:
        @pl.when(away)
        def _():
            swap(10).wait_recv()
            for j in range(3):
                spread(10, j).start()
            swap(11).start()
    factors = []

    def spot(c):
        return slice(c * chunk, (c + 1) * chunk)

    def row_of(at):
        return small_v[at:at + 1, :]

    for c in range(CHUNKS):
        here = spot(c)
        into = reduced(0, c) + x_all[here, :].astype(F32) + row_of(B_OUT)
        normal1, factor1 = norm_stats(into)
        factors.append(factor1)
        normed = normal1 * row_of(G_MIX) + row_of(S_MIX)
        h_own[0, here, :] = normed
        h_own[1, here, :] = normal1
        h_all[here, :] = normed.astype(BF16)
        ag_own(1, h_all, c)


    def feed(lo, n):
        here = slice(lo, lo + n)
        h = h_all[here, :]
        z = nn(h, wu[...]) + row_of(B_UP)
        phi = 0.5 * (1.0 + lax.erf(z * (2.0 ** -0.5)))
        act[here, :] = (z * phi).astype(BF16)
        dgelu[here, :] = phi + z * (jnp.exp(-0.5 * z * z) * (1.0 / math.sqrt(2.0 * math.pi)))

    def shrink(lo, n):
        return nn(act[lo:lo + n, :], wd[...])

    weights_ready([to_up], 7, 8)
    ag_mate(1, h_all)
    feed(*both)
    wu_t[...] = jnp.transpose(wu[...])
    wo_t[...] = jnp.transpose(wo[...])
    for c in range(CHUNKS):
        ag_unit(1, h_all, c)
        if c > 0:
            rs_pass(1, c - 1)
        feed(*units[c])
        if c == 0:
            weights_ready([to_down], 9, 10)
        rs_unit(1, c, shrink(*units[c]))
    rs_pass(1, CHUNKS - 1)
    rs_mate(1, shrink(*both))
    wd_t[...] = jnp.transpose(wd[...])

    def hand_out(i, src, dst, c):
        src, dst = src.at[pl.ds(c * chunk, chunk)], dst.at[pl.ds(c * chunk, chunk)]
        keep = local(src, dst, out_r.at[i, c])
        send = copy_to(src, dst, out_s.at[i, c], out_r.at[i, c], partner) if tight else None
        return keep, send

    def hand_start(*args):
        keep, send = hand_out(*args)
        if tight:
            pl.when(home)(keep.start)
            pl.when(away)(send.start)
        else:
            keep.start()

    to_cot.wait()
    sums = [0.0, 0.0, 0.0]
    for c in range(CHUNKS):
        here = spot(c)
        into = reduced(1, c) + h_own[0, here, :] + row_of(B_DOWN)
        normal2, factor2 = norm_stats(into)
        dy = cot_v[here, :].astype(F32)
        grad2 = norm_back(dy, normal2, factor2, row_of(G_FEED))
        g_own[0, here, :] = grad2
        g2_all[here, :] = grad2.astype(BF16)
        ag_own(2, g2_all, c)
        out_rows[0, here, :] = (normal2 * row_of(G_FEED) + row_of(S_FEED)).astype(BF16)
        hand_start(0, out_rows.at[0], result_o, c)
        for i, term in enumerate((grad2, dy * normal2, dy)):
            sums[i] = sums[i] + jnp.sum(term, axis=0, keepdims=True)
    vec[...] = jnp.zeros(vec.shape, F32)
    for i in range(3):
        vec[0, 3 + i:4 + i, :] = sums[i]

    def weight_grad(at_piece, value):
        quarter = width // 4
        for y in range(2):
            found = value(slice(2 * y * quarter, 2 * (y + 1) * quarter)).astype(BF16)
            for x in range(2):
                for h in range(found.shape[1] // 384):
                    part = found[x * quarter:(x + 1) * quarter, h * 384:(h + 1) * 384]
                    grads[at_piece + h][y, x] = part

    def first_copy(i, h):
        if h == 0:
            src, device = grads[2 * i].at[:, 1 - col_x], next_x
        else:
            src, device = grads[2 * i + 1].at[1 - col_y], next_y
        return copy_to(
            src, first_in.at[2 * i + h], dx_s.at[i, h, 0], dx_r.at[i, h, 0], device
        )

    def second_copy(i, h):
        keep, device = (1 - col_y, next_y) if h == 0 else (1 - col_x, next_x)
        return copy_to(
            grads_mid.at[2 * i + h, keep], second_in.at[2 * i + h], dx_s.at[i, h, 1],
            dx_r.at[i, h, 1], device,
        )

    def first_send(i):
        if tight:
            for h in range(2):
                first_copy(i, h).start()

    def first_land(i):
        if not tight:
            return
        for h in range(2):
            first_copy(i, h).wait_recv()
            for j in range(2):
                own = grads[2 * i][j, col_x] if h == 0 else grads[2 * i + 1][col_y, j]
                came = first_in[2 * i + h, j].astype(F32)
                grads_mid[2 * i + h, j] = (own.astype(F32) + came).astype(BF16)
            second_copy(i, h).start()

    def second_land(i):
        if not tight:
            return
        totals = []
        for h in range(2):
            second_copy(i, h).wait_recv()
            own = grads_mid[2 * i + h, col_y if h == 0 else col_x]
            totals.append(own.astype(F32) + second_in[2 * i + h].astype(F32))
        finish_sum(i, jnp.concatenate(totals, axis=1))

    def finish_sum(i, total):
        grads_sum[i][...] = total.astype(BF16).reshape(grads_sum[i].shape)

        @pl.when(home)
        def _():
            keep_sum(i).start()
            mate_sum(i).start()

        @pl.when(away)
        def _():
            for copy in away_sums(i):
                copy.start()

    share = width // 8

    def direct_copy(i, j, part):
        to = lax.rem(col + 1 + j, 4)
        at = pl.ds(part * share, share)
        return copy_to(
            grads[i + 2].at[to // 2, lax.rem(to, 2), at], grads_in.at[i - OV, j, at],
            dq_s.at[i - OV, j, part], dq_r.at[i - OV, j, part], cols[j],
        )

    def direct_send(i):
        if tight:
            for part in range(2):
                for j in range(3):
                    direct_copy(i, j, part).start()

    def direct_land(i):
        if not tight:
            return
        for part in range(2):
            at = slice(part * share, (part + 1) * share)
            total = grads[i + 2][col_y, col_x, at].astype(F32)
            for j in range(3):
                direct_copy(i, j, part).wait_recv()
                total = total + grads_in[i - OV, j, at].astype(F32)
            grads_sum[i][part] = total.astype(BF16)

            @pl.when(home)
            def _():
                pl.when(core == part)(keep_sum(i).start)
                pl.when(core != part)(mate_sum(i).start)

            @pl.when(away)
            def _():
                pl.when(core == part)(away_sums(i)[0].start)
                pl.when(core != part)(away_sums(i)[1].start)

    def direct_sent(i):
        for part in range(2):
            for j in range(3):
                direct_copy(i, j, part).wait_send()

    def keep_sum(i):
        return local(grads_sum[i].at[core], sums_a[i], dz_sem_r.at[i, 0])

    def mate_sum(i):
        return copy_to(
            grads_sum[i].at[1 - core], sums_a[i], dz_sem_s.at[i, 0], dz_sem_r.at[i, 0], mate
        )

    def away_sums(i):
        return (
            copy_to(
                grads_sum[i].at[core], sums_b[i], dz_sem_s.at[i, 0], dz_sem_r.at[i, 1], across
            ),
            copy_to(
                grads_sum[i].at[1 - core], sums_b[i], dz_sem_s.at[i, 1], dz_sem_r.at[i, 1], partner
            ),
        )

    def feed_back(lo, n):
        here = slice(lo, lo + n)
        dz_s[here, :] = (nn(g2_all[here, :], wd_t[...]) * dgelu[here, :]).astype(BF16)

    def widen(lo, n):
        return nn(dz_s[lo:lo + n, :], wu_t[...])

    ag_mate(2, g2_all)
    feed_back(*both)
    for c in range(CHUNKS):
        ag_unit(2, g2_all, c)
        if c > 0:
            rs_pass(2, c - 1)
        if c == CHUNKS - 1:
            weight_grad(0, lambda at: tn(g2_all[:, at], act[...]))
            first_send(DOWN)
        feed_back(*units[c])
        rs_unit(2, c, widen(*units[c]))
    rs_pass(2, CHUNKS - 1)
    rs_mate(2, widen(*both))

    weight_grad(2, lambda at: tn(h_all[:, at], dz_s[...]))
    vec[1, pl.ds(slot, 1), :] = jnp.sum(dz_s[...].astype(F32), axis=0, keepdims=True)

    sums = [0.0, 0.0, 0.0]
    for c in range(CHUNKS):
        here = spot(c)
        dh = reduced(2, c) + g_own[0, here, :]
        normal1 = h_own[1, here, :]
        grad1 = norm_back(dh, normal1, factors[c], row_of(G_MIX))
        g_own[1, here, :] = grad1
        g1_all[here, :] = grad1.astype(BF16)
        ag_own(3, g1_all, c)
        for i, term in enumerate((grad1, dh * normal1, dh)):
            sums[i] = sums[i] + jnp.sum(term, axis=0, keepdims=True)
    for i in range(3):
        vec[0, i:i + 1, :] = sums[i]

    class Total:
        def __init__(self, own, sent, landing, send, recv):
            self.own, self.sent, self.landing, self.send, self.recv = own, sent, landing, send, recv

        def copy(self, j):
            src = self.own if j < 3 else self.sent.at[j - 3]
            device = (*cols, mate, far, across)[j]
            return copy_to(src, self.landing.at[j], self.send.at[j], self.recv.at[j], device)

        def begin(self):
            if tight:
                for j in range(3):
                    self.copy(j).start()

        def columns(self):
            if tight:
                for j in range(3):
                    self.copy(j).wait_recv()
                self.sent[0] = self.own[...] + self.landing[0] + self.landing[1] + self.landing[2]
                self.copy(3).start()

        def step(self, k):
            if tight:
                self.copy(2 + k).wait_recv()
                self.sent[k] = self.sent[k - 1] + self.landing[2 + k]
                if k < 3:
                    self.copy(3 + k).start()

        def sends_done(self):
            for j in range(6):
                self.copy(j).wait_send()

    vec_total = Total(vec, vec_x, vec_in, vec_s, vec_r)
    bias_total = Total(bias, bias_x, bias_in, bias_s, bias_r)
    vec_total.begin()

    def heads_back(lo, n):
        here = slice(lo, lo + n)
        do_s[here, :] = nn(g1_all[here, :], wo_t[...]).astype(BF16)

    def back(values, here):
        return values * cos_t[here, :] - turn(values) * sin_t[here, :]

    def attend_back(s, carry):
        here = pl.ds(pl.multiple_of(s * rows, rows), rows)
        outs = []
        for head in range(3):
            v_at, o_at = (384, 0) if head < 2 else (512, 128)
            grad_o = masked(do_s[here, o_at:o_at + 128], head)
            grad_p = nt(grad_o, qkv_s[:, v_at:v_at + 128])
            weight = probs[head, here, :]
            dot = jnp.sum(grad_p * weight, axis=1, keepdims=True)
            ds = (weight * (grad_p - dot)).astype(BF16)
            ds_s[head, here, :] = ds
            keys = qkv_s[:, 128:256] if head < 2 else k2_s[...]
            outs.append(nn(ds, keys) * scale)
        dqk_s[here, 0:128] = back(jnp.where(low_lane, outs[0], outs[1]), here).astype(BF16)
        dqk_s[here, 256:384] = back(outs[2], here).astype(BF16)
        return carry

    q_t[0:128, :] = jnp.transpose(qkv_s[:, 0:128])
    q_t[128:256, :] = jnp.transpose(qkv_s[:, 256:384])
    ag_mate(3, g1_all)
    heads_back(*both)
    first_land(DOWN)
    lax.fori_loop(0, 1, attend_back, 0)
    first_send(UP)
    lax.fori_loop(1, 2, attend_back, 0)
    vec_total.columns()
    for c in range(CHUNKS):
        ag_unit(3, g1_all, c)
    heads_back(2 * rows, 2 * rows)
    vec_total.step(1)
    second_land(DOWN)
    do_t[0:128, :] = jnp.transpose(do_s[:, 0:128])
    do_t[128:256, :] = jnp.transpose(do_s[:, 128:256])
    for head in range(2):
        at = slice(head * 64, head * 64 + 64)
        dv_t[at, :] = nn(do_t[at, :], probs_low[head])
    dv_t[128:192, :] = jnp.zeros((64, length), F32)
    dv_t[192:256, :] = nn(do_t[128:192, :], probs_low[2])
    dv_s[:, 0:128] = jnp.transpose(dv_t[0:128, :]).astype(BF16)
    dv_s[:, 128:256] = jnp.transpose(dv_t[128:256, :]).astype(BF16)

    def out_value(at):
        out = tn(g1_all[:, at], o_s[...])
        value = tn(x_all[:, at], dv_s[...])
        return jnp.concatenate(
            [out[:, :128], value[:, :128], out[:, 128:] + value[:, 128:]], axis=1
        )

    weight_grad(4, out_value)
    lax.fori_loop(2, 3, attend_back, 0)
    lax.fori_loop(3, 4, attend_back, 0)
    first_land(UP)
    vec_total.step(2)
    for head in range(3):
        at = slice(head * 64, head * 64 + 64)
        dk_t[at, :] = nn(q_t[at, :], ds_s[head])
    dk_t[192:, :] = jnp.zeros((64, length), F32)
    everything = slice(None)
    dqk_s[:, 128:256] = back(jnp.transpose(dk_t[0:128, :]), everything).astype(BF16)
    key2 = back(jnp.transpose(dk_t[128:256, :]), everything)
    query2 = dqk_s[:, 256:384].astype(F32)
    dqk_s[:, 256:384] = jnp.where(low_lane, query2, pltpu.roll(key2, 64, 1)).astype(BF16)

    query_key = jnp.sum(dqk_s[...].astype(F32), axis=0, keepdims=True)
    values = jnp.sum(dv_s[...].astype(F32), axis=0, keepdims=True)
    bias[...] = jnp.zeros(bias.shape, F32)
    for i in range(3):
        bias[slot, i:i + 1, :] = query_key[:, i * 128:(i + 1) * 128]
    for i in range(2):
        bias[slot, 3 + i:4 + i, :] = values[:, i * 128:(i + 1) * 128]
    value_low = jnp.where(
        low_lane, pltpu.roll(dv_s[:, 128:256].astype(F32), 64, 1), 0.0
    ).astype(BF16)

    def to_input(lo, n):
        term = nn(dqk_s[lo:lo + n, :], wqkv[0:384, :])
        term = term + nn(dv_s[lo:lo + n, 0:128], wqkv[384:512, :])
        return term + nn(value_low[lo:lo + n, :], wqkv[512:640, :])

    bias_total.begin()
    direct_send(OV)
    for c in range(CHUNKS):
        rs_unit(3, c, to_input(*units[c]))
    for c in range(CHUNKS):
        rs_pass(3, c)
    rs_mate(3, to_input(*both))
    weight_grad(5, lambda at: tn(x_all[:, at], dqk_s[...]))
    direct_send(QK)
    second_land(UP)
    bias_total.columns()
    for c in range(CHUNKS):
        here = spot(c)
        out_rows[1, here, :] = (reduced(3, c) + g_own[1, here, :]).astype(BF16)
        hand_start(1, out_rows.at[1], grad_o, c)
    bias_total.step(1)
    vec_total.step(3)
    for i, buf in enumerate((x_all, h_all, g2_all, g1_all)):
        for c in range(CHUNKS):
            for kind in range(3):
                gather_copy(i, buf, c, kind).wait_send()
                if kind != 1:
                    rs_copy(i, c, kind).wait_send()
        rs_whole(i).wait_send()

    def out_waits(i, dst):
        for c in range(CHUNKS):
            hand_out(i, out_rows.at[i], dst, c)[0].wait()
        if tight:
            @pl.when(away)
            def _():
                for c in range(CHUNKS):
                    hand_out(i, out_rows.at[i], dst, c)[1].wait_send()

    out_waits(0, result_o)
    if tight:
        for i in (DOWN, UP):
            for h in range(2):
                first_copy(i, h).wait_send()
                second_copy(i, h).wait_send()
        vec_total.sends_done()

        @pl.when(away)
        def _():
            for item in weight_items:
                for j in range(3):
                    spread(item, j).wait_send()
            for item in range(12):
                swap(item).wait_send()

    direct_land(OV)
    if tight:
        direct_sent(OV)
    bias_total.step(2)
    direct_land(QK)
    bias_total.step(3)
    if tight:
        keep = [local(vec_x.at[3], vec_o, loc.at[0]), local(bias_x.at[3], bias_o, loc.at[1])]
    else:
        keep = [local(vec, vec_o, loc.at[0]), local(bias, bias_o, loc.at[1])]
        keep += [local(grads[i], sums_a[i], loc.at[2 + i]) for i in range(6)]
    for copy in keep:
        copy.start()

    out_waits(1, grad_o)
    for copy in keep:
        copy.wait()
    if tight:
        for i in range(4):
            keep_sum(i).wait()
            away_sums(i)[0].wait_recv()
        direct_sent(QK)
        bias_total.sends_done()

        @pl.when(home)
        def _():
            for i in range(4):
                mate_sum(i).wait_send()

        @pl.when(away)
        def _():
            for i in range(4):
                for copy in away_sums(i):
                    copy.wait_send()


def layer_call(tight, shapes, *args):
    rows, width = shapes
    hidden = width
    length = 4 * rows
    chunk = rows // CHUNKS
    heads_wide, qkv_wide = 256, 640
    widths = (hidden, hidden, 384, 384)
    any_space = pl.BlockSpec(memory_space=pl.ANY)
    quarter = width // 4
    if tight:
        sums = [jax.ShapeDtypeStruct((quarter // 2, w), BF16) for w in widths]
    else:
        sums = [jax.ShapeDtypeStruct((2, 2, quarter, 384), BF16)] * 6
    out_shape = (
        jax.ShapeDtypeStruct((rows, width), BF16),
        jax.ShapeDtypeStruct((rows, width), BF16),
        sums,
        [jax.ShapeDtypeStruct((quarter // 2, w), BF16) for w in widths],
        jax.ShapeDtypeStruct((2, 8, width), F32),
        jax.ShapeDtypeStruct((4, 8, 128), F32),
    )
    V = pltpu.VMEM
    D = pltpu.SemaphoreType.DMA
    pieces = V((4, CHUNKS, chunk, width), BF16)
    scratch = [
        *[V((length, width), BF16)] * 4,
        V((hidden, width), BF16), V((width, hidden), BF16), V((width, heads_wide), BF16),
        *[pieces] * 6, V((2, rows, width), BF16),
        V((8, width), F32), V((16, width), F32), V((rows, width), BF16),
        V((576, width), BF16), V((qkv_wide, width), BF16), V((heads_wide, width), BF16),
        V((width, hidden), BF16), V((hidden, width), BF16),
        *[V((length, 128), F32)] * 4,
        V((length, qkv_wide), BF16), V((length, 128), BF16), V((3, length, length), F32),
        V((3, length, length), BF16), V((3, length, length), BF16), V((length, heads_wide), BF16),
        V((length, hidden), BF16), V((length, hidden), F32), V((length, hidden), BF16),
        V((length, heads_wide), BF16), V((length, 384), BF16), V((length, heads_wide), BF16),
        V((heads_wide, length), BF16), V((heads_wide, length), BF16),
        V((heads_wide, length), F32), V((heads_wide, length), F32),
        V((2, rows, width), F32), V((2, rows, width), F32), V((2 * rows, width), F32),
        [V((2, 2, quarter, 384), BF16)] * 6,
        V((4, 2, quarter, 384), BF16), V((4, quarter, 384), BF16), V((4, 2, quarter, 384), BF16),
        V((2, 3, quarter, 384), BF16),
        [V((2, quarter // 2, w), BF16) for w in widths],
        V((2, 8, width), F32), V((4, 2, 8, width), F32), V((6, 2, 8, width), F32),
        V((4, 8, 128), F32), V((4, 4, 8, 128), F32), V((6, 4, 8, 128), F32),
        V((1, length), jnp.int32), [V(b.shape, BF16) for b in args[9:]],
        *[D((4, CHUNKS, 3))] * 4, D((12,)), D((12,)), D((8, 3)), D((8, 3)),
        D((2, 2, 2)), D((2, 2, 2)), D((2, 3, 2)), D((2, 3, 2)), D((4, 2)), D((4, 2)),
        D((6,)), D((6,)), D((6,)), D((6,)), D((2, CHUNKS)), D((2, CHUNKS)), D((9,)), D((11,)),
    ]
    return pl.pallas_call(
        partial(layer_kernel, tight),
        out_shape=out_shape,
        in_specs=[any_space] * 19,
        out_specs=jax.tree.map(lambda _: any_space, out_shape),
        scratch_shapes=scratch,
        compiler_params=pltpu.CompilerParams(
            collective_id=0, has_side_effects=True, vmem_limit_bytes=61 << 20
        ),
    )(*args)


def finish_kernel(*refs):
    sources, refs = refs[:12], refs[12:]
    outs, refs = refs[:18], refs[18:]
    held, made, sem, out_sem = refs[:12], refs[12:30], refs[30], refs[31]
    (
        o_result, o_tokens, o_query, o_b_query, o_key, o_b_key, o_value, o_b_value, o_out, o_b_out,
        o_gain_mixer, o_shift_mixer, o_up, o_b_up, o_down, o_b_down, o_gain_feed, o_shift_feed,
    ) = made
    writes = [
        pltpu.make_async_copy(src, dst, out_sem.at[i]) for i, (src, dst) in enumerate(zip(made, outs))
    ]
    copies = [
        pltpu.make_async_copy(src, dst, sem.at[i]) for i, (src, dst) in enumerate(zip(sources, held))
    ]
    for copy in copies:
        copy.start()

    def take(i):
        copies[i].wait()
        return held[i][...]

    def total(i):
        return take(2 + i).astype(F32) + take(6 + i).astype(F32)

    o_result[...] = take(0)
    writes[0].start()
    o_tokens[...] = take(1).astype(F32)
    writes[1].start()
    o_down[...] = total(DOWN)
    writes[14].start()
    o_up[...] = total(UP)
    writes[12].start()
    out, query, key, value = split_pieces(total(OV), total(QK))
    o_out[...] = jnp.transpose(out)
    for ref, part in zip((o_query, o_key, o_value), (query, key, value)):
        ref[...] = part
    for i in (8, 2, 4, 6):
        writes[i].start()
    vec, bias = take(10), take(11)
    rows = (o_b_out, o_gain_mixer, o_shift_mixer, o_b_down, o_gain_feed, o_shift_feed)
    for i, ref in enumerate(rows):
        ref[...] = vec[0, i]
    o_b_up[...] = jnp.concatenate([vec[1, k:k + 1, :] for k in range(4)], axis=1).reshape(
        o_b_up.shape
    )
    for ref, (i, j, at) in zip(
        (o_b_query, o_b_key, o_b_value), ((0, 2, 0), (1, 2, 64), (3, 4, 64))
    ):
        parts = []
        for k in range(4):
            parts += [bias[k, i:i + 1, :], bias[k, j:j + 1, at:at + 64]]
        ref[...] = jnp.concatenate(parts, axis=1).reshape(ref.shape)
    for i in (3, 5, 7, 9, 10, 11, 13, 15, 16, 17):
        writes[i].start()
    for write in writes:
        write.wait()


def finish_call(shapes, *args):
    any_space = pl.BlockSpec(memory_space=pl.ANY)
    return pl.pallas_call(
        finish_kernel,
        out_shape=shapes,
        in_specs=[any_space] * len(args),
        out_specs=tuple(any_space for _ in shapes),
        scratch_shapes=[
            *[pltpu.VMEM(a.shape, a.dtype) for a in args],
            *[pltpu.VMEM(a.shape, a.dtype) for a in shapes],
            pltpu.SemaphoreType.DMA((len(args),)), pltpu.SemaphoreType.DMA((len(shapes),)),
        ],
        compiler_params=pltpu.CompilerParams(vmem_limit_bytes=61 << 20),
    )(*args)


def split_pieces(out_value, query_key):
    def pick(block, at, tail):
        return jnp.concatenate([block[..., at:at + 128], block[..., tail:tail + 64]], axis=-1)

    return (
        pick(out_value, 0, 256), pick(query_key, 0, 256), pick(query_key, 128, 320),
        pick(out_value, 128, 320),
    )


def on_device(
    tight,
    tokens,
    segment_ids,
    w_query,
    b_query,
    w_key,
    b_key,
    w_value,
    b_value,
    w_out,
    b_out,
    gain_mixer,
    shift_mixer,
    w_up,
    b_up,
    w_down,
    b_down,
    gain_feed,
    shift_feed,
    cotangent,
):
    rows, width = tokens.shape
    result, grad_rows, sums_a, sums_b, vec, bias = layer_call(
        tight, (rows, width), tokens, cotangent, w_query.T, w_key.T, w_value.T, w_out, w_up, w_down,
        segment_ids, b_query, b_key, b_value, b_up, b_out, gain_mixer, shift_mixer, b_down,
        gain_feed, shift_feed,
    )
    if tight:
        ranks = lax.axis_size("tensor")
        share, here = width // lax.axis_size("dp"), w_query.shape[1]
        hidden = w_up.shape[1]

        def shape(*dims):
            return jax.ShapeDtypeStruct(dims, F32)

        head = (shape(share, here), shape(width)) * 3
        shapes = (
            jax.ShapeDtypeStruct((rows, width), BF16), shape(rows, width), *head,
            shape(here, share), shape(width), shape(width), shape(width),
            shape(share, hidden), shape(hidden * ranks), shape(share, hidden),
            shape(width), shape(width), shape(width),
        )
        outs = finish_call(shapes, result, grad_rows, *sums_a, *sums_b, vec, bias)
        return (*outs[:14], outs[14].T, *outs[15:])
    flat = [a.reshape(width, a.shape[-1]).astype(F32) for a in sums_a]
    flat = [jnp.concatenate(flat[:2], axis=1), jnp.concatenate(flat[2:4], axis=1), *flat[4:]]
    scatter = partial(lax.psum_scatter, axis_name="dp", scatter_dimension=0, tiled=True)
    sum_out, sum_query, sum_key, sum_value = (
        scatter(b) for b in split_pieces(flat[OV], flat[QK])
    )
    sum_out, sum_down = sum_out.T, scatter(flat[DOWN]).T
    vec = lax.psum(vec, ("dp", "tensor"))
    bias = lax.psum(bias, ("dp", "tensor"))
    totals, bias_up = vec[0], vec[1, :4].reshape(-1)
    biases = [
        jnp.concatenate([bias[:, i], bias[:, j, at:at + 64]], axis=1).reshape(-1)
        for i, j, at in ((0, 2, 0), (1, 2, 64), (3, 4, 64))
    ]
    return (
        result,
        grad_rows.astype(F32),
        sum_query,
        biases[0],
        sum_key,
        biases[1],
        sum_value,
        biases[2],
        sum_out,
        totals[0],
        totals[1],
        totals[2],
        scatter(flat[UP]),
        bias_up,
        sum_down,
        totals[3],
        totals[4],
        totals[5],
    )


def solution(mesh):
    in_specs = (
        P(("dp", "tensor"), None),
        P("dp", None),
        P(None, "tensor"),
        P("tensor"),
        P(None, "tensor"),
        P("tensor"),
        P(None, "tensor"),
        P("tensor"),
        P("tensor", None),
        P(),
        P(),
        P(),
        P(None, "tensor"),
        P("tensor"),
        P("tensor", None),
        P(),
        P(),
        P(),
        P(("dp", "tensor"), None),
    )
    out_specs = (
        P(("dp", "tensor"), None),
        P(("dp", "tensor"), None),
        P("dp", "tensor"),
        P(),
        P("dp", "tensor"),
        P(),
        P("dp", "tensor"),
        P(),
        P("tensor", "dp"),
        P(),
        P(),
        P(),
        P("dp", "tensor"),
        P(),
        P("tensor", "dp"),
        P(),
        P(),
        P(),
    )
    tight = mesh.shape["dp"] == 8
    return jax.shard_map(
        partial(on_device, tight), mesh=mesh, in_specs=in_specs, out_specs=out_specs,
        check_vma=False,
    )
```
